256 devices in a mesh: rows: 128 (over z, y, x_hi, core), batch: 2 (over x_lo).
Axes of the slice: x: 4 (x_hi: 2, x_lo: 2; x = x_hi * 2 + x_lo), y: 4, z: 8, core: 2. Of those that a mesh axis runs over, the one named last changes fastest.
Arguments:
- velocity: float32 [4, 512, 4096], P('batch', 'rows'), parts along dimension 0, may hold values from -6 to 6
- cotangent: float32 [4, 512, 4096], P('batch', 'rows'), parts along dimension 0, may hold values from -6 to 6
- w_in: bfloat16 [64, 3, 3, 2], replicated, may hold values from -1.5 to 1.5
- w_mid: bfloat16 [64, 64], replicated, may hold values from -0.75 to 0.75
- w_out: bfloat16 [3, 3, 2, 64], replicated, may hold values from -0.25 to 0.25
Outputs:
- new_velocity: float32 [4, 512, 4096], P('batch', 'rows'), parts along dimension 0
- grad_in: float32 [128, 3, 3, 2], P('batch'), parts along dimension 0
- grad_mid: float32 [128, 64], P('batch'), parts along dimension 0
- grad_out: float32 [6, 3, 2, 64], P('batch'), parts along dimension 0
The draws below stay inside these ranges and needn't reach their ends.
There are 2 independent parts, one for each index of `batch`. The reference program is written for one: setup_inputs(seed, part) draws one part's arguments, and reference() takes and returns one part's arrays. A program takes and returns all parts, laid end to end along the dimension named above; an argument that names none is the same for every part. Nothing has to cross between parts.
All inputs are finite; a program needn't handle non-finite values.
Results may differ from the reference program's by a relative error of at most 0.007.
Values may be sent and summed in bfloat16 or wider, within the bound.
No kernel may reach another device: no remote copies, remote signals or barrier semaphores. Data moves between devices by JAX's collectives and lax.ppermute only.
A program may use at most 128 MiB of HBM per device.

```python
import math
import jax
import jax.numpy as jnp
from jax import lax

NY = 4096
HID = 64
NX = 512


def shard_levels(stream_key, shape, shards, least, largest):
    def one(dim, shards_of):
        draws = jax.random.uniform(jax.random.fold_in(jax.random.fold_in(stream_key, 6), dim), (shards_of,), jnp.float32, least / len(shards), largest / len(shards))
        return jnp.repeat(jnp.exp(draws), shape[dim] // shards_of).reshape((-1,) + (1,) * (len(shape) - dim - 1))

    factor_of = one(*shards[0])
    for cut in shards[1:]:
        factor_of = factor_of * one(*cut)
    return factor_of


def centred(stream_key, extent, deviation, bound, shards=(), held_as=jnp.bfloat16):
    values = deviation * jax.random.normal(stream_key, extent, jnp.float32)
    if shards:
        values = values * shard_levels(stream_key, extent, shards, -0.22, 0.18)
    return jnp.clip(values, -bound, bound).astype(held_as)


def setup_inputs(seed: int = 0, part: int = 0) -> dict:
    key_list = jax.random.split(jax.random.key(seed), 6)
    part_keys = jax.random.split(jax.random.fold_in(key_list[5], part), 6)
    return {
        "velocity": centred(part_keys[0], (2, NX, NY), 1.0, 6.0, ((1, 128),), jnp.float32),
        "cotangent": centred(part_keys[1], (2, NX, NY), 1.0, 6.0, ((1, 128),), jnp.float32),
        "w_in": centred(key_list[2], (HID, 3, 3, 2), 18 ** -0.5, 1.5),
        "w_mid": centred(key_list[3], (HID, HID), HID ** -0.5, 0.75),
        "w_out": centred(key_list[4], (3, 3, 2, HID), (9 * HID) ** -0.5, 0.25),
    }


STEP_SIZE = 0.5
GELU_SCALE = 0.7978845608028654
GELU_CUBIC = 0.044715
OFFSETS = ((-1, -1), (-1, 0), (-1, 1), (0, -1), (0, 0), (0, 1), (1, -1), (1, 0), (1, 1))

def gelu_value(pre):
    tangent = jnp.tanh(GELU_SCALE * (pre + GELU_CUBIC * pre * pre * pre))
    return 0.5 * pre * (1.0 + tangent)

def gelu_slope(pre):
    tangent = jnp.tanh(GELU_SCALE * (pre + GELU_CUBIC * pre * pre * pre))
    return 0.5 * (1.0 + tangent) + 0.5 * pre * (1.0 - tangent * tangent) * GELU_SCALE * (1.0 + 3.0 * GELU_CUBIC * pre * pre)

def stack_inputs(padded, width, offset, count):
    pieces = []
    for row_shift, col_shift in OFFSETS:
        start = width + offset + row_shift
        pieces.append(jnp.roll(padded[:, start:start + count], -col_shift, axis=2))
    return jnp.concatenate(pieces, axis=0)

def hidden_layers(stacked, w_in, w_mid):
    flat = stacked.reshape(stacked.shape[0], -1)
    pre_one = jnp.dot(w_in.reshape(w_in.shape[0], -1), flat, preferred_element_type=jnp.float32)
    act_one = gelu_value(pre_one).astype(jnp.bfloat16)
    pre_two = jnp.dot(w_mid, act_one, preferred_element_type=jnp.float32)
    act_two = gelu_value(pre_two).astype(jnp.bfloat16)
    return (pre_one, act_one, pre_two, act_two)

def conv_out(act_pad, w_out, count, columns):
    hidden = w_out.shape[3]
    outputs = jnp.dot(w_out.reshape(-1, hidden), act_pad, preferred_element_type=jnp.float32)
    outputs = outputs.reshape(9, w_out.shape[2], count + 2, columns)
    total = jnp.zeros((w_out.shape[2], count, columns), jnp.float32)
    for tap_index, (row_shift, col_shift) in enumerate(OFFSETS):
        window = outputs[tap_index, :, 1 + row_shift:1 + row_shift + count]
        total = total + jnp.roll(window, -col_shift, axis=2)
    return total

def advection(padded, width, count):
    rows_near = padded[:, width - 1:width + count + 1]
    flux_rows = rows_near[0:1] * rows_near
    flux_cols = rows_near[1:2] * rows_near
    middle = flux_cols[:, 1:-1]
    return 0.5 * (flux_rows[:, 2:] - flux_rows[:, :-2]) + 0.5 * (jnp.roll(middle, -1, axis=2) - jnp.roll(middle, 1, axis=2))

def own_rows(flat, count, columns):
    return flat.reshape(flat.shape[0], count + 2, columns)[:, 1:1 + count].reshape(flat.shape[0], -1)

def backward_block(dcorr_rim, stacked_own, pre_one_own, act_one_own, pre_two_own, act_pad, w_mid, w_out, count, columns):
    channels = dcorr_rim.shape[0]
    own = dcorr_rim[:, 1:1 + count]
    zero_rows = jnp.zeros((channels, 2, columns), dcorr_rim.dtype)
    zero_pad = jnp.concatenate([zero_rows, own, zero_rows], axis=1)
    shifted = []
    extended = []
    for row_shift, col_shift in OFFSETS:
        shifted.append(jnp.roll(dcorr_rim[:, 1 - row_shift:1 - row_shift + count], col_shift, axis=2))
        extended.append(jnp.roll(zero_pad[:, 1 - row_shift:1 - row_shift + count + 2], col_shift, axis=2))
    shifted = jnp.concatenate(shifted, axis=0).reshape(9 * channels, -1)
    extended = jnp.concatenate(extended, axis=0).reshape(9 * channels, -1)
    w_flat = w_out.reshape(9 * channels, -1)
    contract_last = (((1,), (1,)), ((), ()))
    contract_first = (((0,), (0,)), ((), ()))
    grad_out = lax.dot_general(extended, act_pad, contract_last, preferred_element_type=jnp.float32)
    back_two = lax.dot_general(w_flat, shifted, contract_first, preferred_element_type=jnp.float32)
    delta_two = (back_two * gelu_slope(pre_two_own)).astype(jnp.bfloat16)
    grad_mid = lax.dot_general(delta_two, act_one_own, contract_last, preferred_element_type=jnp.float32)
    back_one = lax.dot_general(w_mid, delta_two, contract_first, preferred_element_type=jnp.float32)
    delta_one = (back_one * gelu_slope(pre_one_own)).astype(jnp.bfloat16)
    grad_in = lax.dot_general(delta_one, stacked_own, contract_last, preferred_element_type=jnp.float32)
    return (grad_in, grad_mid, grad_out)

def wave_numbers(length):
    index = jnp.arange(length, dtype=jnp.int32)
    signed = jnp.where(2 * index < length, index, index - length)
    signed = jnp.where(2 * index == length, 0, signed)
    return signed.astype(jnp.float32) / length

def project(field):
    spectrum = jnp.fft.fft2(field, axes=(1, 2))
    wave_row = wave_numbers(NX)[:, None]
    wave_col = wave_numbers(NY)[None, :]
    square = wave_row * wave_row + wave_col * wave_col
    square = jnp.where(square > 0, square, 1.0)
    along = spectrum[0]
    across = spectrum[1]
    inner_product = (wave_row * along + wave_col * across) / square
    result = jnp.stack([along - wave_row * inner_product, across - wave_col * inner_product])
    return jnp.real(jnp.fft.ifft2(result, axes=(1, 2))).astype(jnp.float32)

def reference(velocity, cotangent, w_in, w_mid, w_out):
    channels = velocity.shape[0]
    block = math.gcd(NX, 64)
    count_blocks = NX // block
    padded = jnp.concatenate([velocity[:, -2:], velocity, velocity[:, :2]], axis=1)

    def network(index):
        window = lax.dynamic_slice_in_dim(padded, index * block, block + 4, 1)
        stacked = stack_inputs(window.astype(jnp.bfloat16), 2, -1, block + 2)
        return (window, stacked, hidden_layers(stacked, w_in, w_mid))

    def forward_block(index):
        window, stacked, layers = network(index)
        return conv_out(layers[3], w_out, block, NY) - advection(window, 2, block)
    change = lax.map(forward_block, jnp.arange(count_blocks, dtype=jnp.int32))
    change = jnp.transpose(change, (1, 0, 2, 3)).reshape(channels, NX, NY)
    provisional = velocity + STEP_SIZE * change
    new_velocity = project(provisional)
    grad_corr = (project(cotangent) * (STEP_SIZE / math.sqrt(NX * NY))).astype(jnp.bfloat16)
    corr_pad = jnp.concatenate([grad_corr[:, -1:], grad_corr, grad_corr[:, :1]], axis=1)

    def backward(index):
        window, stacked, layers = network(index)
        pre_one, act_one, pre_two, act_two = layers
        dcorr_rim = lax.dynamic_slice_in_dim(corr_pad, index * block, block + 2, 1)
        stacked_flat = stacked.reshape(stacked.shape[0], -1)
        return backward_block(dcorr_rim, own_rows(stacked_flat, block, NY), own_rows(pre_one, block, NY), own_rows(act_one, block, NY), own_rows(pre_two, block, NY), act_two, w_mid, w_out, block, NY)
    grads = lax.map(backward, jnp.arange(count_blocks, dtype=jnp.int32))
    grad_in = lax.optimization_barrier(jnp.sum(grads[0], axis=0)).reshape(w_in.shape)
    grad_mid = lax.optimization_barrier(jnp.sum(grads[1], axis=0))
    grad_out = lax.optimization_barrier(jnp.sum(grads[2], axis=0)).reshape(w_out.shape)
    return (new_velocity, grad_in, grad_mid, grad_out)
```

```python
import math

import jax
import jax.numpy as jnp
import ml_dtypes
import numpy as np
from jax import lax
from jax.experimental import pallas as pl
from jax.experimental.pallas import tpu as pltpu
from jax.sharding import PartitionSpec as P

STEP_SIZE = 0.5
GELU_SCALE = 0.7978845608028654
GELU_CUBIC = 0.044715
BF = jnp.bfloat16
F32 = jnp.float32
TILE = 256
VMEM_LIMIT = 48 * 1024 * 1024

R = 4
D = 128
NX = R * D
OUTER = 32
NY = OUTER * 128
C = OUTER // 2
CH = 2
HID = 64


def table_pair(matrix):
    high = np.asarray(matrix, np.float64).astype(ml_dtypes.bfloat16)
    low = (matrix - high.astype(np.float64)).astype(ml_dtypes.bfloat16)
    return np.stack([high, low])


def column_tables():
    a = np.arange(OUTER)
    b = np.arange(128)
    d = np.arange(D)
    c = np.arange(C)
    eye = np.eye(R * CH).reshape(CH, R, CH, R)
    sign = np.where(a % 2 == 0, 1.0, -1.0)
    angle = 2 * np.pi * np.outer(c, a) / OUTER
    first = np.stack([np.cos(angle), -np.sin(angle)])
    first[0, 0] = 1.0
    first[1, 0] = sign
    forward_a = np.einsum("pca,hrgs->phcrags", first, eye).reshape(256, 256)
    last = np.stack([2 * np.cos(angle), -2 * np.sin(angle)])
    last[0, 0] = 1.0
    last[1, 0] = sign
    last = last / NY
    inverse_a = np.einsum("pca,gshr->agsphcr", last, eye).reshape(256, 256)
    half = np.zeros((2, 4, CH, 2))
    for h in range(CH):
        for e in range(2):
            half[h, h * 2 + e, h, e] = 1.0
    rim = np.zeros((8, CH, 2))
    rim[:4] = np.eye(4).reshape(4, CH, 2)
    inverse_rim = np.einsum("pca,khr->akphcr", last, rim).reshape(256, 128)
    theta = 2 * np.pi * np.outer(c, b) / NY
    cosine = np.cos(theta)
    sine = np.sin(theta)
    cosine[0] = 1.0
    sine[0] = 0.0
    spread = lambda t, n: np.broadcast_to(t[None, :, None, :], (CH, C, n, 128)).reshape(-1, 128)
    twist = np.stack([spread(cosine, R), spread(sine, R)]).astype(np.float32)
    twist_rim = np.stack([spread(cosine, 2), spread(sine, 2)]).astype(np.float32)
    phi = 2 * np.pi * np.outer(d, b) / 128
    matrix = np.zeros((D, 2, 2, 128))
    matrix[:, 0, 0] = np.cos(phi)
    matrix[:, 0, 1] = np.sin(phi)
    matrix[:, 1, 0] = -np.sin(phi)
    matrix[:, 1, 1] = np.cos(phi)
    psi = 2 * np.pi * np.outer(16 + 32 * (d - 64), b) / NY
    alternate = np.where(b % 2 == 0, 1.0, -1.0)
    zero = np.zeros((D, 2, 2, 128))
    zero[:64, 0, 0] = np.cos(phi[:64])
    zero[:64, 1, 0] = -np.sin(phi[:64])
    zero[0, 1, 0] = alternate
    zero[64:, 0, 1] = np.cos(psi[64:])
    zero[64:, 1, 1] = -np.sin(psi[64:])
    back = np.zeros((2, 128, D, 2))
    back[0, :, :, 0] = np.cos(phi).T
    back[0, :, :, 1] = -np.sin(phi).T
    back[1, :, :, 0] = np.sin(phi).T
    back[1, :, :, 1] = np.cos(phi).T
    back_zero = np.zeros((2, 128, D, 2))
    back_zero[0, :, :64, 0] = 2 * np.cos(phi[:64]).T
    back_zero[0, :, :64, 1] = -2 * np.sin(phi[:64]).T
    back_zero[0, :, 0, 0] = 1.0
    back_zero[0, :, 0, 1] = alternate
    back_zero[1, :, 64:, 0] = 2 * np.cos(psi[64:]).T
    back_zero[1, :, 64:, 1] = -2 * np.sin(psi[64:]).T
    return {
        "forward_a": table_pair(forward_a),
        "forward_b": table_pair(matrix.reshape(256, 256)),
        "forward_b0": table_pair(zero.reshape(256, 256)),
        "twist": twist,
        "inverse_b": table_pair(back.reshape(256, 256)),
        "inverse_b0": table_pair(back_zero.reshape(256, 256)),
        "inverse_a": inverse_a,
        "inverse_rim": inverse_rim,
        "untwist": np.ascontiguousarray(twist.transpose(0, 2, 1)),
        "untwist_rim": np.ascontiguousarray(twist_rim.transpose(0, 2, 1)),
    }


def row_tables():
    s = np.arange(D)
    m1 = np.arange(D)
    m2 = np.arange(R)
    phi = 2 * np.pi * np.outer(m1, s) / D
    forward = np.zeros((2, D, D, 2))
    forward[0, :, :, 0] = np.cos(phi)
    forward[0, :, :, 1] = np.sin(phi)
    forward[1, :, :, 0] = -np.sin(phi)
    forward[1, :, :, 1] = np.cos(phi)
    inverse = np.zeros((D, 2, 2, D))
    inverse[:, 0, 0] = np.cos(phi).T
    inverse[:, 0, 1] = -np.sin(phi).T
    inverse[:, 1, 0] = np.sin(phi).T
    inverse[:, 1, 1] = np.cos(phi).T
    inverse = inverse / NX
    eye = np.eye(CH * C)

    def short(rows, flip):
        angle = 2 * np.pi * np.outer(m2, rows) / R
        block = np.zeros((2, R, 2, len(rows)))
        block[0, :, 0] = np.cos(angle)
        block[1, :, 0] = -np.sin(angle) * flip
        block[0, :, 1] = np.sin(angle) * flip
        block[1, :, 1] = np.cos(angle)
        block = np.round(block)
        return np.einsum("pmqr,gk->pgmqkr", block, eye).reshape(2 * CH * C * R, 2, -1)

    own = np.arange(R)
    rim = np.array([-1, R])
    rim_block = np.zeros((256, 2, 128))
    rim_block[:, :, :64] = short(rim, 1.0)

    def lanes(rows):
        theta = 2 * np.pi * np.outer(m1, rows) / NX
        both = np.stack([np.cos(theta), np.sin(theta)])
        wide = np.broadcast_to(both[:, :, None, :], (2, D, CH * C, len(rows))).reshape(2, D, -1)
        out = np.zeros((2, D, 128), np.float32)
        out[:, :, : wide.shape[2]] = wide
        return out

    return {
        "row_forward": table_pair(forward.reshape(256, 256)),
        "row_inverse": table_pair(inverse.reshape(256, 256)),
        "short_forward": short(own, -1.0).reshape(256, 256).astype(ml_dtypes.bfloat16),
        "short_inverse": short(own, 1.0).reshape(256, 256).astype(ml_dtypes.bfloat16),
        "short_rim": rim_block.reshape(256, 256).astype(ml_dtypes.bfloat16),
        "spin": lanes(own),
        "spin_rim": lanes(rim),
    }


def velocity_row(ch, row):
    if 0 <= row < R:
        return ch * R + row
    return 8 + ch * 2 + row + 2 if row < 0 else 12 + ch * 2 + row - R


def dual_row(ch, row):
    if 0 <= row < R:
        return ch * R + row
    return 8 + ch * 2 + (0 if row < 0 else 1)


def network_tables():
    taps = np.zeros((6, 18, 48))
    for i in range(-1, 5):
        for a in range(-1, 2):
            for b in range(-1, 2):
                for ch in range(CH):
                    t = (3 * (a + 1) + b + 1) * 2 + ch
                    taps[i + 1, t, (b + 1) * 16 + velocity_row(ch, i + a)] = 1
    outs = np.zeros((6, 24, 18))
    for k in range(-1, 5):
        for a in range(-1, 2):
            i = k - a
            if 0 <= i < R:
                for b in range(-1, 2):
                    for o in range(CH):
                        outs[k + 1, (b + 1) * 8 + o * R + i, (3 * (a + 1) + b + 1) * 2 + o] = 1
    duals = np.zeros((R, 18, 48))
    for i in range(R):
        for a in range(-1, 2):
            for b in range(-1, 2):
                for o in range(CH):
                    t = (3 * (a + 1) + b + 1) * 2 + o
                    duals[i, t, (b + 1) * 16 + dual_row(o, i - a)] = 1
    place_mid = np.zeros((64, 128))
    place_mid[:, :64] = np.eye(64)
    place_in = np.zeros((R, 48, 128))
    place_in[:, :, 64:82] = taps[1:5].transpose(0, 2, 1)
    place_out = np.zeros((R, 48, 128))
    place_out[:, :, 82:100] = duals.transpose(0, 2, 1)
    spread = np.zeros((64, 2, 2, 2, 64))
    for h in range(64):
        for core in range(2):
            for part in range(2):
                spread[h, core, part, part, h] = 1
    low = lambda t: t.astype(ml_dtypes.bfloat16)
    return {
        "taps": low(taps),
        "outs": low(outs),
        "duals": low(duals),
        "place_mid": low(place_mid),
        "place_in": low(place_in),
        "place_out": low(place_out),
        "spread": low(spread.reshape(256, 128)),
    }


def dot(x, y):
    return jnp.dot(x, y, preferred_element_type=F32)


def dot_nt(x, y):
    return lax.dot_general(x, y, (((1,), (1,)), ((), ())), preferred_element_type=F32)


def dot_tn(x, y):
    return lax.dot_general(x, y, (((0,), (0,)), ((), ())), preferred_element_type=F32)


def halves(x):
    high = x.astype(BF)
    return high, (x - high.astype(F32)).astype(BF)


def exact(form, pair, x):
    high, low = halves(x)
    return form(pair[0], high) + (form(pair[1], high) + form(pair[0], low))


def pair_low(form, pair, x):
    return form(pair[0], x) + form(pair[1], x)


def to_blocks(x):
    return jnp.concatenate([x[:, 128 * a : 128 * a + 128] for a in range(OUTER)], axis=0)


def from_blocks(x):
    rows = x.shape[0] // OUTER
    return jnp.concatenate([x[rows * a : rows * a + rows] for a in range(OUTER)], axis=1)


def column_forward(x, forward_a, forward_b, forward_b0, twist):
    y = exact(dot, forward_a, to_blocks(x))
    real, imag = y[:128], y[128:]
    cosine, sine = twist[0], twist[1]
    both = jnp.concatenate([real * cosine + imag * sine, imag * cosine - real * sine], axis=1)
    general = exact(dot_nt, forward_b, both)
    zero = exact(dot_nt, forward_b0, both)
    lane = lax.broadcasted_iota(jnp.int32, general.shape, 1)
    return jnp.where(lane % 64 < R, zero, general).astype(BF)


def column_inverse_first(x, inverse_b, inverse_b0, untwist, period, width):
    general = pair_low(dot, inverse_b, x)
    zero = pair_low(dot, inverse_b0, x)
    lane = lax.broadcasted_iota(jnp.int32, general.shape, 1)
    y = jnp.where(lane % period < width, zero, general)
    real, imag = y[:128], y[128:]
    cosine, sine = untwist[0], untwist[1]
    return real * cosine - imag * sine, imag * cosine + real * sine


def spectral(x, device, row_forward, short_forward, spin):
    v = pair_low(dot, row_forward, x)
    real, imag = v[:128], v[128:]
    cosine, sine = spin[0], spin[1]
    both = jnp.concatenate([real * cosine + imag * sine, imag * cosine - real * sine], axis=1)
    high, low = halves(both)
    full = dot(high, short_forward) + dot(low, short_forward)
    m1 = lax.broadcasted_iota(jnp.int32, (128, 128), 0)
    lane = lax.broadcasted_iota(jnp.int32, (128, 128), 1)
    m = m1 + 128 * (lane % R)
    m = jnp.where(2 * m < NX, m, jnp.where(2 * m == NX, 0, m - NX))
    c = (lane % 64) // R
    n = c + OUTER * device
    n = jnp.where(2 * n < NY, n, n - NY)
    packed = jnp.where(device < 64, OUTER * device, 16 + OUTER * (device - 64))
    n = jnp.where(c == 0, packed, n)
    wave_row = m.astype(F32) * (1.0 / NX)
    wave_col = n.astype(F32) * (1.0 / NY)
    row_square = wave_row * wave_row
    col_square = wave_col * wave_col
    square = row_square + col_square
    some = square > 0
    inverse = 1.0 / jnp.where(some, square, 1.0)
    same = jnp.where(some, jnp.where(lane < 64, col_square, row_square) * inverse, 1.0)
    cross = -(wave_row * wave_col) * inverse
    real, imag = full[:, :128], full[:, 128:]
    real = same * real + cross * pltpu.roll(real, 64, 1)
    imag = same * imag + cross * pltpu.roll(imag, 64, 1)
    return jnp.concatenate([real, imag], axis=1)


def row_back(both, row_inverse, short, spin):
    high, low = halves(both)
    full = dot(high, short) + dot(low, short)
    real, imag = full[:, :128], full[:, 128:]
    cosine, sine = spin[0], spin[1]
    v = jnp.concatenate([real * cosine - imag * sine, imag * cosine + real * sine], axis=0)
    return exact(dot, row_inverse, v).astype(BF)


def gelu_parts(pre):
    square = pre * pre
    tangent = jnp.tanh(pre * (GELU_SCALE + (GELU_SCALE * GELU_CUBIC) * square))
    gate = 0.5 + 0.5 * tangent
    return square, gate, pre * gate


def slope_of(square, gate, value):
    return gate + value * (1.0 - gate) * (2 * GELU_SCALE + (6 * GELU_SCALE * GELU_CUBIC) * square)


def dual_kernel(field, forward_a, forward_b, forward_b0, twist, sent):
    x = jnp.concatenate([field[0], field[1]], axis=0)
    sent[...] = column_forward(x, forward_a, forward_b, forward_b0, twist).reshape(D, 2, 128)


def network_kernel(
    velocity,
    before,
    after,
    w_in,
    w_mid,
    w_out,
    taps,
    outs,
    forward_a,
    forward_b,
    forward_b0,
    twist,
    sent,
    act_one,
    act_two,
    slope_one,
    slope_two,
    stack,
    act_all,
    partial,
):
    own = jnp.concatenate([velocity[0], velocity[1]], axis=0)
    low_before = before[...].astype(F32)
    low_after = after[...].astype(F32)
    base = jnp.concatenate([own, low_before, low_after], axis=0)
    stack[0:16, :] = pltpu.roll(base, 1, 1).astype(BF)
    stack[16:32, :] = base.astype(BF)
    stack[32:48, :] = pltpu.roll(base, NY - 1, 1).astype(BF)
    first = jnp.concatenate([dot(w_in[...], taps[i]).astype(BF) for i in range(6)], axis=0)
    third = jnp.concatenate([dot(outs[i], w_out[...]).astype(BF) for i in range(6)], axis=1)
    middle = w_mid[...]

    def step(index, _):
        at = pl.ds(pl.multiple_of(index * TILE, TILE), TILE)
        pre = dot(first, stack[:, at])
        for i in range(6):
            keep = 1 <= i <= R
            rows = pl.ds(64 * (i - 1), 64)
            square, gate, value = gelu_parts(pre[64 * i : 64 * i + 64])
            low = value.astype(BF)
            if keep:
                act_one[rows, at] = low
                slope_one[rows, at] = slope_of(square, gate, value).astype(BF)
            square, gate, value = gelu_parts(dot(middle, low))
            low = value.astype(BF)
            act_all[pl.ds(64 * i, 64), :] = low
            if keep:
                act_two[rows, at] = low
                slope_two[rows, at] = slope_of(square, gate, value).astype(BF)
        partial[:, at] = dot(third, act_all[...])
        return 0

    lax.fori_loop(0, NY // TILE, step, 0)
    correction = (
        pltpu.roll(partial[0:8, :], 1, 1) + partial[8:16, :] + pltpu.roll(partial[16:24, :], NY - 1, 1)
    )
    extended = [
        jnp.concatenate([low_before[2 * c + 1 : 2 * c + 2], velocity[c], low_after[2 * c : 2 * c + 1]], axis=0)
        for c in range(CH)
    ]
    across = velocity[1]
    pieces = []
    for c in range(CH):
        flux = extended[0] * extended[c]
        side = across * velocity[c]
        pieces.append(
            (flux[2:] - flux[:-2]) + (pltpu.roll(side, NY - 1, 1) - pltpu.roll(side, 1, 1))
        )
    advect = 0.5 * jnp.concatenate(pieces, axis=0)
    provisional = own + STEP_SIZE * (correction - advect)
    sent[...] = column_forward(provisional, forward_a, forward_b, forward_b0, twist).reshape(D, 2, 128)


def middle_kernel(
    device, got, other, row_forward, row_inverse, short_forward, short_inverse, short_rim, spin, spin_rim, sent
):
    both = spectral(got[...].reshape(256, 128), device[0], row_forward, short_forward[...], spin)
    sent[:, 0] = row_back(both, row_inverse, short_inverse[...], spin).reshape(D, 2, 128)
    sent[:, 1] = row_back(both, row_inverse, short_rim[...], spin_rim).reshape(D, 2, 128)
    sent[:, 2] = other[...]


def backward_kernel(
    device,
    got,
    act_one,
    act_two,
    slope_one,
    slope_two,
    stack,
    w_mid,
    w_out,
    duals,
    place_mid,
    place_in,
    place_out,
    spread,
    row_forward,
    row_inverse,
    short_forward,
    short_inverse,
    spin,
    inverse_b,
    inverse_b0,
    inverse_a,
    inverse_rim,
    untwist,
    untwist_rim,
    sent,
    dual_stack,
    sum_mid,
    sum_in,
    sum_out,
):
    both = spectral(got[:, 2].reshape(256, 128), device[0], row_forward, short_forward[...], spin)
    sent[:, 0] = row_back(both, row_inverse, short_inverse[...], spin).reshape(D, 2, 128)
    real, imag = column_inverse_first(got[:, 0].reshape(256, 128), inverse_b, inverse_b0, untwist, 64, R)
    own = exact(dot_nt, inverse_a, jnp.concatenate([real, imag], axis=1))
    rim = got[:, 1].reshape(256, 128)
    real, imag = column_inverse_first(rim[:, :64], inverse_b, inverse_b0, untwist_rim, 32, 2)
    rim = exact(dot_nt, inverse_rim, jnp.concatenate([real, imag], axis=1))
    base = jnp.concatenate([from_blocks(own), from_blocks(rim)], axis=0)
    dual_stack[0:16, :] = pltpu.roll(base, NY - 1, 1).astype(BF)
    dual_stack[16:32, :] = base.astype(BF)
    dual_stack[32:48, :] = pltpu.roll(base, 1, 1).astype(BF)
    spread_out = jnp.concatenate([dot_tn(w_out[...], duals[i]).astype(BF) for i in range(R)], axis=0)
    middle = w_mid[...]
    sum_mid[...] = jnp.zeros_like(sum_mid)
    sum_in[...] = jnp.zeros_like(sum_in)
    sum_out[...] = jnp.zeros_like(sum_out)

    def step(index, _):
        at = pl.ds(pl.multiple_of(index * TILE, TILE), TILE)
        dual = dual_stack[:, at]
        back_two = dot(spread_out, dual)
        delta_two = (back_two * slope_two[:, at].astype(F32)).astype(BF)
        hidden = act_one[:, at]
        wide = lambda t: jnp.concatenate([t[64 * i : 64 * i + 64] for i in range(R)], axis=1)
        wide_two = wide(delta_two)
        sum_mid[...] += dot_nt(wide_two, wide(hidden))
        back_one = dot_tn(middle, wide_two)
        tall = jnp.concatenate([back_one[:, TILE * i : TILE * i + TILE] for i in range(R)], axis=0)
        delta_one = (tall * slope_one[:, at].astype(F32)).astype(BF)
        sum_in[...] += dot_nt(delta_one, stack[:, at])
        sum_out[...] += dot_nt(act_two[:, at], dual)
        return 0

    lax.fori_loop(0, NY // TILE, step, 0)
    high, low = halves(sum_mid[...])
    total = dot(high, place_mid[...]) + dot(low, place_mid[...])
    for source, place in ((sum_in, place_in), (sum_out, place_out)):
        for i in range(R):
            high, low = halves(source[64 * i : 64 * i + 64, :])
            total = total + (dot(high, place[i]) + dot(low, place[i]))
    high, low = halves(total)
    sent[:, 1] = dot(spread[...], jnp.concatenate([high, low], axis=0)).astype(BF).reshape(D, 2, 128)


def sum_kernel(got, total):
    ones = jnp.ones((64, 256), BF)
    total[...] = dot(ones, got[:, 1].reshape(256, 128))


def field_kernel(got, inverse_b, inverse_b0, inverse_a, untwist, field):
    real, imag = column_inverse_first(got[:, 0].reshape(256, 128), inverse_b, inverse_b0, untwist, 64, R)
    x = from_blocks(exact(dot_nt, inverse_a, jnp.concatenate([real, imag], axis=1)))
    field[0] = x[:R]
    field[1] = x[R:]


def call(kernel, outputs, inputs, scratch=(), scalars=0):
    vmem = pl.BlockSpec(memory_space=pltpu.VMEM)
    smem = pl.BlockSpec(memory_space=pltpu.SMEM)
    single = not isinstance(outputs, list)
    return pl.pallas_call(
        kernel,
        out_shape=outputs,
        in_specs=[smem] * scalars + [vmem] * (len(inputs) - scalars),
        out_specs=vmem if single else [vmem] * len(outputs),
        scratch_shapes=list(scratch),
        compiler_params=pltpu.CompilerParams(vmem_limit_bytes=VMEM_LIMIT),
    )(*inputs)


def exchange(x, groups=None):
    return lax.all_to_all(x, "rows", split_axis=0, concat_axis=0, tiled=True, axis_index_groups=groups)


def body(velocity, cotangent, w_in, w_mid, w_out):
    columns = column_tables()
    rows = row_tables()
    net = network_tables()
    scale = STEP_SIZE / math.sqrt(NX * NY)
    shape = jax.ShapeDtypeStruct
    flat_in = w_in.reshape(HID, 18)
    flat_out = w_out.reshape(18, HID)
    device = lax.axis_index("rows").reshape(1)
    size = D
    up = [(i, (i + 1) % size) for i in range(size)]
    down = [(j, i) for i, j in up]
    low = velocity.astype(BF)
    before = lax.ppermute(low[:, R - 2 :].reshape(4, NY), "rows", up)
    after = lax.ppermute(low[:, :2].reshape(4, NY), "rows", down)

    forward = [columns[k] for k in ("forward_a", "forward_b", "forward_b0", "twist")]
    dual_sent = call(dual_kernel, shape((D, 2, 128), BF), [cotangent, *forward])
    dual_got = exchange(dual_sent)

    big = shape((R * HID, NY), BF)
    field_sent, act_one, act_two, slope_one, slope_two, stack = call(
        network_kernel,
        [shape((D, 2, 128), BF), big, big, big, big, shape((48, NY), BF)],
        [velocity, before, after, flat_in, w_mid, flat_out, net["taps"], net["outs"], *forward],
        [pltpu.VMEM((6 * HID, TILE), BF), pltpu.VMEM((24, NY), F32)],
    )
    middle = [rows[k] for k in ("row_forward", "row_inverse", "short_forward", "short_inverse")]
    second_sent = call(
        middle_kernel,
        shape((D, 3, 2, 128), BF),
        [device, dual_got, field_sent, *middle, rows["short_rim"], rows["spin"], rows["spin_rim"]],
        scalars=1,
    )
    second_got = exchange(second_sent)
    third_sent = call(
        backward_kernel,
        shape((D, 2, 2, 128), BF),
        [
            device,
            second_got,
            act_one,
            act_two,
            slope_one,
            slope_two,
            stack,
            w_mid,
            flat_out,
            net["duals"],
            net["place_mid"],
            net["place_in"],
            net["place_out"],
            net["spread"],
            *middle,
            rows["spin"],
            columns["inverse_b"],
            columns["inverse_b0"],
            table_pair(columns["inverse_a"] * scale),
            table_pair(columns["inverse_rim"] * scale),
            columns["untwist"],
            columns["untwist_rim"],
        ],
        [
            pltpu.VMEM((48, NY), BF),
            pltpu.VMEM((HID, HID), F32),
            pltpu.VMEM((R * HID, 48), F32),
            pltpu.VMEM((R * HID, 48), F32),
        ],
        scalars=1,
    )
    third_got = exchange(third_sent)
    total = call(sum_kernel, shape((64, 128), F32), [third_got])
    groups = [[2 * h + core for h in range(64)] for core in range(2)]
    grads = exchange(total.reshape(64, 1, 128), groups).reshape(64, 128)
    new_velocity = call(
        field_kernel,
        shape((CH, R, NY), F32),
        [third_got, columns["inverse_b"], columns["inverse_b0"], table_pair(columns["inverse_a"]), columns["untwist"]],
    )
    grad_mid = grads[:, :64]
    grad_in = grads[:, 64:82].reshape(HID, 3, 3, 2)
    grad_out = grads[:, 82:100].T.reshape(3, 3, 2, HID)
    return new_velocity, grad_in, grad_mid, grad_out


def solution(mesh):
    in_specs = (P("batch", "rows", None), P("batch", "rows", None), P(), P(), P())
    out_specs = (
        P("batch", "rows", None),
        P("batch", None, None, None),
        P("batch", None),
        P("batch", None, None, None),
    )
    return jax.shard_map(body, mesh=mesh, in_specs=in_specs, out_specs=out_specs, check_vma=False)
```

```python
import functools
import math

import jax
import jax.numpy as jnp
import ml_dtypes
import numpy as np
from jax import lax
from jax.experimental import pallas as pl
from jax.experimental.pallas import tpu as pltpu
from jax.sharding import PartitionSpec as P

STEP_SIZE = 0.5
GELU_SCALE = 0.7978845608028654
GELU_CUBIC = 0.044715
BF = jnp.bfloat16
F32 = jnp.float32
TILE = 1024
VMEM_LIMIT = 24 * 1024 * 1024

R = 4
D = 128
NX = R * D
OUTER = 32
NY = OUTER * 128
C = OUTER // 2
CH = 2
HID = 64


def table_pair(matrix):
    high = np.asarray(matrix, np.float64).astype(ml_dtypes.bfloat16)
    low = (matrix - high.astype(np.float64)).astype(ml_dtypes.bfloat16)
    return np.stack([high, low])


def column_tables():
    a = np.arange(OUTER)
    b = np.arange(128)
    d = np.arange(D)
    c = np.arange(C)
    eye = np.eye(R * CH).reshape(CH, R, CH, R)
    sign = np.where(a % 2 == 0, 1.0, -1.0)
    angle = 2 * np.pi * np.outer(c, a) / OUTER
    first = np.stack([np.cos(angle), -np.sin(angle)])
    first[0, 0] = 1.0
    first[1, 0] = sign
    forward_a = np.einsum("pca,hrgs->phcrags", first, eye).reshape(256, 256)
    last = np.stack([2 * np.cos(angle), -2 * np.sin(angle)])
    last[0, 0] = 1.0
    last[1, 0] = sign
    last = last / NY
    inverse_a = np.einsum("pca,gshr->agsphcr", last, eye).reshape(256, 256)
    half = np.zeros((2, 4, CH, 2))
    for h in range(CH):
        for e in range(2):
            half[h, h * 2 + e, h, e] = 1.0
    rim = np.zeros((8, CH, 2))
    rim[:4] = np.eye(4).reshape(4, CH, 2)
    inverse_rim = np.einsum("pca,khr->akphcr", last, rim).reshape(256, 128)
    theta = 2 * np.pi * np.outer(c, b) / NY
    cosine = np.cos(theta)
    sine = np.sin(theta)
    cosine[0] = 1.0
    sine[0] = 0.0
    spread = lambda t, n: np.broadcast_to(t[None, :, None, :], (CH, C, n, 128)).reshape(-1, 128)
    twist = np.stack([spread(cosine, R), spread(sine, R)]).astype(np.float32)
    twist_rim = np.stack([spread(cosine, 2), spread(sine, 2)]).astype(np.float32)
    phi = 2 * np.pi * np.outer(d, b) / 128
    matrix = np.zeros((D, 2, 2, 128))
    matrix[:, 0, 0] = np.cos(phi)
    matrix[:, 0, 1] = np.sin(phi)
    matrix[:, 1, 0] = -np.sin(phi)
    matrix[:, 1, 1] = np.cos(phi)
    psi = 2 * np.pi * np.outer(16 + 32 * (d - 64), b) / NY
    alternate = np.where(b % 2 == 0, 1.0, -1.0)
    zero = np.zeros((D, 2, 2, 128))
    zero[:64, 0, 0] = np.cos(phi[:64])
    zero[:64, 1, 0] = -np.sin(phi[:64])
    zero[0, 1, 0] = alternate
    zero[64:, 0, 1] = np.cos(psi[64:])
    zero[64:, 1, 1] = -np.sin(psi[64:])
    back = np.zeros((2, 128, D, 2))
    back[0, :, :, 0] = np.cos(phi).T
    back[0, :, :, 1] = -np.sin(phi).T
    back[1, :, :, 0] = np.sin(phi).T
    back[1, :, :, 1] = np.cos(phi).T
    back_zero = np.zeros((2, 128, D, 2))
    back_zero[0, :, :64, 0] = 2 * np.cos(phi[:64]).T
    back_zero[0, :, :64, 1] = -2 * np.sin(phi[:64]).T
    back_zero[0, :, 0, 0] = 1.0
    back_zero[0, :, 0, 1] = alternate
    back_zero[1, :, 64:, 0] = 2 * np.cos(psi[64:]).T
    back_zero[1, :, 64:, 1] = -2 * np.sin(psi[64:]).T
    return {
        "forward_a": table_pair(forward_a),
        "forward_b": table_pair(matrix.reshape(256, 256)),
        "forward_b0": table_pair(zero.reshape(256, 256)),
        "twist": twist,
        "inverse_b": table_pair(back.reshape(256, 256)),
        "inverse_b0": table_pair(back_zero.reshape(256, 256)),
        "inverse_a": inverse_a,
        "inverse_rim": inverse_rim,
        "untwist": np.ascontiguousarray(twist.transpose(0, 2, 1)),
        "untwist_rim": np.ascontiguousarray(twist_rim.transpose(0, 2, 1)),
    }


def row_tables():
    s = np.arange(D)
    m1 = np.arange(D)
    m2 = np.arange(R)
    phi = 2 * np.pi * np.outer(m1, s) / D
    forward = np.zeros((2, D, D, 2))
    forward[0, :, :, 0] = np.cos(phi)
    forward[0, :, :, 1] = np.sin(phi)
    forward[1, :, :, 0] = -np.sin(phi)
    forward[1, :, :, 1] = np.cos(phi)
    inverse = np.zeros((D, 2, 2, D))
    inverse[:, 0, 0] = np.cos(phi).T
    inverse[:, 0, 1] = -np.sin(phi).T
    inverse[:, 1, 0] = np.sin(phi).T
    inverse[:, 1, 1] = np.cos(phi).T
    inverse = inverse / NX
    eye = np.eye(CH * C)

    def short(rows, flip):
        angle = 2 * np.pi * np.outer(m2, rows) / R
        block = np.zeros((2, R, 2, len(rows)))
        block[0, :, 0] = np.cos(angle)
        block[1, :, 0] = -np.sin(angle) * flip
        block[0, :, 1] = np.sin(angle) * flip
        block[1, :, 1] = np.cos(angle)
        block = np.round(block)
        return np.einsum("pmqr,gk->pgmqkr", block, eye).reshape(2 * CH * C * R, 2, -1)

    own = np.arange(R)
    rim = np.array([-1, R])
    rim_block = np.zeros((256, 2, 128))
    rim_block[:, :, :64] = short(rim, 1.0)

    def lanes(rows):
        theta = 2 * np.pi * np.outer(m1, rows) / NX
        both = np.stack([np.cos(theta), np.sin(theta)])
        wide = np.broadcast_to(both[:, :, None, :], (2, D, CH * C, len(rows))).reshape(2, D, -1)
        out = np.zeros((2, D, 128), np.float32)
        out[:, :, : wide.shape[2]] = wide
        return out

    return {
        "row_forward": table_pair(forward.reshape(256, 256)),
        "row_inverse": table_pair(inverse.reshape(256, 256)),
        "short_forward": short(own, -1.0).reshape(256, 256).astype(ml_dtypes.bfloat16),
        "short_inverse": short(own, 1.0).reshape(256, 256).astype(ml_dtypes.bfloat16),
        "short_rim": rim_block.reshape(256, 256).astype(ml_dtypes.bfloat16),
        "spin": lanes(own),
        "spin_rim": lanes(rim),
    }


def velocity_row(ch, row):
    if 0 <= row < R:
        return ch * R + row
    return 8 + ch * 2 + row + 2 if row < 0 else 12 + ch * 2 + row - R


def dual_row(ch, row):
    if 0 <= row < R:
        return ch * R + row
    return 8 + ch * 2 + (0 if row < 0 else 1)


def network_tables():
    taps = np.zeros((6, 18, 48))
    for i in range(-1, 5):
        for a in range(-1, 2):
            for b in range(-1, 2):
                for ch in range(CH):
                    t = (3 * (a + 1) + b + 1) * 2 + ch
                    taps[i + 1, t, (b + 1) * 16 + velocity_row(ch, i + a)] = 1
    outs = np.zeros((6, 24, 18))
    for k in range(-1, 5):
        for a in range(-1, 2):
            i = k - a
            if 0 <= i < R:
                for b in range(-1, 2):
                    for o in range(CH):
                        outs[k + 1, (b + 1) * 8 + o * R + i, (3 * (a + 1) + b + 1) * 2 + o] = 1
    duals = np.zeros((R, 18, 48))
    for i in range(R):
        for a in range(-1, 2):
            for b in range(-1, 2):
                for o in range(CH):
                    t = (3 * (a + 1) + b + 1) * 2 + o
                    duals[i, t, (b + 1) * 16 + dual_row(o, i - a)] = 1
    place_mid = np.zeros((64, 128))
    place_mid[:, :64] = np.eye(64)
    place_in = np.zeros((R, 48, 128))
    place_in[:, :, 64:82] = taps[1:5].transpose(0, 2, 1)
    place_out = np.zeros((R, 48, 128))
    place_out[:, :, 82:100] = duals.transpose(0, 2, 1)
    low = lambda t: t.astype(ml_dtypes.bfloat16)
    return {
        "taps": low(taps),
        "outs": low(outs),
        "duals": low(duals),
        "place_mid": low(place_mid),
        "place_in": low(place_in),
        "place_out": low(place_out),
    }


def dot(x, y):
    return jnp.dot(x, y, preferred_element_type=F32)


def dot_nt(x, y):
    return lax.dot_general(x, y, (((1,), (1,)), ((), ())), preferred_element_type=F32)


def dot_tn(x, y):
    return lax.dot_general(x, y, (((0,), (0,)), ((), ())), preferred_element_type=F32)


def halves(x):
    high = x.astype(BF)
    return high, (x - high.astype(F32)).astype(BF)


def exact(form, pair, x):
    high, low = halves(x)
    return form(pair[0], high) + (form(pair[1], high) + form(pair[0], low))


def pair_low(form, pair, x):
    return form(pair[0], x) + form(pair[1], x)


def to_blocks(x):
    return jnp.concatenate([x[:, 128 * a : 128 * a + 128] for a in range(OUTER)], axis=0)


def from_blocks(x):
    rows = x.shape[0] // OUTER
    return jnp.concatenate([x[rows * a : rows * a + rows] for a in range(OUTER)], axis=1)


def column_forward(x, forward_a, forward_b, forward_b0, twist):
    y = exact(dot, forward_a, to_blocks(x))
    real, imag = y[:128], y[128:]
    cosine, sine = twist[0], twist[1]
    both = jnp.concatenate([real * cosine + imag * sine, imag * cosine - real * sine], axis=1)
    general = exact(dot_nt, forward_b, both)
    zero = exact(dot_nt, forward_b0, both)
    lane = lax.broadcasted_iota(jnp.int32, general.shape, 1)
    return jnp.where(lane % 64 < R, zero, general).astype(BF)


def column_inverse_first(x, inverse_b, inverse_b0, untwist, period, width):
    general = pair_low(dot, inverse_b, x)
    zero = pair_low(dot, inverse_b0, x)
    lane = lax.broadcasted_iota(jnp.int32, general.shape, 1)
    y = jnp.where(lane % period < width, zero, general)
    real, imag = y[:128], y[128:]
    cosine, sine = untwist[0], untwist[1]
    return real * cosine - imag * sine, imag * cosine + real * sine


def multiplier(device):
    m1 = lax.broadcasted_iota(jnp.int32, (128, 128), 0)
    lane = lax.broadcasted_iota(jnp.int32, (128, 128), 1)
    m = m1 + 128 * (lane % R)
    m = jnp.where(2 * m < NX, m, jnp.where(2 * m == NX, 0, m - NX))
    c = (lane % 64) // R
    n = c + OUTER * device
    n = jnp.where(2 * n < NY, n, n - NY)
    packed = jnp.where(device < 64, OUTER * device, 16 + OUTER * (device - 64))
    n = jnp.where(c == 0, packed, n)
    wave_row = m.astype(F32) * (1.0 / NX)
    wave_col = n.astype(F32) * (1.0 / NY)
    row_square = wave_row * wave_row
    col_square = wave_col * wave_col
    square = row_square + col_square
    some = square > 0
    inverse = 1.0 / jnp.where(some, square, 1.0)
    same = jnp.where(some, jnp.where(lane < 64, col_square, row_square) * inverse, 1.0)
    return same, -(wave_row * wave_col) * inverse


def side_by_side(parts):
    return jnp.concatenate(parts, axis=1)


def gelu_parts(pre):
    square = pre * pre
    tangent = jnp.tanh(pre * (GELU_SCALE + (GELU_SCALE * GELU_CUBIC) * square))
    gate = 0.5 + 0.5 * tangent
    return square, gate, pre * gate


def slope_of(square, gate, value):
    return gate + value * (1.0 - gate) * (2 * GELU_SCALE + (6 * GELU_SCALE * GELU_CUBIC) * square)


def dual_kernel(field, forward_a, forward_b, forward_b0, twist, sent):
    x = jnp.concatenate([field[0], field[1]], axis=0)
    sent[...] = column_forward(x, forward_a, forward_b, forward_b0, twist).reshape(D, 2, 128)


def network_kernel(
    dual_sent,
    before,
    after,
    velocity,
    w_in,
    w_mid,
    w_out,
    taps,
    outs,
    forward_a,
    forward_b,
    forward_b0,
    twist,
    sent,
    act_one_out,
    act_two_out,
    slope_one_out,
    slope_two_out,
    stack_out,
    act_one,
    act_two,
    slope_one,
    slope_two,
    stack,
    act_all,
    partial,
    semaphores,
):
    sent[:, 1] = dual_sent[...]
    held = (act_one, act_two, slope_one, slope_two)
    homes = (act_one_out, act_two_out, slope_one_out, slope_two_out)
    whole = pltpu.make_async_copy(stack, stack_out, semaphores.at[4, 0])
    own = jnp.concatenate([velocity[0], velocity[1]], axis=0)
    low_before = before[...].astype(F32)
    low_after = after[...].astype(F32)
    base = jnp.concatenate([own, low_before, low_after], axis=0)
    stack[0:16, :] = pltpu.roll(base, 1, 1).astype(BF)
    stack[16:32, :] = base.astype(BF)
    stack[32:48, :] = pltpu.roll(base, NY - 1, 1).astype(BF)
    whole.start()
    velocity, w_out = velocity.ready(), w_out.ready()
    first = jnp.concatenate([dot(w_in[...], taps[i]).astype(BF) for i in range(6)], axis=0)
    third = jnp.concatenate([dot(outs[i], w_out[...]).astype(BF) for i in range(6)], axis=1)
    middle = w_mid[...]

    def step(index, _):
        at = pl.ds(pl.multiple_of(index * TILE, TILE), TILE)
        pre = dot(first, stack[:, at])
        for i in range(6):
            keep = 1 <= i <= R
            rows = pl.ds(64 * (i - 1), 64)
            square, gate, value = gelu_parts(pre[64 * i : 64 * i + 64])
            low = value.astype(BF)
            if keep:
                act_one[rows, at] = low
                slope_one[rows, at] = slope_of(square, gate, value).astype(BF)
            square, gate, value = gelu_parts(dot(middle, low))
            low = value.astype(BF)
            act_all[pl.ds(64 * i, 64), :] = low
            if keep:
                act_two[rows, at] = low
                slope_two[rows, at] = slope_of(square, gate, value).astype(BF)
        partial[:, at] = dot(third, act_all[...])
        for k in range(4):
            pltpu.make_async_copy(held[k].at[:, at], homes[k].at[:, at], semaphores.at[k, index]).start()
        return 0

    lax.fori_loop(0, NY // TILE, step, 0)
    correction = (
        pltpu.roll(partial[0:8, :], 1, 1) + partial[8:16, :] + pltpu.roll(partial[16:24, :], NY - 1, 1)
    )
    extended = [
        jnp.concatenate([low_before[2 * c + 1 : 2 * c + 2], velocity[c], low_after[2 * c : 2 * c + 1]], axis=0)
        for c in range(CH)
    ]
    across = velocity[1]
    pieces = []
    for c in range(CH):
        flux = extended[0] * extended[c]
        side = across * velocity[c]
        pieces.append(
            (flux[2:] - flux[:-2]) + (pltpu.roll(side, NY - 1, 1) - pltpu.roll(side, 1, 1))
        )
    advect = 0.5 * jnp.concatenate(pieces, axis=0)
    provisional = own + STEP_SIZE * (correction - advect)
    sent[:, 0] = column_forward(provisional, forward_a, forward_b, forward_b0, twist).reshape(D, 2, 128)
    whole.wait()
    for k in range(4):
        for index in range(NY // TILE):
            at = pl.ds(index * TILE, TILE)
            pltpu.make_async_copy(held[k].at[:, at], homes[k].at[:, at], semaphores.at[k, index]).wait()


def middle_kernel(
    device, got, row_forward, spin, short_forward, short_inverse, short_rim, spin_rim, row_inverse, sent
):
    same, cross = multiplier(device[0])
    v = pair_low(dot, row_forward, side_by_side([got[:, k].reshape(256, 128) for k in range(2)]))
    cosine, sine = spin[0], spin[1]
    fields = []
    for k in range(2):
        real, imag = v[:128, 128 * k : 128 * k + 128], v[128:, 128 * k : 128 * k + 128]
        fields.append(side_by_side([real * cosine + imag * sine, imag * cosine - real * sine]))
    high, low = halves(jnp.concatenate(fields, axis=0))
    full = dot(high, short_forward[...]) + dot(low, short_forward[...])
    fields = []
    for k in range(2):
        part = full[128 * k : 128 * k + 128]
        real, imag = part[:, :128], part[:, 128:]
        real = same * real + cross * pltpu.roll(real, 64, 1)
        imag = same * imag + cross * pltpu.roll(imag, 64, 1)
        fields.append(side_by_side([real, imag]))
    high, low = halves(jnp.concatenate(fields, axis=0))
    full = dot(high, short_inverse[...]) + dot(low, short_inverse[...])
    rim = dot(high[128:], short_rim[...]) + dot(low[128:], short_rim[...])
    parts = []
    for part, (cosine, sine) in (
        (full[:128], (cosine, sine)),
        (full[128:], (cosine, sine)),
        (rim, (spin_rim[0], spin_rim[1])),
    ):
        real, imag = part[:, :128], part[:, 128:]
        parts.append(jnp.concatenate([real * cosine - imag * sine, imag * cosine + real * sine], axis=0))
    out = exact(dot, row_inverse, side_by_side(parts)).astype(BF)
    for k in range(3):
        sent[:, k] = out[:, 128 * k : 128 * k + 128].reshape(D, 2, 128)


def backward_kernel(
    got,
    inverse_b,
    inverse_b0,
    untwist,
    untwist_rim,
    inverse_a,
    inverse_rim,
    w_mid,
    w_out,
    duals,
    place_mid,
    place_in,
    place_out,
    stack,
    act_one_home,
    act_two_home,
    slope_one_home,
    slope_two_home,
    sent,
    act_one,
    act_two,
    slope_one,
    slope_two,
    dual_stack,
    sum_mid,
    sum_in,
    sum_out,
    semaphores,
):
    held = (act_one, act_two, slope_one, slope_two)
    homes = (act_one_home, act_two_home, slope_one_home, slope_two_home)
    for index in range(NY // TILE):
        for k in range(4):
            at = pl.ds(index * TILE, TILE)
            pltpu.make_async_copy(homes[k].at[:, at], held[k].at[:, at], semaphores.at[k, index]).start()
    real, imag = column_inverse_first(got[:, 1].reshape(256, 128), inverse_b, inverse_b0, untwist, 64, R)
    own = exact(dot_nt, inverse_a, side_by_side([real, imag]))
    rim = got[:, 2].reshape(256, 128)
    real, imag = column_inverse_first(rim[:, :64], inverse_b, inverse_b0, untwist_rim, 32, 2)
    rim = exact(dot_nt, inverse_rim, side_by_side([real, imag]))
    base = jnp.concatenate([from_blocks(own), from_blocks(rim)], axis=0)
    dual_stack[0:16, :] = pltpu.roll(base, NY - 1, 1).astype(BF)
    dual_stack[16:32, :] = base.astype(BF)
    dual_stack[32:48, :] = pltpu.roll(base, 1, 1).astype(BF)
    spread_out = jnp.concatenate([dot_tn(w_out[...], duals[i]).astype(BF) for i in range(R)], axis=0)
    middle = w_mid[...]
    stack = stack.ready()
    sum_mid[...] = jnp.zeros_like(sum_mid)
    sum_in[...] = jnp.zeros_like(sum_in)
    sum_out[...] = jnp.zeros_like(sum_out)

    def step(index, _):
        at = pl.ds(pl.multiple_of(index * TILE, TILE), TILE)
        for k in range(4):
            pltpu.make_async_copy(homes[k].at[:, at], held[k].at[:, at], semaphores.at[k, index]).wait()
        dual = dual_stack[:, at]
        back_two = dot(spread_out, dual)
        delta_two = (back_two * slope_two[:, at].astype(F32)).astype(BF)
        hidden = act_one[:, at]
        wide = lambda t: jnp.concatenate([t[64 * i : 64 * i + 64] for i in range(R)], axis=1)
        wide_two = wide(delta_two)
        sum_mid[...] += dot_nt(wide_two, wide(hidden))
        back_one = dot_tn(middle, wide_two)
        tall = jnp.concatenate([back_one[:, TILE * i : TILE * i + TILE] for i in range(R)], axis=0)
        delta_one = (tall * slope_one[:, at].astype(F32)).astype(BF)
        sum_in[...] += dot_nt(delta_one, stack[:, at])
        sum_out[...] += dot_nt(act_two[:, at], dual)
        return 0

    lax.fori_loop(0, NY // TILE, step, 0)
    high, low = halves(sum_mid[...])
    total = dot(high, place_mid[...]) + dot(low, place_mid[...])
    for source, place in ((sum_in, place_in), (sum_out, place_out)):
        for i in range(R):
            high, low = halves(source[64 * i : 64 * i + 64, :])
            total = total + (dot(high, place[i]) + dot(low, place[i]))
    low = total.astype(BF)
    for k in range(8):
        sent[k] = low


def partial_sum_kernel(got, sent):
    total = got[0].astype(F32)
    for k in range(1, 8):
        total = total + got[k].astype(F32)
    low = total.astype(BF)
    for k in range(16):
        sent[k] = low


def total_kernel(got, grad_mid, grad_in, grad_out):
    total = got[0].astype(F32)
    for k in range(1, 16):
        total = total + got[k].astype(F32)
    grad_mid[...] = total[:, :64]
    grad_in[...] = total[:, 64:82]
    flipped = total.T[82:100]
    for t in range(9):
        grad_out[t // 3, t % 3] = flipped[2 * t : 2 * t + 2]


def field_kernel(got, inverse_b, inverse_b0, untwist, inverse_a, field):
    real, imag = column_inverse_first(got[:, 0].reshape(256, 128), inverse_b, inverse_b0, untwist, 64, R)
    x = from_blocks(exact(dot_nt, inverse_a, side_by_side([real, imag])))
    field[0] = x[:R]
    field[1] = x[R:]


class Staged:
    def __init__(self, copy, ref):
        self.copy, self.ref, self.waited = copy, ref, False

    def ready(self):
        if not self.waited:
            self.copy.wait()
            self.waited = True
        return self.ref

    def __getitem__(self, index):
        return self.ready()[index]


def call(kernel, outputs, inputs, scratch=(), scalars=0, staged=0, far=0, far_out=0):
    count = len(inputs)
    outputs = outputs if isinstance(outputs, list) else [outputs]
    spec = lambda space: pl.BlockSpec(memory_space=space)
    specs = [spec(pltpu.SMEM)] * scalars
    specs += [spec(pltpu.VMEM)] * (count - scalars - staged - far)
    specs += [spec(pltpu.HBM)] * (staged + far)
    out_specs = [spec(pltpu.VMEM)] * (len(outputs) - far_out) + [spec(pltpu.HBM)] * far_out
    first = count - staged - far

    def run(*refs):
        given = list(refs[:count])
        rest = refs[count + len(outputs) :]
        if staged:
            for k in range(staged):
                target = rest[len(scratch) + k]
                copy = pltpu.make_async_copy(given[first + k], target, rest[-1].at[k])
                copy.start()
                given[first + k] = Staged(copy, target)
        kernel(*given, *refs[count : count + len(outputs)], *rest[: len(scratch)])
        for k in range(staged):
            given[first + k].ready()

    held = [pltpu.VMEM(x.shape, x.dtype) for x in inputs[first : first + staged]]
    pinned = [pltpu.with_memory_space_constraint(jnp.asarray(x), pltpu.HBM) for x in inputs[first:]]
    inputs = [*inputs[:first], *pinned]
    far_first = len(outputs) - far_out
    outputs = outputs[:far_first] + [pltpu.HBM(x.shape, x.dtype) for x in outputs[far_first:]]
    if staged:
        held.append(pltpu.SemaphoreType.DMA((staged,)))
    result = pl.pallas_call(
        run,
        out_shape=outputs,
        in_specs=specs,
        out_specs=out_specs,
        scratch_shapes=list(scratch) + held,
        compiler_params=pltpu.CompilerParams(vmem_limit_bytes=VMEM_LIMIT),
    )(*inputs)
    return result if len(outputs) > 1 else result[0]


def exchange(x, groups=None):
    return lax.all_to_all(x, "rows", split_axis=0, concat_axis=0, tiled=True, axis_index_groups=groups)


def body(velocity, cotangent, w_in, w_mid, w_out):
    columns = column_tables()
    rows = row_tables()
    net = network_tables()
    scale = STEP_SIZE / math.sqrt(NX * NY)
    shape = jax.ShapeDtypeStruct
    flat_in = w_in.reshape(HID, 18)
    flat_out = w_out.reshape(18, HID)
    device = lax.axis_index("rows").reshape(1)
    size = D
    up = [(i, (i + 1) % size) for i in range(size)]
    down = [(j, i) for i, j in up]
    low = velocity.astype(BF)
    before = lax.ppermute(low[:, R - 2 :].reshape(4, NY), "rows", up)
    after = lax.ppermute(low[:, :2].reshape(4, NY), "rows", down)

    forward = [columns[k] for k in ("forward_a", "forward_b", "forward_b0", "twist")]
    dual_sent = call(dual_kernel, shape((D, 2, 128), BF), [cotangent, *forward], staged=5)

    big = shape((R * HID, NY), BF)
    own_tiles = [pltpu.VMEM((R * HID, NY), BF)] * 4
    first_sent, act_one, act_two, slope_one, slope_two, stack = call(
        network_kernel,
        [shape((D, 2, 2, 128), BF), big, big, big, big, shape((48, NY), BF)],
        [dual_sent, before, after, velocity, flat_in, w_mid, flat_out, net["taps"], net["outs"], *forward],
        own_tiles
        + [
            pltpu.VMEM((48, NY), BF),
            pltpu.VMEM((6 * HID, TILE), BF),
            pltpu.VMEM((24, NY), F32),
            pltpu.SemaphoreType.DMA((5, NY // TILE)),
        ],
        staged=10,
        far_out=5,
    )
    first_got = exchange(first_sent)
    second_sent = call(
        middle_kernel,
        shape((D, 3, 2, 128), BF),
        [
            device,
            first_got,
            *[rows[k] for k in ("row_forward", "spin", "short_forward", "short_inverse", "short_rim", "spin_rim")],
            rows["row_inverse"],
        ],
        scalars=1,
        staged=7,
    )
    second_got = exchange(second_sent)
    back = [columns[k] for k in ("inverse_b", "inverse_b0", "untwist")]
    partial = call(
        backward_kernel,
        shape((8, 64, 128), BF),
        [
            second_got,
            *back,
            columns["untwist_rim"],
            table_pair(columns["inverse_a"] * scale),
            table_pair(columns["inverse_rim"] * scale),
            w_mid,
            flat_out,
            *[net[k] for k in ("duals", "place_mid", "place_in", "place_out")],
            stack,
            act_one,
            act_two,
            slope_one,
            slope_two,
        ],
        own_tiles
        + [
            pltpu.VMEM((48, NY), BF),
            pltpu.VMEM((HID, HID), F32),
            pltpu.VMEM((R * HID, 48), F32),
            pltpu.VMEM((R * HID, 48), F32),
            pltpu.SemaphoreType.DMA((4, NY // TILE)),
        ],
        staged=13,
        far=4,
    )
    along_z = [[16 * z + r for z in range(8)] for r in range(16)]
    across_z = [[16 * z + r for r in range(16)] for z in range(8)]
    partial = call(partial_sum_kernel, shape((16, 64, 128), BF), [exchange(partial, along_z)])
    new_velocity = call(
        field_kernel,
        shape((CH, R, NY), F32),
        [second_got, *back, table_pair(columns["inverse_a"])],
        staged=4,
    )
    grad_mid, grad_in, grad_out = call(
        total_kernel,
        [shape((HID, HID), F32), shape((HID, 18), F32), shape((3, 3, 2, HID), F32)],
        [exchange(partial, across_z)],
    )
    return new_velocity, grad_in.reshape(HID, 3, 3, 2), grad_mid, grad_out


def solution(mesh):
    in_specs = (P("batch", "rows", None), P("batch", "rows", None), P(), P(), P())
    out_specs = (
        P("batch", "rows", None),
        P("batch", None, None, None),
        P("batch", None),
        P("batch", None, None, None),
    )
    return jax.shard_map(body, mesh=mesh, in_specs=in_specs, out_specs=out_specs, check_vma=False)
```

```python
import functools
import math

import jax
import jax.numpy as jnp
import ml_dtypes
import numpy as np
from jax import lax
from jax.experimental import pallas as pl
from jax.experimental.pallas import tpu as pltpu
from jax.sharding import PartitionSpec as P

STEP_SIZE = 0.5
GELU_SCALE = 0.7978845608028654
GELU_CUBIC = 0.044715
BF = jnp.bfloat16
F32 = jnp.float32
TILE = 1024
BACK_TILE = 2048
VMEM_LIMIT = 24 * 1024 * 1024

R = 4
D = 128
NX = R * D
OUTER = 32
NY = OUTER * 128
C = OUTER // 2
CH = 2
HID = 64
OWN = R * HID
STEP_ROWS = (-2, -1, 0, 1)


def table_pair(matrix):
    high = np.asarray(matrix, np.float64).astype(ml_dtypes.bfloat16)
    low = (matrix - high.astype(np.float64)).astype(ml_dtypes.bfloat16)
    return np.stack([high, low])


def column_tables():
    a = np.arange(OUTER)
    b = np.arange(128)
    d = np.arange(D)
    c = np.arange(C)
    eye = np.eye(R * CH).reshape(CH, R, CH, R)
    sign = np.where(a % 2 == 0, 1.0, -1.0)
    angle = 2 * np.pi * np.outer(c, a) / OUTER
    first = np.stack([np.cos(angle), -np.sin(angle)])
    first[0, 0] = 1.0
    first[1, 0] = sign
    forward_a = np.einsum("pca,hrgs->phcrags", first, eye).reshape(256, 256)
    last = np.stack([2 * np.cos(angle), -2 * np.sin(angle)])
    last[0, 0] = 1.0
    last[1, 0] = sign
    last = last / NY
    inverse_a = np.einsum("pca,gshr->agsphcr", last, eye).reshape(256, 256)
    half = np.zeros((2, 4, CH, 2))
    for h in range(CH):
        for e in range(2):
            half[h, h * 2 + e, h, e] = 1.0
    rim = np.zeros((8, CH, 2))
    rim[:4] = np.eye(4).reshape(4, CH, 2)
    inverse_rim = np.einsum("pca,khr->akphcr", last, rim).reshape(256, 128)
    theta = 2 * np.pi * np.outer(c, b) / NY
    cosine = np.cos(theta)
    sine = np.sin(theta)
    cosine[0] = 1.0
    sine[0] = 0.0
    spread = lambda t, n: np.broadcast_to(t[None, :, None, :], (CH, C, n, 128)).reshape(-1, 128)
    twist = np.stack([spread(cosine, R), spread(sine, R)]).astype(np.float32)
    twist_rim = np.stack([spread(cosine, 2), spread(sine, 2)]).astype(np.float32)
    phi = 2 * np.pi * np.outer(d, b) / 128
    matrix = np.zeros((D, 2, 2, 128))
    matrix[:, 0, 0] = np.cos(phi)
    matrix[:, 0, 1] = np.sin(phi)
    matrix[:, 1, 0] = -np.sin(phi)
    matrix[:, 1, 1] = np.cos(phi)
    psi = 2 * np.pi * np.outer(16 + 32 * (d - 64), b) / NY
    alternate = np.where(b % 2 == 0, 1.0, -1.0)
    zero = np.zeros((D, 2, 2, 128))
    zero[:64, 0, 0] = np.cos(phi[:64])
    zero[:64, 1, 0] = -np.sin(phi[:64])
    zero[0, 1, 0] = alternate
    zero[64:, 0, 1] = np.cos(psi[64:])
    zero[64:, 1, 1] = -np.sin(psi[64:])
    back = np.zeros((2, 128, D, 2))
    back[0, :, :, 0] = np.cos(phi).T
    back[0, :, :, 1] = -np.sin(phi).T
    back[1, :, :, 0] = np.sin(phi).T
    back[1, :, :, 1] = np.cos(phi).T
    back_zero = np.zeros((2, 128, D, 2))
    back_zero[0, :, :64, 0] = 2 * np.cos(phi[:64]).T
    back_zero[0, :, :64, 1] = -2 * np.sin(phi[:64]).T
    back_zero[0, :, 0, 0] = 1.0
    back_zero[0, :, 0, 1] = alternate
    back_zero[1, :, 64:, 0] = 2 * np.cos(psi[64:]).T
    back_zero[1, :, 64:, 1] = -2 * np.sin(psi[64:]).T
    return {
        "forward_a": table_pair(forward_a),
        "forward_b": table_pair(matrix.reshape(256, 256)),
        "forward_b0": table_pair(zero.reshape(256, 256))[0],
        "twist": twist,
        "inverse_b": table_pair(back.reshape(256, 256)),
        "inverse_b0": table_pair(back_zero.reshape(256, 256))[0],
        "inverse_a": inverse_a,
        "inverse_rim": inverse_rim,
        "untwist": np.ascontiguousarray(twist.transpose(0, 2, 1)),
        "untwist_rim": np.ascontiguousarray(twist_rim.transpose(0, 2, 1)),
    }


def row_tables():
    s = np.arange(D)
    m1 = np.arange(D)
    m2 = np.arange(R)
    phi = 2 * np.pi * np.outer(m1, s) / D
    forward = np.zeros((2, D, D, 2))
    forward[0, :, :, 0] = np.cos(phi)
    forward[0, :, :, 1] = np.sin(phi)
    forward[1, :, :, 0] = -np.sin(phi)
    forward[1, :, :, 1] = np.cos(phi)
    inverse = np.zeros((D, 2, 2, D))
    inverse[:, 0, 0] = np.cos(phi).T
    inverse[:, 0, 1] = -np.sin(phi).T
    inverse[:, 1, 0] = np.sin(phi).T
    inverse[:, 1, 1] = np.cos(phi).T
    inverse = inverse / NX
    eye = np.eye(CH * C)

    def short(rows, flip):
        angle = 2 * np.pi * np.outer(m2, rows) / R
        block = np.zeros((2, R, 2, len(rows)))
        block[0, :, 0] = np.cos(angle)
        block[1, :, 0] = -np.sin(angle) * flip
        block[0, :, 1] = np.sin(angle) * flip
        block[1, :, 1] = np.cos(angle)
        block = np.round(block)
        return np.einsum("pmqr,gk->pgmqkr", block, eye).reshape(2 * CH * C * R, 2, -1)

    own = np.arange(R)
    rim = np.array([-1, R])
    rim_block = np.zeros((256, 2, 128))
    rim_block[:, :, :64] = short(rim, 1.0)

    def lanes(rows):
        theta = 2 * np.pi * np.outer(m1, rows) / NX
        both = np.stack([np.cos(theta), np.sin(theta)])
        wide = np.broadcast_to(both[:, :, None, :], (2, D, CH * C, len(rows))).reshape(2, D, -1)
        out = np.zeros((2, D, 128), np.float32)
        out[:, :, : wide.shape[2]] = wide
        return out

    return {
        "row_forward": table_pair(forward.reshape(256, 256)),
        "row_inverse": table_pair(inverse.reshape(256, 256)),
        "short_forward": short(own, -1.0).reshape(256, 256).astype(ml_dtypes.bfloat16),
        "short_inverse": short(own, 1.0).reshape(256, 256).astype(ml_dtypes.bfloat16),
        "short_rim": rim_block.reshape(256, 256).astype(ml_dtypes.bfloat16),
        "spin": lanes(own),
        "spin_step": lanes(np.array(STEP_ROWS)),
        "spin_rim": lanes(rim - 2),
    }


def velocity_row(ch, row):
    return ch * R + row if row >= 0 else 8 + ch * R + row + R


def dual_row(ch, row):
    if row in STEP_ROWS:
        return ch * R + row + 2
    return 8 + ch * 2 + (0 if row < -2 else 1)


def network_tables():
    order = (*STEP_ROWS, -3, 2)
    taps = np.zeros((6, 18, 48))
    for at, i in enumerate(order):
        for a in range(-1, 2):
            for b in range(-1, 2):
                for ch in range(CH):
                    t = (3 * (a + 1) + b + 1) * 2 + ch
                    taps[at, t, (b + 1) * 16 + velocity_row(ch, i + a)] = 1
    outs = np.zeros((6, 24, 18))
    for at, k in enumerate(order):
        for a in range(-1, 2):
            i = k - a
            if i in STEP_ROWS:
                for b in range(-1, 2):
                    for o in range(CH):
                        outs[at, (b + 1) * 8 + o * R + i + 2, (3 * (a + 1) + b + 1) * 2 + o] = 1
    duals = np.zeros((R, 18, 48))
    for at, i in enumerate(STEP_ROWS):
        for a in range(-1, 2):
            for b in range(-1, 2):
                for o in range(CH):
                    t = (3 * (a + 1) + b + 1) * 2 + o
                    duals[at, t, (b + 1) * 16 + dual_row(o, i - a)] = 1
    low = lambda t: t.astype(ml_dtypes.bfloat16)
    return {
        "taps": low(taps),
        "outs": low(outs),
        "duals": low(duals),
    }


def dot(x, y):
    return jnp.dot(x, y, preferred_element_type=F32)


def dot_nt(x, y):
    return lax.dot_general(x, y, (((1,), (1,)), ((), ())), preferred_element_type=F32)


def dot_tn(x, y):
    return lax.dot_general(x, y, (((0,), (0,)), ((), ())), preferred_element_type=F32)


def halves(x):
    high = x.astype(BF)
    return high, (x - high.astype(F32)).astype(BF)


def exact(form, pair, x):
    high, low = halves(x)
    return form(pair[0], high) + (form(pair[1], high) + form(pair[0], low))


def pair_low(form, pair, x):
    return form(pair[0], x) + form(pair[1], x)


def to_blocks(x):
    return jnp.concatenate([x[:, 128 * a : 128 * a + 128] for a in range(OUTER)], axis=0)


def from_blocks(x):
    rows = x.shape[0] // OUTER
    return jnp.concatenate([x[rows * a : rows * a + rows] for a in range(OUTER)], axis=1)


def column_forward(x, forward_a, forward_b, forward_b0, twist):
    y = exact(dot, forward_a, to_blocks(x))
    real, imag = y[:128], y[128:]
    cosine, sine = twist[0], twist[1]
    both = jnp.concatenate([real * cosine + imag * sine, imag * cosine - real * sine], axis=1)
    general = exact(dot_nt, forward_b, both)
    zero = dot_nt(forward_b0[...], both.astype(BF))
    lane = lax.broadcasted_iota(jnp.int32, general.shape, 1)
    return jnp.where(lane % 64 < R, zero, general).astype(BF)


def column_inverse_first(x, inverse_b, inverse_b0, untwist, period, width):
    general = pair_low(dot, inverse_b, x)
    zero = dot(inverse_b0[...], x)
    lane = lax.broadcasted_iota(jnp.int32, general.shape, 1)
    y = jnp.where(lane % period < width, zero, general)
    real, imag = y[:128], y[128:]
    cosine, sine = untwist[0], untwist[1]
    return real * cosine - imag * sine, imag * cosine + real * sine


def multiplier(device):
    m1 = lax.broadcasted_iota(jnp.int32, (128, 128), 0)
    lane = lax.broadcasted_iota(jnp.int32, (128, 128), 1)
    m = m1 + 128 * (lane % R)
    m = jnp.where(2 * m < NX, m, jnp.where(2 * m == NX, 0, m - NX))
    c = (lane % 64) // R
    n = c + OUTER * device
    n = jnp.where(2 * n < NY, n, n - NY)
    packed = jnp.where(device < 64, OUTER * device, 16 + OUTER * (device - 64))
    n = jnp.where(c == 0, packed, n)
    wave_row = m.astype(F32) * (1.0 / NX)
    wave_col = n.astype(F32) * (1.0 / NY)
    row_square = wave_row * wave_row
    col_square = wave_col * wave_col
    square = row_square + col_square
    some = square > 0
    inverse = 1.0 / jnp.where(some, square, 1.0)
    same = jnp.where(some, jnp.where(lane < 64, col_square, row_square) * inverse, 1.0)
    sign = jnp.where(lane % 2 == 0, 1.0, -1.0)
    return sign * same, -sign * (wave_row * wave_col) * inverse


def side_by_side(parts):
    return jnp.concatenate(parts, axis=1)


def staggered(count, *stages):
    values = {}
    for step in range(count + len(stages) - 1):
        for lag in reversed(range(len(stages))):
            index = step - lag
            if 0 <= index < count:
                values[index] = stages[lag](index, values.get(index))


def flat_taps(weights):
    rows = [weights[t // 3, t % 3].astype(F32) for t in range(9)]
    return jnp.concatenate(rows, axis=0).astype(BF)


def diagonal(block, count):
    empty = jnp.zeros_like(block)
    rows = [side_by_side([block if i == k else empty for k in range(count)]) for i in range(count)]
    return jnp.concatenate(rows, axis=0)


def gelu_parts(pre):
    square = pre * pre
    tangent = jnp.tanh(pre * (GELU_SCALE + (GELU_SCALE * GELU_CUBIC) * square))
    gate = 0.5 + 0.5 * tangent
    return square, gate, pre * gate


def slope_of(square, gate, value):
    return gate + value * (1.0 - gate) * (2 * GELU_SCALE + (6 * GELU_SCALE * GELU_CUBIC) * square)


def dual_kernel(field, forward_a, forward_b, forward_b0, twist, *refs):
    sent = refs[-1]
    x = jnp.concatenate([field[0], field[1]], axis=0)
    sent[...] = column_forward(x, forward_a, forward_b, forward_b0, twist).reshape(D, 2, 128)


def network_kernel(
    dual_sent,
    above,
    forward_a,
    forward_b,
    forward_b0,
    twist,
    velocity,
    w_in,
    w_mid,
    w_out,
    taps,
    outs,
    sent,
    act_one_out,
    act_two_out,
    slope_one_out,
    slope_two_out,
    stack_out,
    act_one,
    act_two,
    slope_one,
    slope_two,
    stack,
    partial,
    semaphores,
):
    sent[:, 1] = dual_sent[...]
    held = (act_one, act_two, slope_one, slope_two)
    homes = (act_one_out, act_two_out, slope_one_out, slope_two_out)
    whole = pltpu.make_async_copy(stack, stack_out, semaphores.at[4, 0])
    low_above = [above[c].astype(F32) for c in range(CH)]
    base = jnp.concatenate([velocity[0], velocity[1], *low_above], axis=0)
    stack[0:16, :] = pltpu.roll(base, 1, 1).astype(BF)
    stack[16:32, :] = base.astype(BF)
    stack[32:48, :] = pltpu.roll(base, NY - 1, 1).astype(BF)
    whole.start()
    flat_in, flat_out = flat_taps(w_in), flat_taps(w_out)
    first = jnp.concatenate([dot_tn(flat_in, taps[i]).astype(BF) for i in range(6)], axis=0)
    third = side_by_side([dot(outs[i], flat_out).astype(BF) for i in range(6)])
    middle = diagonal(w_mid[...], R)

    def columns(index):
        return slice(index * TILE, index * TILE + TILE)

    def layer_one(index, _):
        return dot(first, stack[:, columns(index)])

    def gelu_one(index, pre):
        at = columns(index)
        square, gate, value = gelu_parts(pre[:OWN])
        low = value.astype(BF)
        act_one[:, at] = low
        slope_one[:, at] = slope_of(square, gate, value).astype(BF)
        return low, gelu_parts(pre[OWN:])[2].astype(BF)

    def layer_two(index, low):
        return dot(middle, low[0]), dot(middle[:128, :128], low[1])

    def gelu_two(index, pre):
        at = columns(index)
        square, gate, value = gelu_parts(pre[0])
        low = value.astype(BF)
        act_two[:, at] = low
        slope_two[:, at] = slope_of(square, gate, value).astype(BF)
        for k in range(4):
            pltpu.make_async_copy(held[k].at[:, at], homes[k].at[:, at], semaphores.at[k, index]).start()
        return jnp.concatenate([low, gelu_parts(pre[1])[2].astype(BF)], axis=0)

    def layer_three(index, low):
        partial[:, columns(index)] = dot(third, low)

    staggered(NY // TILE, layer_one, gelu_one, layer_two, gelu_two, layer_three)
    correction = (
        pltpu.roll(partial[0:8, :], 1, 1) + partial[8:16, :] + pltpu.roll(partial[16:24, :], NY - 1, 1)
    )
    near = [jnp.concatenate([low_above[c][1:], velocity[c][:3]], axis=0) for c in range(CH)]
    rows = [field[1:5] for field in near]
    pieces = []
    for c in range(CH):
        flux = near[0] * near[c]
        side = rows[1] * rows[c]
        pieces.append(
            (flux[2:] - flux[:-2]) + (pltpu.roll(side, NY - 1, 1) - pltpu.roll(side, 1, 1))
        )
    advect = 0.5 * jnp.concatenate(pieces, axis=0)
    provisional = jnp.concatenate(rows, axis=0) + STEP_SIZE * (correction - advect)
    sent[:, 0] = column_forward(provisional, forward_a, forward_b, forward_b0, twist).reshape(D, 2, 128)
    whole.wait()
    for k in range(4):
        for index in range(NY // TILE):
            at = pl.ds(index * TILE, TILE)
            pltpu.make_async_copy(held[k].at[:, at], homes[k].at[:, at], semaphores.at[k, index]).wait()


def middle_kernel(
    device, got, row_forward, spin, spin_step, short_forward, short_inverse, short_rim, spin_rim, row_inverse, sent
):
    same, cross = multiplier(device[0])
    v = pair_low(dot, row_forward, side_by_side([got[:, k].reshape(256, 128) for k in range(2)]))
    plain = (spin[0], spin[1])
    step = (spin_step[0], spin_step[1])
    fields = []
    for k, (cosine, sine) in enumerate((step, plain)):
        real, imag = v[:128, 128 * k : 128 * k + 128], v[128:, 128 * k : 128 * k + 128]
        fields.append(side_by_side([real * cosine + imag * sine, imag * cosine - real * sine]))
    high, low = halves(jnp.concatenate(fields, axis=0))
    full = dot(high, short_forward[...]) + dot(low, short_forward[...])
    fields = []
    for k in range(2):
        part = full[128 * k : 128 * k + 128]
        real, imag = part[:, :128], part[:, 128:]
        real = same * real + cross * pltpu.roll(real, 64, 1)
        imag = same * imag + cross * pltpu.roll(imag, 64, 1)
        fields.append(side_by_side([real, imag]))
    high, low = halves(jnp.concatenate(fields, axis=0))
    full = dot(high, short_inverse[...]) + dot(low, short_inverse[...])
    rim = dot(high[128:], short_rim[...]) + dot(low[128:], short_rim[...])
    parts = []
    for part, (cosine, sine) in (
        (full[:128], plain),
        (full[128:], step),
        (rim, (spin_rim[0], spin_rim[1])),
    ):
        real, imag = part[:, :128], part[:, 128:]
        parts.append(jnp.concatenate([real * cosine - imag * sine, imag * cosine + real * sine], axis=0))
    out = exact(dot, row_inverse, side_by_side(parts)).astype(BF)
    for k in range(3):
        sent[:, k] = out[:, 128 * k : 128 * k + 128].reshape(D, 2, 128)


def backward_kernel(
    got,
    inverse_b,
    inverse_b0,
    untwist,
    untwist_rim,
    inverse_a,
    inverse_rim,
    w_mid,
    w_out,
    duals,
    taps,
    stack,
    act_one_home,
    act_two_home,
    slope_one_home,
    slope_two_home,
    sent,
    act_one,
    act_two,
    slope_one,
    slope_two,
    dual_stack,
    sum_mid,
    sum_in,
    sum_out,
    semaphores,
):
    held = (slope_two, act_one, act_two, slope_one)
    homes = (slope_two_home, act_one_home, act_two_home, slope_one_home)
    count = NY // BACK_TILE
    for index in range(count):
        for k in range(4):
            at = pl.ds(index * BACK_TILE, BACK_TILE)
            pltpu.make_async_copy(homes[k].at[:, at], held[k].at[:, at], semaphores.at[k, index]).start()
    real, imag = column_inverse_first(got[:, 1].reshape(256, 128), inverse_b, inverse_b0, untwist, 64, R)
    own = exact(dot_nt, inverse_a, side_by_side([real, imag]))
    rim = got[:, 2].reshape(256, 128)
    real, imag = column_inverse_first(rim[:, :64], inverse_b, inverse_b0, untwist_rim, 32, 2)
    rim = exact(dot_nt, inverse_rim, side_by_side([real, imag]))
    base = jnp.concatenate([from_blocks(own), from_blocks(rim)], axis=0)
    dual_stack[0:16, :] = pltpu.roll(base, NY - 1, 1).astype(BF)
    dual_stack[16:32, :] = base.astype(BF)
    dual_stack[32:48, :] = pltpu.roll(base, 1, 1).astype(BF)
    flat_out = flat_taps(w_out)
    spread_out = jnp.concatenate([dot_tn(flat_out, duals[i]).astype(BF) for i in range(R)], axis=0)
    middle = diagonal(w_mid[...].T, R)
    sum_mid[...] = jnp.zeros_like(sum_mid)
    sum_in[...] = jnp.zeros_like(sum_in)
    sum_out[...] = jnp.zeros_like(sum_out)

    def step(index, _):
        at = pl.ds(pl.multiple_of(index * BACK_TILE, BACK_TILE), BACK_TILE)
        for k in range(4):
            pltpu.make_async_copy(homes[k].at[:, at], held[k].at[:, at], semaphores.at[k, index]).wait()
        dual = dual_stack[:, at]
        back_two = dot(spread_out, dual)
        delta_two = (back_two * slope_two[:, at].astype(F32)).astype(BF)
        sum_mid[...] += dot_nt(delta_two, act_one[:, at])
        delta_one = (dot(middle, delta_two) * slope_one[:, at].astype(F32)).astype(BF)
        sum_in[...] += dot_nt(delta_one, stack[:, at])
        sum_out[...] += dot_nt(act_two[:, at], dual)
        return 0

    lax.fori_loop(0, count, step, 0, unroll=2)
    mid = sum(sum_mid[64 * i : 64 * i + 64, 64 * i : 64 * i + 64] for i in range(R))
    flips = []
    for source, choose in ((sum_in, taps), (sum_out, duals)):
        flip = jnp.zeros((18, HID), F32)
        for i in range(R):
            high, low = halves(source[64 * i : 64 * i + 64, :])
            flip = flip + (dot_nt(choose[i], high) + dot_nt(choose[i], low))
        flips.append(flip)
    packed = jnp.concatenate([side_by_side([mid[:32], mid[32:]]), side_by_side(flips)], axis=0)
    low = packed.astype(BF).reshape(25, 2, 128)
    for k in range(8):
        sent[k] = low


def added(got, count):
    total = got[0].astype(F32)
    for k in range(1, count):
        total = total + got[k].astype(F32)
    return total


def partial_sum_kernel(got, sent):
    low = added(got, 8).astype(BF)
    for k in range(16):
        sent[k] = low


def total_kernel(got, grad_mid, grad_in, grad_out):
    total = added(got, 16).reshape(50, 128)
    grad_mid[:32] = total[:32, :64]
    grad_mid[32:] = total[:32, 64:]
    for t in range(9):
        grad_out[t // 3, t % 3] = total[32 + 2 * t : 34 + 2 * t, 64:]
    grad_in[...] = total[32:, :64].T


def field_kernel(got, inverse_b, inverse_b0, untwist, inverse_a, field):
    real, imag = column_inverse_first(got[:, 0].reshape(256, 128), inverse_b, inverse_b0, untwist, 64, R)
    x = from_blocks(exact(dot_nt, inverse_a, side_by_side([real, imag])))
    field[0] = x[:R]
    field[1] = x[R:]


class Staged:
    def __init__(self, copy, ref):
        self.copy, self.ref, self.waited = copy, ref, False

    def ready(self):
        if not self.waited:
            self.copy.wait()
            self.waited = True
        return self.ref

    def __getitem__(self, index):
        return self.ready()[index]


def call(kernel, outputs, inputs, scratch=(), scalars=0, staged=0, kept=0, far=0, far_out=0):
    count = len(inputs)
    outputs = outputs if isinstance(outputs, list) else [outputs]
    spec = lambda space: pl.BlockSpec(memory_space=space)
    specs = [spec(pltpu.SMEM)] * scalars
    specs += [spec(pltpu.VMEM)] * (count - scalars - staged - far)
    specs += [spec(pltpu.HBM)] * (staged + far)
    out_specs = [spec(pltpu.VMEM)] * (len(outputs) - far_out) + [spec(pltpu.HBM)] * far_out
    out_specs += [spec(pltpu.VMEM)] * kept
    first = count - staged - far
    dropped = staged - kept

    def run(*refs):
        given = list(refs[:count])
        own = len(outputs) - kept
        targets = refs[count + own : count + own + kept]
        rest = refs[count + own + kept :]
        if staged:
            for k in range(staged):
                target = rest[len(scratch) + k] if k < dropped else targets[k - dropped]
                copy = pltpu.make_async_copy(given[first + k], target, rest[-1].at[k])
                copy.start()
                given[first + k] = Staged(copy, target)
        kernel(*given, *refs[count : count + own], *rest[: len(scratch)])
        for k in range(staged):
            given[first + k].ready()

    held = [pltpu.VMEM(x.shape, x.dtype) for x in inputs[first : first + dropped]]
    kept_out = [pltpu.VMEM(x.shape, x.dtype) for x in inputs[first + dropped : first + staged]]
    pinned = [pltpu.with_memory_space_constraint(jnp.asarray(x), pltpu.HBM) for x in inputs[first:]]
    inputs = [*inputs[:first], *pinned]
    far_first = len(outputs) - far_out
    outputs = outputs[:far_first] + [pltpu.HBM(x.shape, x.dtype) for x in outputs[far_first:]]
    outputs += kept_out
    if staged:
        held.append(pltpu.SemaphoreType.DMA((staged,)))
    result = pl.pallas_call(
        run,
        out_shape=outputs,
        in_specs=specs,
        out_specs=out_specs,
        scratch_shapes=list(scratch) + held,
        compiler_params=pltpu.CompilerParams(vmem_limit_bytes=VMEM_LIMIT),
    )(*inputs)
    return result if len(outputs) > 1 else result[0]


def prefetch(arrays, after):
    count = len(arrays)

    def run(*refs):
        targets, semaphores = refs[count + 1 : 2 * count + 1], refs[-1]
        copies = [pltpu.make_async_copy(refs[k], targets[k], semaphores.at[k]) for k in range(count)]
        for copy in copies:
            copy.start()
        for copy in copies:
            copy.wait()

    arrays = [jnp.asarray(x) for x in arrays]
    return pl.pallas_call(
        run,
        out_shape=[pltpu.VMEM(x.shape, x.dtype) for x in arrays],
        in_specs=[pl.BlockSpec(memory_space=pltpu.HBM)] * count + [pl.BlockSpec(memory_space=pl.ANY)],
        out_specs=[pl.BlockSpec(memory_space=pltpu.VMEM)] * count,
        scratch_shapes=[pltpu.SemaphoreType.DMA((count,))],
        compiler_params=pltpu.CompilerParams(vmem_limit_bytes=VMEM_LIMIT),
    )(*[pltpu.with_memory_space_constraint(x, pltpu.HBM) for x in arrays], after)


def exchange(x, groups=None):
    return lax.all_to_all(x, "rows", split_axis=0, concat_axis=0, tiled=True, axis_index_groups=groups)


def body(velocity, cotangent, w_in, w_mid, w_out):
    columns = column_tables()
    rows = row_tables()
    net = network_tables()
    scale = STEP_SIZE / math.sqrt(NX * NY)
    shape = jax.ShapeDtypeStruct
    w_in = jnp.transpose(w_in, (1, 2, 3, 0))
    device = lax.axis_index("rows").reshape(1)
    down = [(i, (i + 1) % D) for i in range(D)]
    above = lax.ppermute(velocity.astype(BF), "rows", down)

    forward = [columns[k] for k in ("forward_a", "forward_b", "forward_b0", "twist")]
    ahead = [*forward, velocity, w_in, w_mid, w_out, net["taps"], net["outs"]]
    dual_sent, *ahead = call(
        dual_kernel, shape((D, 2, 128), BF), [cotangent, *ahead], staged=1 + len(ahead), kept=len(ahead)
    )

    big = shape((R * HID, NY), BF)
    own_tiles = [pltpu.VMEM((R * HID, NY), BF)] * 4
    first_sent, act_one, act_two, slope_one, slope_two, stack = call(
        network_kernel,
        [shape((D, 2, 2, 128), BF), big, big, big, big, shape((48, NY), BF)],
        [dual_sent, above, *ahead],
        own_tiles
        + [
            pltpu.VMEM((48, NY), BF),
            pltpu.VMEM((24, NY), F32),
            pltpu.SemaphoreType.DMA((5, NY // TILE)),
        ],
        far_out=5,
    )
    first_got = exchange(first_sent)
    names = ("row_forward", "spin", "spin_step", "short_forward", "short_inverse", "short_rim", "spin_rim")
    tables = prefetch([*[rows[k] for k in names], rows["row_inverse"]], first_sent)
    second_sent = call(
        middle_kernel, shape((D, 3, 2, 128), BF), [device, first_got, *tables], scalars=1
    )
    second_got = exchange(second_sent)
    back = [columns[k] for k in ("inverse_b", "inverse_b0", "untwist")]
    tables = prefetch(
        [
            *back,
            columns["untwist_rim"],
            table_pair(columns["inverse_a"] * scale),
            table_pair(columns["inverse_rim"] * scale),
            w_mid,
            w_out,
            net["duals"],
            net["taps"],
            stack,
        ],
        second_sent,
    )
    partial = call(
        backward_kernel,
        shape((8, 25, 2, 128), BF),
        [second_got, *tables, act_one, act_two, slope_one, slope_two],
        own_tiles
        + [
            pltpu.VMEM((48, NY), BF),
            pltpu.VMEM((OWN, OWN), F32),
            pltpu.VMEM((R * HID, 48), F32),
            pltpu.VMEM((R * HID, 48), F32),
            pltpu.SemaphoreType.DMA((4, NY // BACK_TILE)),
        ],
        far=4,
    )
    along_z = [[16 * z + r for z in range(8)] for r in range(16)]
    across_z = [[16 * z + r for r in range(16)] for z in range(8)]
    partial = call(partial_sum_kernel, shape((16, 25, 2, 128), BF), [exchange(partial, along_z)])
    new_velocity = call(
        field_kernel,
        shape((CH, R, NY), F32),
        [second_got, *back, table_pair(columns["inverse_a"])],
        staged=4,
    )
    grad_mid, grad_in, grad_out = call(
        total_kernel,
        [shape((HID, HID), F32), shape((HID, 18), F32), shape((3, 3, 2, HID), F32)],
        [exchange(partial, across_z)],
    )
    return new_velocity, grad_in.reshape(HID, 3, 3, 2), grad_mid, grad_out


def solution(mesh):
    in_specs = (P("batch", "rows", None), P("batch", "rows", None), P(), P(), P())
    out_specs = (
        P("batch", "rows", None),
        P("batch", None, None, None),
        P("batch", None),
        P("batch", None, None, None),
    )
    return jax.shard_map(body, mesh=mesh, in_specs=in_specs, out_specs=out_specs, check_vma=False)
```

```python
import functools
import math

import jax
import jax.numpy as jnp
import ml_dtypes
import numpy as np
from jax import lax
from jax.experimental import pallas as pl
from jax.experimental.pallas import tpu as pltpu
from jax.sharding import PartitionSpec as P

STEP_SIZE = 0.5
GELU_SCALE = 0.7978845608028654
GELU_CUBIC = 0.044715
BF = jnp.bfloat16
F32 = jnp.float32
TILE = 1024
BACK_TILE = 2048
VMEM_LIMIT = 32 * 1024 * 1024

R = 4
D = 128
NX = R * D
OUTER = 32
NY = OUTER * 128
C = OUTER // 2
CH = 2
HID = 64
OWN = R * HID
STEP_ROWS = (-2, -1, 0, 1)
LATE_ROWS = (-2, -1, 0, -3)
EARLY_ROWS = (1, 2)


def table_pair(matrix):
    high = np.asarray(matrix, np.float64).astype(ml_dtypes.bfloat16)
    low = (matrix - high.astype(np.float64)).astype(ml_dtypes.bfloat16)
    return np.stack([high, low])


def column_tables():
    a = np.arange(OUTER)
    b = np.arange(128)
    d = np.arange(D)
    c = np.arange(C)
    eye = np.eye(R * CH).reshape(CH, R, CH, R)
    sign = np.where(a % 2 == 0, 1.0, -1.0)
    angle = 2 * np.pi * np.outer(c, a) / OUTER
    first = np.stack([np.cos(angle), -np.sin(angle)])
    first[0, 0] = 1.0
    first[1, 0] = sign
    forward_a = np.einsum("pca,hrgs->phcrags", first, eye).reshape(256, 256)
    last = np.stack([2 * np.cos(angle), -2 * np.sin(angle)])
    last[0, 0] = 1.0
    last[1, 0] = sign
    last = last / NY
    inverse_a = np.einsum("pca,gshr->agsphcr", last, eye).reshape(256, 256)
    half = np.zeros((2, 4, CH, 2))
    for h in range(CH):
        for e in range(2):
            half[h, h * 2 + e, h, e] = 1.0
    rim = np.zeros((8, CH, 2))
    rim[:4] = np.eye(4).reshape(4, CH, 2)
    inverse_rim = np.einsum("pca,khr->akphcr", last, rim).reshape(256, 128)
    theta = 2 * np.pi * np.outer(c, b) / NY
    cosine = np.cos(theta)
    sine = np.sin(theta)
    cosine[0] = 1.0
    sine[0] = 0.0
    spread = lambda t, n: np.broadcast_to(t[None, :, None, :], (CH, C, n, 128)).reshape(-1, 128)
    twist = np.stack([spread(cosine, R), spread(sine, R)]).astype(np.float32)
    twist_rim = np.stack([spread(cosine, 2), spread(sine, 2)]).astype(np.float32)
    phi = 2 * np.pi * np.outer(d, b) / 128
    matrix = np.zeros((D, 2, 2, 128))
    matrix[:, 0, 0] = np.cos(phi)
    matrix[:, 0, 1] = np.sin(phi)
    matrix[:, 1, 0] = -np.sin(phi)
    matrix[:, 1, 1] = np.cos(phi)
    psi = 2 * np.pi * np.outer(16 + 32 * (d - 64), b) / NY
    alternate = np.where(b % 2 == 0, 1.0, -1.0)
    zero = np.zeros((D, 2, 2, 128))
    zero[:64, 0, 0] = np.cos(phi[:64])
    zero[:64, 1, 0] = -np.sin(phi[:64])
    zero[0, 1, 0] = alternate
    zero[64:, 0, 1] = np.cos(psi[64:])
    zero[64:, 1, 1] = -np.sin(psi[64:])
    back = np.zeros((2, 128, D, 2))
    back[0, :, :, 0] = np.cos(phi).T
    back[0, :, :, 1] = -np.sin(phi).T
    back[1, :, :, 0] = np.sin(phi).T
    back[1, :, :, 1] = np.cos(phi).T
    back_zero = np.zeros((2, 128, D, 2))
    back_zero[0, :, :64, 0] = 2 * np.cos(phi[:64]).T
    back_zero[0, :, :64, 1] = -2 * np.sin(phi[:64]).T
    back_zero[0, :, 0, 0] = 1.0
    back_zero[0, :, 0, 1] = alternate
    back_zero[1, :, 64:, 0] = 2 * np.cos(psi[64:]).T
    back_zero[1, :, 64:, 1] = -2 * np.sin(psi[64:]).T
    return {
        "forward_a": table_pair(forward_a),
        "forward_b": table_pair(matrix.reshape(256, 256)),
        "forward_b0": table_pair(zero.reshape(256, 256))[0],
        "twist": twist,
        "inverse_b": table_pair(back.reshape(256, 256)),
        "inverse_b0": table_pair(back_zero.reshape(256, 256))[0],
        "inverse_a": inverse_a,
        "inverse_rim": inverse_rim,
        "untwist": np.ascontiguousarray(twist.transpose(0, 2, 1)),
        "untwist_rim": np.ascontiguousarray(twist_rim.transpose(0, 2, 1)),
    }


def row_tables():
    s = np.arange(D)
    m1 = np.arange(D)
    m2 = np.arange(R)
    phi = 2 * np.pi * np.outer(m1, s) / D
    forward = np.zeros((2, D, D, 2))
    forward[0, :, :, 0] = np.cos(phi)
    forward[0, :, :, 1] = np.sin(phi)
    forward[1, :, :, 0] = -np.sin(phi)
    forward[1, :, :, 1] = np.cos(phi)
    inverse = np.zeros((D, 2, 2, D))
    inverse[:, 0, 0] = np.cos(phi).T
    inverse[:, 0, 1] = -np.sin(phi).T
    inverse[:, 1, 0] = np.sin(phi).T
    inverse[:, 1, 1] = np.cos(phi).T
    inverse = inverse / NX
    eye = np.eye(CH * C)

    def short(rows, flip):
        angle = 2 * np.pi * np.outer(m2, rows) / R
        block = np.zeros((2, R, 2, len(rows)))
        block[0, :, 0] = np.cos(angle)
        block[1, :, 0] = -np.sin(angle) * flip
        block[0, :, 1] = np.sin(angle) * flip
        block[1, :, 1] = np.cos(angle)
        block = np.round(block)
        return np.einsum("pmqr,gk->pgmqkr", block, eye).reshape(2 * CH * C * R, 2, -1)

    own = np.arange(R)
    rim = np.array([-1, R])
    rim_block = np.zeros((256, 2, 128))
    rim_block[:, :, :64] = short(rim, 1.0)

    def lanes(rows):
        theta = 2 * np.pi * np.outer(m1, rows) / NX
        both = np.stack([np.cos(theta), np.sin(theta)])
        wide = np.broadcast_to(both[:, :, None, :], (2, D, CH * C, len(rows))).reshape(2, D, -1)
        out = np.zeros((2, D, 128), np.float32)
        out[:, :, : wide.shape[2]] = wide
        return out

    return {
        "row_forward": table_pair(forward.reshape(256, 256)),
        "row_inverse": table_pair(inverse.reshape(256, 256)),
        "short_forward": short(own, -1.0).reshape(256, 256).astype(ml_dtypes.bfloat16),
        "short_inverse": short(own, 1.0).reshape(256, 256).astype(ml_dtypes.bfloat16),
        "short_rim": rim_block.reshape(256, 256).astype(ml_dtypes.bfloat16),
        "spin": lanes(own),
        "spin_step": lanes(np.array(STEP_ROWS)),
        "spin_rim": lanes(rim - 2),
    }


def velocity_row(ch, row):
    return ch * R + row if row >= 0 else 8 + ch * R + row + R


def dual_row(ch, row):
    if row in STEP_ROWS:
        return ch * R + row + 2
    return 8 + ch * 2 + (0 if row < -2 else 1)


def network_tables():
    order = (*LATE_ROWS, *EARLY_ROWS)
    taps = np.zeros((6, 18, 48))
    for at, i in enumerate(order):
        for a in range(-1, 2):
            for b in range(-1, 2):
                for ch in range(CH):
                    t = (3 * (a + 1) + b + 1) * 2 + ch
                    taps[at, t, (b + 1) * 16 + velocity_row(ch, i + a)] = 1
    outs = np.zeros((6, 24, 18))
    for at, k in enumerate(order):
        for a in range(-1, 2):
            i = k - a
            if i in STEP_ROWS:
                for b in range(-1, 2):
                    for o in range(CH):
                        outs[at, (b + 1) * 8 + o * R + i + 2, (3 * (a + 1) + b + 1) * 2 + o] = 1
    duals = np.zeros((R, 18, 48))
    for at, i in enumerate(STEP_ROWS):
        for a in range(-1, 2):
            for b in range(-1, 2):
                for o in range(CH):
                    t = (3 * (a + 1) + b + 1) * 2 + o
                    duals[at, t, (b + 1) * 16 + dual_row(o, i - a)] = 1
    low = lambda t: t.astype(ml_dtypes.bfloat16)
    inner = taps.reshape(6, 18, 3, 16)[4:, :, :, :8].reshape(2, 18, 24)
    return {
        "taps": low(taps),
        "taps_inner": low(inner),
        "taps_step": low(taps[[0, 1, 2, 4]]),
        "outs": low(outs),
        "duals": low(duals),
    }


def dot(x, y):
    return jnp.dot(x, y, preferred_element_type=F32)


def dot_nt(x, y):
    return lax.dot_general(x, y, (((1,), (1,)), ((), ())), preferred_element_type=F32)


def dot_tn(x, y):
    return lax.dot_general(x, y, (((0,), (0,)), ((), ())), preferred_element_type=F32)


def halves(x):
    high = x.astype(BF)
    return high, (x - high.astype(F32)).astype(BF)


def exact(form, pair, x):
    high, low = halves(x)
    return form(pair[0], high) + (form(pair[1], high) + form(pair[0], low))


def pair_low(form, pair, x):
    return form(pair[0], x) + form(pair[1], x)


def to_blocks(x):
    return jnp.concatenate([x[:, 128 * a : 128 * a + 128] for a in range(OUTER)], axis=0)


def from_blocks(x):
    rows = x.shape[0] // OUTER
    return jnp.concatenate([x[rows * a : rows * a + rows] for a in range(OUTER)], axis=1)


def column_forward(x, forward_a, forward_b, forward_b0, twist):
    y = exact(dot, forward_a, to_blocks(x))
    real, imag = y[:128], y[128:]
    cosine, sine = twist[0], twist[1]
    both = jnp.concatenate([real * cosine + imag * sine, imag * cosine - real * sine], axis=1)
    general = exact(dot_nt, forward_b, both)
    zero = dot_nt(forward_b0[...], both.astype(BF))
    lane = lax.broadcasted_iota(jnp.int32, general.shape, 1)
    return jnp.where(lane % 64 < R, zero, general).astype(BF)


def column_inverse_first(x, inverse_b, inverse_b0, untwist):
    general = pair_low(dot, inverse_b, x)
    zero = dot(inverse_b0[...], x)
    lane = lax.broadcasted_iota(jnp.int32, general.shape, 1)
    y = jnp.where(lane % 64 < R, zero, general)
    real, imag = y[:128], y[128:]
    cosine, sine = untwist[0], untwist[1]
    return real * cosine - imag * sine, imag * cosine + real * sine


def multiplier(device):
    m1 = lax.broadcasted_iota(jnp.int32, (128, 128), 0)
    lane = lax.broadcasted_iota(jnp.int32, (128, 128), 1)
    m = m1 + 128 * (lane % R)
    m = jnp.where(2 * m < NX, m, jnp.where(2 * m == NX, 0, m - NX))
    c = (lane % 64) // R
    n = c + OUTER * device
    n = jnp.where(2 * n < NY, n, n - NY)
    packed = jnp.where(device < 64, OUTER * device, 16 + OUTER * (device - 64))
    n = jnp.where(c == 0, packed, n)
    wave_row = m.astype(F32) * (1.0 / NX)
    wave_col = n.astype(F32) * (1.0 / NY)
    row_square = wave_row * wave_row
    col_square = wave_col * wave_col
    square = row_square + col_square
    some = square > 0
    inverse = 1.0 / jnp.where(some, square, 1.0)
    same = jnp.where(some, jnp.where(lane < 64, col_square, row_square) * inverse, 1.0)
    sign = jnp.where(lane % 2 == 0, 1.0, -1.0)
    return sign * same, -sign * (wave_row * wave_col) * inverse


def side_by_side(parts):
    return jnp.concatenate(parts, axis=1)


def staggered(count, *stages):
    values = {}
    for step in range(count + len(stages) - 1):
        for lag in reversed(range(len(stages))):
            index = step - lag
            if 0 <= index < count:
                values[index] = stages[lag](index, values.get(index))


def flat_taps(weights):
    rows = [weights[t // 3, t % 3].astype(F32) for t in range(9)]
    return jnp.concatenate(rows, axis=0).astype(BF)


def diagonal(block, count):
    empty = jnp.zeros_like(block)
    rows = [side_by_side([block if i == k else empty for k in range(count)]) for i in range(count)]
    return jnp.concatenate(rows, axis=0)


def gelu_parts(pre):
    square = pre * pre
    tangent = jnp.tanh(pre * (GELU_SCALE + (GELU_SCALE * GELU_CUBIC) * square))
    gate = 0.5 + 0.5 * tangent
    return square, gate, pre * gate


def slope_of(square, gate, value):
    return gate + value * (1.0 - gate) * (2 * GELU_SCALE + (6 * GELU_SCALE * GELU_CUBIC) * square)


def early_kernel(
    field,
    forward_a,
    forward_b,
    forward_b0,
    twist,
    velocity,
    w_in,
    w_mid,
    w_out,
    taps,
    outs,
    taps_inner,
    sent,
    early_one,
    early_two,
    inner,
):
    x = jnp.concatenate([field[0], field[1]], axis=0)
    sent[...] = column_forward(x, forward_a, forward_b, forward_b0, twist).reshape(D, 2, 128)
    base = jnp.concatenate([velocity[0], velocity[1]], axis=0)
    shifts = [pltpu.roll(base, 1, 1), base, pltpu.roll(base, NY - 1, 1)]
    inner[...] = jnp.concatenate(shifts, axis=0).astype(BF)
    flat_in = flat_taps(w_in.ready())
    first = jnp.concatenate([dot_tn(flat_in, taps_inner[i]).astype(BF) for i in range(2)], axis=0)
    middle = diagonal(w_mid[...], 2)

    def columns(index):
        return slice(index * TILE, index * TILE + TILE)

    def layer_one(index, _):
        return dot(first, inner[:, columns(index)])

    def gelu_one(index, pre):
        low = gelu_parts(pre)[2].astype(BF)
        early_one[:, columns(index)] = low[:HID]
        return low

    def layer_two(index, low):
        return dot(middle, low)

    def gelu_two(index, pre):
        early_two[:, columns(index)] = gelu_parts(pre)[2].astype(BF)

    staggered(NY // TILE, layer_one, gelu_one, layer_two, gelu_two)


def network_kernel(
    dual_sent,
    early_one,
    early_two,
    above,
    forward_a,
    forward_b,
    forward_b0,
    twist,
    velocity,
    w_in,
    w_mid,
    w_out,
    taps,
    outs,
    _,
    sent,
    stack,
    act_one_out,
    act_two_out,
    act_one,
    act_two,
    partial,
    semaphores,
):
    sent[:, 1] = dual_sent[...]
    mine = 3 * HID
    ready = [
        pltpu.make_async_copy(early_one, act_one_out.at[mine:], semaphores.at[2, 0]),
        pltpu.make_async_copy(early_two.at[:HID], act_two_out.at[mine:], semaphores.at[2, 1]),
    ]
    for copy in ready:
        copy.start()
    held = (act_one, act_two)
    homes = (act_one_out, act_two_out)
    upper = [above[c] for c in range(CH)]
    base = jnp.concatenate([velocity[0], velocity[1], *upper], axis=0)
    stack[0:16, :] = pltpu.roll(base, 1, 1).astype(BF)
    stack[16:32, :] = base.astype(BF)
    stack[32:48, :] = pltpu.roll(base, NY - 1, 1).astype(BF)
    flat_in, flat_out = flat_taps(w_in), flat_taps(w_out)
    first = jnp.concatenate([dot_tn(flat_in, taps[i]).astype(BF) for i in range(4)], axis=0)
    third = side_by_side([dot(outs[i], flat_out).astype(BF) for i in range(6)])
    middle = diagonal(w_mid[...], R)

    def columns(index):
        return slice(index * TILE, index * TILE + TILE)

    def layer_one(index, _):
        return dot(first, stack[:, columns(index)])

    def gelu_one(index, pre):
        low = gelu_parts(pre)[2].astype(BF)
        act_one[:, columns(index)] = low[:mine]
        return low

    def layer_two(index, low):
        return dot(middle, low)

    def gelu_two(index, pre):
        at = columns(index)
        low = gelu_parts(pre)[2].astype(BF)
        act_two[:, at] = low[:mine]
        for k in range(2):
            pltpu.make_async_copy(
                held[k].at[:, at], homes[k].at[:mine, at], semaphores.at[k, index]
            ).start()
        return low

    def layer_three(index, low):
        at = columns(index)
        partial[:, at] = dot(third[:, :OWN], low) + dot(third[:, OWN:], early_two[:, at])

    staggered(NY // TILE, layer_one, gelu_one, layer_two, gelu_two, layer_three)
    correction = (
        pltpu.roll(partial[0:8, :], 1, 1) + partial[8:16, :] + pltpu.roll(partial[16:24, :], NY - 1, 1)
    )
    near = [jnp.concatenate([upper[c][1:], velocity[c][:3]], axis=0) for c in range(CH)]
    rows = [field[1:5] for field in near]
    pieces = []
    for c in range(CH):
        flux = near[0] * near[c]
        side = rows[1] * rows[c]
        pieces.append(
            (flux[2:] - flux[:-2]) + (pltpu.roll(side, NY - 1, 1) - pltpu.roll(side, 1, 1))
        )
    advect = 0.5 * jnp.concatenate(pieces, axis=0)
    provisional = jnp.concatenate(rows, axis=0) + STEP_SIZE * (correction - advect)
    sent[:, 0] = column_forward(provisional, forward_a, forward_b, forward_b0, twist).reshape(D, 2, 128)
    for copy in ready:
        copy.wait()
    for k in range(2):
        for index in range(NY // TILE):
            at = pl.ds(index * TILE, TILE)
            pltpu.make_async_copy(held[k].at[:, at], homes[k].at[:mine, at], semaphores.at[k, index]).wait()


def middle_kernel(
    device, got, row_forward, spin, spin_step, short_forward, short_inverse, short_rim, spin_rim, row_inverse, sent
):
    same, cross = multiplier(device[0])
    v = pair_low(dot, row_forward, side_by_side([got[:, k].reshape(256, 128) for k in range(2)]))
    plain = (spin[0], spin[1])
    step = (spin_step[0], spin_step[1])
    fields = []
    for k, (cosine, sine) in enumerate((step, plain)):
        real, imag = v[:128, 128 * k : 128 * k + 128], v[128:, 128 * k : 128 * k + 128]
        fields.append(side_by_side([real * cosine + imag * sine, imag * cosine - real * sine]))
    high, low = halves(jnp.concatenate(fields, axis=0))
    full = dot(high, short_forward[...]) + dot(low, short_forward[...])
    fields = []
    for k in range(2):
        part = full[128 * k : 128 * k + 128]
        real, imag = part[:, :128], part[:, 128:]
        real = same * real + cross * pltpu.roll(real, 64, 1)
        imag = same * imag + cross * pltpu.roll(imag, 64, 1)
        fields.append(side_by_side([real, imag]))
    high, low = halves(jnp.concatenate(fields, axis=0))
    full = dot(high, short_inverse[...]) + dot(low, short_inverse[...])
    rim = dot(high[128:], short_rim[...]) + dot(low[128:], short_rim[...])
    parts = []
    for part, (cosine, sine) in (
        (full[:128], plain),
        (full[128:], step),
        (rim, (spin_rim[0], spin_rim[1])),
    ):
        real, imag = part[:, :128], part[:, 128:]
        parts.append(jnp.concatenate([real * cosine - imag * sine, imag * cosine + real * sine], axis=0))
    out = exact(dot, row_inverse, side_by_side(parts)).astype(BF)
    for k in range(3):
        sent[:, k] = out[:, 128 * k : 128 * k + 128].reshape(D, 2, 128)


def backward_kernel(
    got,
    inverse_b,
    inverse_b0,
    untwist,
    inverse_a,
    inverse_rim,
    w_mid,
    w_out,
    duals,
    taps,
    stack,
    act_one_home,
    act_two_home,
    slope_one_home,
    slope_two_home,
    sent,
    act_one,
    act_two,
    slope_one,
    slope_two,
    dual_stack,
    sum_mid,
    sum_in,
    sum_out,
    semaphores,
):
    held = (slope_two, act_one, act_two, slope_one)
    homes = (slope_two_home, act_one_home, act_two_home, slope_one_home)
    count = NY // BACK_TILE

    def fetch(index):
        at = pl.ds(pl.multiple_of(index * BACK_TILE, BACK_TILE), BACK_TILE)
        for k in range(4):
            pltpu.make_async_copy(homes[k].at[:, at], held[k].at[:, at], semaphores.at[k, index]).start()

    fetch(0)
    both = side_by_side([got[:, 1].reshape(256, 128), got[:, 2].reshape(256, 128)])
    general = pair_low(dot, inverse_b, both)
    zero = dot(inverse_b0[...], both)
    lane = lax.broadcasted_iota(jnp.int32, general.shape, 1)
    beyond = jnp.where(lane < 128, lane % 64 - R, lane % 32 - 2)
    y = jnp.where(beyond < 0, zero, general)
    real, imag = y[:128], y[128:]
    cosine, sine = untwist[0], untwist[1]
    real, imag = real * cosine - imag * sine, imag * cosine + real * sine
    own = exact(dot_nt, inverse_a, side_by_side([real[:, :128], imag[:, :128]]))
    rim = exact(dot_nt, inverse_rim, side_by_side([real[:, 128:192], imag[:, 128:192]]))
    base = jnp.concatenate([from_blocks(own), from_blocks(rim)], axis=0)
    dual_stack[0:16, :] = pltpu.roll(base, NY - 1, 1).astype(BF)
    dual_stack[16:32, :] = base.astype(BF)
    dual_stack[32:48, :] = pltpu.roll(base, 1, 1).astype(BF)
    flat_out = flat_taps(w_out)
    spread_out = jnp.concatenate([dot_tn(flat_out, duals[i]).astype(BF) for i in range(R)], axis=0)
    middle = diagonal(w_mid[...].T, R)
    sum_mid[...] = jnp.zeros_like(sum_mid)
    sum_in[...] = jnp.zeros_like(sum_in)
    sum_out[...] = jnp.zeros_like(sum_out)

    def step(index, _):
        at = pl.ds(pl.multiple_of(index * BACK_TILE, BACK_TILE), BACK_TILE)
        @pl.when(index + 1 < count)
        def _():
            fetch(index + 1)

        def arrived(k):
            pltpu.make_async_copy(homes[k].at[:, at], held[k].at[:, at], semaphores.at[k, index]).wait()
            return held[k][:, at]

        dual = dual_stack[:, at]
        back_two = dot(spread_out, dual)
        delta_two = (back_two * arrived(0)).astype(BF)
        sum_mid[...] += dot_nt(delta_two, arrived(1))
        back_one = dot(middle, delta_two)
        sum_out[...] += dot_nt(arrived(2), dual)
        delta_one = (back_one * arrived(3)).astype(BF)
        sum_in[...] += dot_nt(delta_one, stack[:, at])
        return 0

    lax.fori_loop(0, count, step, 0, unroll=2)
    mid = sum(sum_mid[64 * i : 64 * i + 64, 64 * i : 64 * i + 64] for i in range(R))
    flips = []
    for source, choose in ((sum_in, taps), (sum_out, duals)):
        flip = jnp.zeros((18, HID), F32)
        for i in range(R):
            high, low = halves(source[64 * i : 64 * i + 64, :])
            flip = flip + (dot_nt(choose[i], high) + dot_nt(choose[i], low))
        flips.append(flip)
    packed = jnp.concatenate([side_by_side([mid[:32], mid[32:]]), side_by_side(flips)], axis=0)
    low = packed.astype(BF).reshape(25, 2, 128)
    for k in range(8):
        sent[k] = low


def added(got, count):
    total = got[0].astype(F32)
    for k in range(1, count):
        total = total + got[k].astype(F32)
    return total


def partial_sum_kernel(got, sent):
    low = added(got, 8).astype(BF)
    for k in range(16):
        sent[k] = low


def total_kernel(got, grad_mid, grad_in, grad_out):
    total = added(got, 16).reshape(50, 128)
    grad_mid[:32] = total[:32, :64]
    grad_mid[32:] = total[:32, 64:]
    for t in range(9):
        pair = total[32 + 2 * t : 34 + 2 * t]
        grad_in[t // 3, t % 3] = pair[:, :64]
        grad_out[t // 3, t % 3] = pair[:, 64:]


def field_kernel(got, inverse_b, inverse_b0, untwist, inverse_a, field):
    real, imag = column_inverse_first(got[:, 0].reshape(256, 128), inverse_b, inverse_b0, untwist)
    x = from_blocks(exact(dot_nt, inverse_a, side_by_side([real, imag])))
    field[0] = x[:R]
    field[1] = x[R:]


class Staged:
    def __init__(self, copy, ref):
        self.copy, self.ref, self.waited = copy, ref, False

    def ready(self):
        if not self.waited:
            self.copy.wait()
            self.waited = True
        return self.ref

    def __getitem__(self, index):
        return self.ready()[index]


def call(kernel, outputs, inputs, scratch=(), scalars=0, staged=0, kept=0, far=0, far_out=0):
    count = len(inputs)
    outputs = outputs if isinstance(outputs, list) else [outputs]
    spec = lambda space: pl.BlockSpec(memory_space=space)
    specs = [spec(pltpu.SMEM)] * scalars
    specs += [spec(pltpu.VMEM)] * (count - scalars - staged - far)
    specs += [spec(pltpu.HBM)] * (staged + far)
    out_specs = [spec(pltpu.VMEM)] * (len(outputs) - far_out) + [spec(pltpu.HBM)] * far_out
    out_specs += [spec(pltpu.VMEM)] * kept
    first = count - staged - far
    dropped = staged - kept

    def run(*refs):
        given = list(refs[:count])
        own = len(outputs) - kept
        targets = refs[count + own : count + own + kept]
        rest = refs[count + own + kept :]
        if staged:
            for k in range(staged):
                target = rest[len(scratch) + k] if k < dropped else targets[k - dropped]
                copy = pltpu.make_async_copy(given[first + k], target, rest[-1].at[k])
                copy.start()
                given[first + k] = Staged(copy, target)
        kernel(*given, *refs[count : count + own], *rest[: len(scratch)])
        for k in range(staged):
            given[first + k].ready()

    held = [pltpu.VMEM(x.shape, x.dtype) for x in inputs[first : first + dropped]]
    kept_out = [pltpu.VMEM(x.shape, x.dtype) for x in inputs[first + dropped : first + staged]]
    pinned = [pltpu.with_memory_space_constraint(jnp.asarray(x), pltpu.HBM) for x in inputs[first:]]
    inputs = [*inputs[:first], *pinned]
    far_first = len(outputs) - far_out
    outputs = outputs[:far_first] + [pltpu.HBM(x.shape, x.dtype) for x in outputs[far_first:]]
    outputs += kept_out
    if staged:
        held.append(pltpu.SemaphoreType.DMA((staged,)))
    result = pl.pallas_call(
        run,
        out_shape=outputs,
        in_specs=specs,
        out_specs=out_specs,
        scratch_shapes=list(scratch) + held,
        compiler_params=pltpu.CompilerParams(vmem_limit_bytes=VMEM_LIMIT),
    )(*inputs)
    return result if len(outputs) > 1 else result[0]


def slope_one_kernel(stack, w_in, taps):
    flat_in = flat_taps(w_in)
    first = jnp.concatenate([dot_tn(flat_in, taps[i]).astype(BF) for i in range(R)], axis=0)
    return lambda at: slope_of(*gelu_parts(dot(first, stack[:, at])))


def slope_two_kernel(act_one, w_mid):
    middle = diagonal(w_mid[...], R)
    return lambda at: slope_of(*gelu_parts(dot(middle, act_one[:, at])))


def prefetch(arrays, after, maker, inputs, near=()):
    count, given = len(arrays), len(inputs)

    def run(*refs):
        sources, close, refs = refs[: count + given], refs[count + given + 1 :][: len(near)], refs[count + given + 1 + len(near) :]
        targets, slope_out, refs = refs[:count], refs[count], refs[count + 1 :]
        held, slope, semaphores, out_semaphores = refs[:given], *refs[given:]
        copies = []
        for k in list(range(count, count + given)) + list(range(count)):
            target = targets[k] if k < count else held[k - count]
            copies.append(pltpu.make_async_copy(sources[k], target, semaphores.at[k]))
            copies[-1].start()
        for copy in copies[:given]:
            copy.wait()
        slopes = maker(*close, *held)
        stores = []
        for index in range(NY // TILE):
            at = slice(index * TILE, index * TILE + TILE)
            slope[:, at] = slopes(at)
            stores.append(pltpu.make_async_copy(slope.at[:, at], slope_out.at[:, at], out_semaphores.at[index]))
            stores[-1].start()
        for copy in copies[given:] + stores:
            copy.wait()

    arrays = [jnp.asarray(x) for x in [*arrays, *inputs]]
    *tables, slope = pl.pallas_call(
        run,
        out_shape=[pltpu.VMEM(x.shape, x.dtype) for x in arrays[:count]] + [pltpu.HBM((OWN, NY), F32)],
        in_specs=[pl.BlockSpec(memory_space=pltpu.HBM)] * (count + given)
        + [pl.BlockSpec(memory_space=pl.ANY)]
        + [pl.BlockSpec(memory_space=pltpu.VMEM)] * len(near),
        out_specs=[pl.BlockSpec(memory_space=pltpu.VMEM)] * count + [pl.BlockSpec(memory_space=pltpu.HBM)],
        scratch_shapes=[pltpu.VMEM(x.shape, x.dtype) for x in arrays[count:]]
        + [
            pltpu.VMEM((OWN, NY), F32),
            pltpu.SemaphoreType.DMA((count + given,)),
            pltpu.SemaphoreType.DMA((NY // TILE,)),
        ],
        compiler_params=pltpu.CompilerParams(vmem_limit_bytes=VMEM_LIMIT),
    )(*[pltpu.with_memory_space_constraint(x, pltpu.HBM) for x in arrays], after, *near)
    return tables, slope


def exchange(x, groups=None):
    return lax.all_to_all(x, "rows", split_axis=0, concat_axis=0, tiled=True, axis_index_groups=groups)


def body(velocity, cotangent, w_in, w_mid, w_out):
    columns = column_tables()
    rows = row_tables()
    net = network_tables()
    scale = STEP_SIZE / math.sqrt(NX * NY)
    shape = jax.ShapeDtypeStruct
    w_in = jnp.transpose(w_in, (1, 2, 3, 0))
    device = lax.axis_index("rows").reshape(1)
    down = [(i, (i + 1) % D) for i in range(D)]
    above = lax.ppermute(velocity, "rows", down)

    forward = [columns[k] for k in ("forward_a", "forward_b", "forward_b0", "twist")]
    ahead = [*forward, velocity, w_in, w_mid, w_out, net["taps"], net["outs"], net["taps_inner"]]
    dual_sent, early_one, early_two, *ahead = call(
        early_kernel,
        [shape((D, 2, 128), BF), pltpu.VMEM((HID, NY), BF), pltpu.VMEM((2 * HID, NY), BF)],
        [cotangent, *ahead],
        [pltpu.VMEM((24, NY), BF)],
        staged=1 + len(ahead),
        kept=len(ahead),
    )

    big = shape((OWN, NY), BF)
    first_sent, stack, act_one, act_two = call(
        network_kernel,
        [shape((D, 2, 2, 128), BF), pltpu.VMEM((48, NY), BF), big, big],
        [dual_sent, early_one, early_two, above, *ahead],
        [
            pltpu.VMEM((3 * HID, NY), BF),
            pltpu.VMEM((3 * HID, NY), BF),
            pltpu.VMEM((24, NY), F32),
            pltpu.SemaphoreType.DMA((3, NY // TILE)),
        ],
        far_out=2,
    )
    first_got = exchange(first_sent)
    names = ("row_forward", "spin", "spin_step", "short_forward", "short_inverse", "short_rim", "spin_rim")
    tables, slope_one = prefetch(
        [*[rows[k] for k in names], rows["row_inverse"]],
        first_sent,
        slope_one_kernel,
        [w_in, net["taps_step"]],
        [stack],
    )
    second_sent = call(
        middle_kernel, shape((D, 3, 2, 128), BF), [device, first_got, *tables], scalars=1
    )
    second_got = exchange(second_sent)
    back = [columns[k] for k in ("inverse_b", "inverse_b0", "untwist")]
    empty = np.zeros((2, 128, 64), np.float32)
    untwists = np.concatenate([columns["untwist"], columns["untwist_rim"], empty], axis=2)
    tables, slope_two = prefetch(
        [
            *back[:2],
            untwists,
            table_pair(columns["inverse_a"] * scale),
            table_pair(columns["inverse_rim"] * scale),
            w_mid,
            w_out,
            net["duals"],
            net["taps_step"],
        ],
        second_sent,
        slope_two_kernel,
        [act_one, w_mid],
    )
    partial = call(
        backward_kernel,
        shape((8, 25, 2, 128), BF),
        [second_got, *tables, stack, act_one, act_two, slope_one, slope_two],
        [
            *[pltpu.VMEM((OWN, NY), t) for t in (BF, BF, F32, F32)],
            pltpu.VMEM((48, NY), BF),
            pltpu.VMEM((OWN, OWN), F32),
            pltpu.VMEM((OWN, 48), F32),
            pltpu.VMEM((OWN, 48), F32),
            pltpu.SemaphoreType.DMA((4, NY // BACK_TILE)),
        ],
        far=4,
    )
    along_z = [[16 * z + r for z in range(8)] for r in range(16)]
    across_z = [[16 * z + r for r in range(16)] for z in range(8)]
    partial = call(partial_sum_kernel, shape((16, 25, 2, 128), BF), [exchange(partial, along_z)])
    new_velocity = call(
        field_kernel,
        shape((CH, R, NY), F32),
        [second_got, *back, table_pair(columns["inverse_a"])],
        staged=4,
    )
    grad_mid, grad_in, grad_out = call(
        total_kernel,
        [shape((HID, HID), F32), shape((3, 3, 2, HID), F32), shape((3, 3, 2, HID), F32)],
        [exchange(partial, across_z)],
    )
    return new_velocity, jnp.transpose(grad_in, (3, 0, 1, 2)), grad_mid, grad_out


def solution(mesh):
    in_specs = (P("batch", "rows", None), P("batch", "rows", None), P(), P(), P())
    out_specs = (
        P("batch", "rows", None),
        P("batch", None, None, None),
        P("batch", None),
        P("batch", None, None, None),
    )
    return jax.shard_map(body, mesh=mesh, in_specs=in_specs, out_specs=out_specs, check_vma=False)
```

```python
import functools
import math

import jax
import jax.numpy as jnp
import ml_dtypes
import numpy as np
from jax import lax
from jax.experimental import pallas as pl
from jax.experimental.pallas import tpu as pltpu
from jax.sharding import PartitionSpec as P

STEP_SIZE = 0.5
GELU_SCALE = 0.7978845608028654
GELU_CUBIC = 0.044715
BF = jnp.bfloat16
F32 = jnp.float32
TILE = 1024
BACK_TILE = 2048
SUM_BITS = 0b0001111
VMEM_LIMIT = 32 * 1024 * 1024

R = 4
D = 128
NX = R * D
OUTER = 32
NY = OUTER * 128
C = OUTER // 2
CH = 2
HID = 64
OWN = R * HID
STEP_ROWS = (-2, -1, 0, 1)
LATE_ROWS = (-2, -1, 0, -3)
EARLY_ROWS = (1, 2)


def table_pair(matrix):
    high = np.asarray(matrix, np.float64).astype(ml_dtypes.bfloat16)
    low = (matrix - high.astype(np.float64)).astype(ml_dtypes.bfloat16)
    return np.stack([high, low])


def column_tables():
    a = np.arange(OUTER)
    b = np.arange(128)
    d = np.arange(D)
    c = np.arange(C)
    eye = np.eye(R * CH).reshape(CH, R, CH, R)
    sign = np.where(a % 2 == 0, 1.0, -1.0)
    angle = 2 * np.pi * np.outer(c, a) / OUTER
    first = np.stack([np.cos(angle), -np.sin(angle)])
    first[0, 0] = 1.0
    first[1, 0] = sign
    forward_a = np.einsum("pca,hrgs->phcrags", first, eye).reshape(256, 256)
    last = np.stack([2 * np.cos(angle), -2 * np.sin(angle)])
    last[0, 0] = 1.0
    last[1, 0] = sign
    last = last / NY
    inverse_a = np.einsum("pca,gshr->agsphcr", last, eye).reshape(256, 256)
    half = np.zeros((2, 4, CH, 2))
    for h in range(CH):
        for e in range(2):
            half[h, h * 2 + e, h, e] = 1.0
    rim = np.zeros((8, CH, 2))
    rim[:4] = np.eye(4).reshape(4, CH, 2)
    inverse_rim = np.einsum("pca,khr->akphcr", last, rim).reshape(256, 128)
    theta = 2 * np.pi * np.outer(c, b) / NY
    cosine = np.cos(theta)
    sine = np.sin(theta)
    cosine[0] = 1.0
    sine[0] = 0.0
    spread = lambda t, n: np.broadcast_to(t[None, :, None, :], (CH, C, n, 128)).reshape(-1, 128)
    twist = np.stack([spread(cosine, R), spread(sine, R)]).astype(np.float32)
    twist_rim = np.stack([spread(cosine, 2), spread(sine, 2)]).astype(np.float32)
    phi = 2 * np.pi * np.outer(d, b) / 128
    matrix = np.zeros((D, 2, 2, 128))
    matrix[:, 0, 0] = np.cos(phi)
    matrix[:, 0, 1] = np.sin(phi)
    matrix[:, 1, 0] = -np.sin(phi)
    matrix[:, 1, 1] = np.cos(phi)
    psi = 2 * np.pi * np.outer(16 + 32 * (d - 64), b) / NY
    alternate = np.where(b % 2 == 0, 1.0, -1.0)
    zero = np.zeros((D, 2, 2, 128))
    zero[:64, 0, 0] = np.cos(phi[:64])
    zero[:64, 1, 0] = -np.sin(phi[:64])
    zero[0, 1, 0] = alternate
    zero[64:, 0, 1] = np.cos(psi[64:])
    zero[64:, 1, 1] = -np.sin(psi[64:])
    back = np.zeros((2, 128, D, 2))
    back[0, :, :, 0] = np.cos(phi).T
    back[0, :, :, 1] = -np.sin(phi).T
    back[1, :, :, 0] = np.sin(phi).T
    back[1, :, :, 1] = np.cos(phi).T
    back_zero = np.zeros((2, 128, D, 2))
    back_zero[0, :, :64, 0] = 2 * np.cos(phi[:64]).T
    back_zero[0, :, :64, 1] = -2 * np.sin(phi[:64]).T
    back_zero[0, :, 0, 0] = 1.0
    back_zero[0, :, 0, 1] = alternate
    back_zero[1, :, 64:, 0] = 2 * np.cos(psi[64:]).T
    back_zero[1, :, 64:, 1] = -2 * np.sin(psi[64:]).T
    return {
        "forward_a": table_pair(forward_a),
        "forward_b": table_pair(matrix.reshape(256, 256)),
        "forward_b0": table_pair(zero.reshape(256, 256))[0],
        "twist": twist,
        "inverse_b": table_pair(back.reshape(256, 256)),
        "inverse_b0": table_pair(back_zero.reshape(256, 256))[0],
        "inverse_a": inverse_a,
        "inverse_rim": inverse_rim,
        "untwist": np.ascontiguousarray(twist.transpose(0, 2, 1)),
        "untwist_rim": np.ascontiguousarray(twist_rim.transpose(0, 2, 1)),
    }


def row_tables():
    s = np.arange(D)
    m1 = np.arange(D)
    m2 = np.arange(R)
    phi = 2 * np.pi * np.outer(m1, s) / D
    forward = np.zeros((2, D, D, 2))
    forward[0, :, :, 0] = np.cos(phi)
    forward[0, :, :, 1] = np.sin(phi)
    forward[1, :, :, 0] = -np.sin(phi)
    forward[1, :, :, 1] = np.cos(phi)
    inverse = np.zeros((D, 2, 2, D))
    inverse[:, 0, 0] = np.cos(phi).T
    inverse[:, 0, 1] = -np.sin(phi).T
    inverse[:, 1, 0] = np.sin(phi).T
    inverse[:, 1, 1] = np.cos(phi).T
    inverse = inverse / NX
    eye = np.eye(CH * C)

    def short(rows, flip):
        angle = 2 * np.pi * np.outer(m2, rows) / R
        block = np.zeros((2, R, 2, len(rows)))
        block[0, :, 0] = np.cos(angle)
        block[1, :, 0] = -np.sin(angle) * flip
        block[0, :, 1] = np.sin(angle) * flip
        block[1, :, 1] = np.cos(angle)
        block = np.round(block)
        return np.einsum("pmqr,gk->pgmqkr", block, eye).reshape(2 * CH * C * R, 2, -1)

    own = np.arange(R)
    rim = np.array([-1, R])
    rim_block = np.zeros((256, 2, 128))
    rim_block[:, :, :64] = short(rim, 1.0)

    def lanes(rows):
        theta = 2 * np.pi * np.outer(m1, rows) / NX
        both = np.stack([np.cos(theta), np.sin(theta)])
        wide = np.broadcast_to(both[:, :, None, :], (2, D, CH * C, len(rows))).reshape(2, D, -1)
        out = np.zeros((2, D, 128), np.float32)
        out[:, :, : wide.shape[2]] = wide
        return out

    return {
        "row_forward": table_pair(forward.reshape(256, 256)),
        "row_inverse": table_pair(inverse.reshape(256, 256)),
        "short_forward": short(own, -1.0).reshape(256, 256).astype(ml_dtypes.bfloat16),
        "short_inverse": short(own, 1.0).reshape(256, 256).astype(ml_dtypes.bfloat16),
        "short_rim": rim_block.reshape(256, 256).astype(ml_dtypes.bfloat16),
        "spin": lanes(own),
        "spin_step": lanes(np.array(STEP_ROWS)),
        "spin_rim": lanes(rim - 2),
    }


def velocity_row(ch, row):
    return ch * R + row if row >= 0 else 8 + ch * R + row + R


def dual_row(ch, row):
    if row in STEP_ROWS:
        return ch * R + row + 2
    return 8 + ch * 2 + (0 if row < -2 else 1)


def network_tables():
    order = (*LATE_ROWS, *EARLY_ROWS)
    taps = np.zeros((6, 18, 48))
    for at, i in enumerate(order):
        for a in range(-1, 2):
            for b in range(-1, 2):
                for ch in range(CH):
                    t = (3 * (a + 1) + b + 1) * 2 + ch
                    taps[at, t, (b + 1) * 16 + velocity_row(ch, i + a)] = 1
    outs = np.zeros((6, 24, 18))
    for at, k in enumerate(order):
        for a in range(-1, 2):
            i = k - a
            if i in STEP_ROWS:
                for b in range(-1, 2):
                    for o in range(CH):
                        outs[at, (b + 1) * 8 + o * R + i + 2, (3 * (a + 1) + b + 1) * 2 + o] = 1
    duals = np.zeros((R, 18, 48))
    for at, i in enumerate(STEP_ROWS):
        for a in range(-1, 2):
            for b in range(-1, 2):
                for o in range(CH):
                    t = (3 * (a + 1) + b + 1) * 2 + o
                    duals[at, t, (b + 1) * 16 + dual_row(o, i - a)] = 1
    low = lambda t: t.astype(ml_dtypes.bfloat16)
    inner = taps.reshape(6, 18, 3, 16)[4:, :, :, :8].reshape(2, 18, 24)
    return {
        "taps": low(taps),
        "taps_inner": low(inner),
        "taps_step": low(taps[[0, 1, 2, 4]]),
        "outs": low(outs),
        "duals": low(duals),
    }


def dot(x, y):
    return jnp.dot(x, y, preferred_element_type=F32)


def dot_nt(x, y):
    return lax.dot_general(x, y, (((1,), (1,)), ((), ())), preferred_element_type=F32)


def dot_tn(x, y):
    return lax.dot_general(x, y, (((0,), (0,)), ((), ())), preferred_element_type=F32)


def halves(x):
    high = x.astype(BF)
    return high, (x - high.astype(F32)).astype(BF)


def exact(form, pair, x):
    high, low = halves(x)
    return form(pair[0], high) + (form(pair[1], high) + form(pair[0], low))


def pair_low(form, pair, x):
    return form(pair[0], x) + form(pair[1], x)


def to_blocks(x):
    return jnp.concatenate([x[:, 128 * a : 128 * a + 128] for a in range(OUTER)], axis=0)


def from_blocks(x):
    rows = x.shape[0] // OUTER
    return jnp.concatenate([x[rows * a : rows * a + rows] for a in range(OUTER)], axis=1)


def column_forward(x, forward_a, forward_b, forward_b0, twist):
    y = exact(dot, forward_a, to_blocks(x))
    real, imag = y[:128], y[128:]
    cosine, sine = twist[0], twist[1]
    both = jnp.concatenate([real * cosine + imag * sine, imag * cosine - real * sine], axis=1)
    general = exact(dot_nt, forward_b, both)
    zero = dot_nt(forward_b0[...], both.astype(BF))
    lane = lax.broadcasted_iota(jnp.int32, general.shape, 1)
    return jnp.where(lane % 64 < R, zero, general).astype(BF)


def column_inverse_first(x, inverse_b, inverse_b0, untwist):
    general = pair_low(dot, inverse_b, x)
    zero = dot(inverse_b0[...], x)
    lane = lax.broadcasted_iota(jnp.int32, general.shape, 1)
    y = jnp.where(lane % 64 < R, zero, general)
    real, imag = y[:128], y[128:]
    cosine, sine = untwist[0], untwist[1]
    return real * cosine - imag * sine, imag * cosine + real * sine


def multiplier(device):
    m1 = lax.broadcasted_iota(jnp.int32, (128, 128), 0)
    lane = lax.broadcasted_iota(jnp.int32, (128, 128), 1)
    m = m1 + 128 * (lane % R)
    m = jnp.where(2 * m < NX, m, jnp.where(2 * m == NX, 0, m - NX))
    c = (lane % 64) // R
    n = c + OUTER * device
    n = jnp.where(2 * n < NY, n, n - NY)
    packed = jnp.where(device < 64, OUTER * device, 16 + OUTER * (device - 64))
    n = jnp.where(c == 0, packed, n)
    wave_row = m.astype(F32) * (1.0 / NX)
    wave_col = n.astype(F32) * (1.0 / NY)
    row_square = wave_row * wave_row
    col_square = wave_col * wave_col
    square = row_square + col_square
    some = square > 0
    inverse = 1.0 / jnp.where(some, square, 1.0)
    same = jnp.where(some, jnp.where(lane < 64, col_square, row_square) * inverse, 1.0)
    sign = jnp.where(lane % 2 == 0, 1.0, -1.0)
    return sign * same, -sign * (wave_row * wave_col) * inverse


def side_by_side(parts):
    return jnp.concatenate(parts, axis=1)


def staggered(count, *stages):
    values = {}
    for step in range(count + len(stages) - 1):
        for lag in reversed(range(len(stages))):
            index = step - lag
            if 0 <= index < count:
                values[index] = stages[lag](index, values.get(index))


def flat_taps(weights):
    rows = [weights[t // 3, t % 3].astype(F32) for t in range(9)]
    return jnp.concatenate(rows, axis=0).astype(BF)


def diagonal(block, count):
    empty = jnp.zeros_like(block)
    rows = [side_by_side([block if i == k else empty for k in range(count)]) for i in range(count)]
    return jnp.concatenate(rows, axis=0)


def gelu_parts(pre):
    square = pre * pre
    tangent = jnp.tanh(pre * (GELU_SCALE + (GELU_SCALE * GELU_CUBIC) * square))
    gate = 0.5 + 0.5 * tangent
    return square, gate, pre * gate


def slope_of(square, gate, value):
    return gate + value * (1.0 - gate) * (2 * GELU_SCALE + (6 * GELU_SCALE * GELU_CUBIC) * square)


def early_kernel(
    field,
    w_in,
    w_mid,
    w_out,
    taps,
    outs,
    taps_inner,
    forward_a,
    forward_b,
    forward_b0,
    twist,
    velocity,
    sent,
    early_one,
    early_two,
    first_all,
    third,
    middle_all,
    inner,
):
    x = jnp.concatenate([field[0], field[1]], axis=0)
    sent[...] = column_forward(x, forward_a, forward_b, forward_b0, twist).reshape(D, 2, 128)
    base = jnp.concatenate([velocity[0], velocity[1]], axis=0)
    shifts = [pltpu.roll(base, 1, 1), base, pltpu.roll(base, NY - 1, 1)]
    inner[...] = jnp.concatenate(shifts, axis=0).astype(BF)
    flat_in = flat_taps(w_in.ready())
    first = jnp.concatenate([dot_tn(flat_in, taps_inner[i]).astype(BF) for i in range(2)], axis=0)
    middle = diagonal(w_mid[...], 2)
    for i in range(6):
        first_all[HID * i : HID * i + HID] = dot_tn(flat_in, taps[i]).astype(BF)
    flat_out = flat_taps(w_out.ready())
    third[...] = side_by_side([dot(outs[i], flat_out).astype(BF) for i in range(6)])
    middle_all[...] = diagonal(w_mid[...], R)

    def columns(index):
        return slice(index * TILE, index * TILE + TILE)

    def layer_one(index, _):
        return dot(first, inner[:, columns(index)])

    def gelu_one(index, pre):
        low = gelu_parts(pre)[2].astype(BF)
        early_one[:, columns(index)] = low[:HID]
        return low

    def layer_two(index, low):
        return dot(middle, low)

    def gelu_two(index, pre):
        early_two[:, columns(index)] = gelu_parts(pre)[2].astype(BF)

    staggered(NY // TILE, layer_one, gelu_one, layer_two, gelu_two)


def network_kernel(
    dual_sent,
    early_one,
    early_two,
    first_all,
    third,
    middle_all,
    above,
    forward_a,
    forward_b,
    forward_b0,
    twist,
    velocity,
    sent,
    stack,
    act_one_out,
    act_two_out,
    act_one,
    act_two,
    partial,
    semaphores,
):
    sent[:, 1] = dual_sent[...]
    mine = 3 * HID
    ready = [
        pltpu.make_async_copy(early_one, act_one_out.at[mine:], semaphores.at[2, 0]),
        pltpu.make_async_copy(early_two.at[:HID], act_two_out.at[mine:], semaphores.at[2, 1]),
    ]
    for copy in ready:
        copy.start()
    held = (act_one, act_two)
    homes = (act_one_out, act_two_out)
    upper = [above[c] for c in range(CH)]
    base = jnp.concatenate([velocity[0], velocity[1], *upper], axis=0)
    stack[0:16, :] = pltpu.roll(base, 1, 1).astype(BF)
    stack[16:32, :] = base.astype(BF)
    stack[32:48, :] = pltpu.roll(base, NY - 1, 1).astype(BF)
    first, middle = first_all[:OWN], middle_all[...]

    def columns(index):
        return slice(index * TILE, index * TILE + TILE)

    def layer_one(index, _):
        return dot(first, stack[:, columns(index)])

    def gelu_one(index, pre):
        low = gelu_parts(pre)[2].astype(BF)
        act_one[:, columns(index)] = low[:mine]
        return low

    def layer_two(index, low):
        return dot(middle, low)

    def gelu_two(index, pre):
        at = columns(index)
        low = gelu_parts(pre)[2].astype(BF)
        act_two[:, at] = low[:mine]
        for k in range(2):
            pltpu.make_async_copy(
                held[k].at[:, at], homes[k].at[:mine, at], semaphores.at[k, index]
            ).start()
        return low

    def layer_three(index, low):
        at = columns(index)
        partial[:, at] = dot(third[:, :OWN], low) + dot(third[:, OWN:], early_two[:, at])

    staggered(NY // TILE, layer_one, gelu_one, layer_two, gelu_two, layer_three)
    correction = (
        pltpu.roll(partial[0:8, :], 1, 1) + partial[8:16, :] + pltpu.roll(partial[16:24, :], NY - 1, 1)
    )
    near = [jnp.concatenate([upper[c][1:], velocity[c][:3]], axis=0) for c in range(CH)]
    rows = [field[1:5] for field in near]
    pieces = []
    for c in range(CH):
        flux = near[0] * near[c]
        side = rows[1] * rows[c]
        pieces.append(
            (flux[2:] - flux[:-2]) + (pltpu.roll(side, NY - 1, 1) - pltpu.roll(side, 1, 1))
        )
    advect = 0.5 * jnp.concatenate(pieces, axis=0)
    provisional = jnp.concatenate(rows, axis=0) + STEP_SIZE * (correction - advect)
    sent[:, 0] = column_forward(provisional, forward_a, forward_b, forward_b0, twist).reshape(D, 2, 128)
    for copy in ready:
        copy.wait()
    for k in range(2):
        for index in range(NY // TILE):
            at = pl.ds(index * TILE, TILE)
            pltpu.make_async_copy(held[k].at[:, at], homes[k].at[:mine, at], semaphores.at[k, index]).wait()


def middle_kernel(
    device, got, row_forward, spin, spin_step, short_forward, short_inverse, short_rim, spin_rim, row_inverse, sent
):
    same, cross = multiplier(device[0])
    v = pair_low(dot, row_forward, side_by_side([got[:, k].reshape(256, 128) for k in range(2)]))
    plain = (spin[0], spin[1])
    step = (spin_step[0], spin_step[1])
    fields = []
    for k, (cosine, sine) in enumerate((step, plain)):
        real, imag = v[:128, 128 * k : 128 * k + 128], v[128:, 128 * k : 128 * k + 128]
        fields.append(side_by_side([real * cosine + imag * sine, imag * cosine - real * sine]))
    high, low = halves(jnp.concatenate(fields, axis=0))
    full = dot(high, short_forward[...]) + dot(low, short_forward[...])
    fields = []
    for k in range(2):
        part = full[128 * k : 128 * k + 128]
        real, imag = part[:, :128], part[:, 128:]
        real = same * real + cross * pltpu.roll(real, 64, 1)
        imag = same * imag + cross * pltpu.roll(imag, 64, 1)
        fields.append(side_by_side([real, imag]))
    high, low = halves(jnp.concatenate(fields, axis=0))
    full = dot(high, short_inverse[...]) + dot(low, short_inverse[...])
    rim = dot(high[128:], short_rim[...]) + dot(low[128:], short_rim[...])
    parts = []
    for part, (cosine, sine) in (
        (full[:128], plain),
        (full[128:], step),
        (rim, (spin_rim[0], spin_rim[1])),
    ):
        real, imag = part[:, :128], part[:, 128:]
        parts.append(jnp.concatenate([real * cosine - imag * sine, imag * cosine + real * sine], axis=0))
    out = exact(dot, row_inverse, side_by_side(parts)).astype(BF)
    for k in range(3):
        sent[:, k] = out[:, 128 * k : 128 * k + 128].reshape(D, 2, 128)


def backward_kernel(
    got,
    inverse_b,
    inverse_b0,
    untwist,
    inverse_a,
    inverse_rim,
    w_mid,
    w_out,
    duals,
    taps,
    stack,
    act_one_home,
    act_two_home,
    slope_one_home,
    slope_two_home,
    sent,
    act_one,
    act_two,
    slope_one,
    slope_two,
    dual_stack,
    sum_mid,
    sum_in,
    sum_out,
    semaphores,
):
    held = (slope_two, act_one, act_two, slope_one)
    homes = (slope_two_home, act_one_home, act_two_home, slope_one_home)
    count = NY // BACK_TILE

    def fetch(index):
        at = pl.ds(pl.multiple_of(index * BACK_TILE, BACK_TILE), BACK_TILE)
        for k in range(4):
            pltpu.make_async_copy(homes[k].at[:, at], held[k].at[:, at], semaphores.at[k, index]).start()

    fetch(0)
    both = side_by_side([got[:, 1].reshape(256, 128), got[:, 2].reshape(256, 128)])
    general = pair_low(dot, inverse_b, both)
    zero = dot(inverse_b0[...], both)
    lane = lax.broadcasted_iota(jnp.int32, general.shape, 1)
    beyond = jnp.where(lane < 128, lane % 64 - R, lane % 32 - 2)
    y = jnp.where(beyond < 0, zero, general)
    real, imag = y[:128], y[128:]
    cosine, sine = untwist[0], untwist[1]
    real, imag = real * cosine - imag * sine, imag * cosine + real * sine
    own = exact(dot_nt, inverse_a, side_by_side([real[:, :128], imag[:, :128]]))
    rim = exact(dot_nt, inverse_rim, side_by_side([real[:, 128:192], imag[:, 128:192]]))
    base = jnp.concatenate([from_blocks(own), from_blocks(rim)], axis=0)
    dual_stack[0:16, :] = pltpu.roll(base, NY - 1, 1).astype(BF)
    dual_stack[16:32, :] = base.astype(BF)
    dual_stack[32:48, :] = pltpu.roll(base, 1, 1).astype(BF)
    flat_out = flat_taps(w_out)
    spread_out = jnp.concatenate([dot_tn(flat_out, duals[i]).astype(BF) for i in range(R)], axis=0)
    middle = diagonal(w_mid[...].T, R)
    sum_mid[...] = jnp.zeros_like(sum_mid)
    sum_in[...] = jnp.zeros_like(sum_in)
    sum_out[...] = jnp.zeros_like(sum_out)

    def step(index, _):
        at = pl.ds(pl.multiple_of(index * BACK_TILE, BACK_TILE), BACK_TILE)
        @pl.when(index + 1 < count)
        def _():
            fetch(index + 1)

        def arrived(k):
            pltpu.make_async_copy(homes[k].at[:, at], held[k].at[:, at], semaphores.at[k, index]).wait()
            return held[k][:, at]

        dual = dual_stack[:, at]
        back_two = dot(spread_out, dual)
        delta_two = (back_two * arrived(0)).astype(BF)
        sum_mid[...] += dot_nt(delta_two, arrived(1))
        back_one = dot(middle, delta_two)
        sum_out[...] += dot_nt(arrived(2), dual)
        delta_one = (back_one * arrived(3)).astype(BF)
        sum_in[...] += dot_nt(delta_one, stack[:, at])
        return 0

    lax.fori_loop(0, count, step, 0, unroll=2)
    mid = sum(sum_mid[64 * i : 64 * i + 64, 64 * i : 64 * i + 64] for i in range(R))
    flips = []
    for source, choose in ((sum_in, taps), (sum_out, duals)):
        flip = jnp.zeros((18, HID), F32)
        for i in range(R):
            high, low = halves(source[64 * i : 64 * i + 64, :])
            flip = flip + (dot_nt(choose[i], high) + dot_nt(choose[i], low))
        flips.append(flip)
    packed = jnp.concatenate([side_by_side([mid[:32], mid[32:]]), side_by_side(flips)], axis=0)
    low = packed.astype(BF).reshape(25, 2, 128)
    for k in range(sent.shape[0]):
        sent[k] = low


def added(got):
    total = got[0].astype(F32)
    for k in range(1, got.shape[0]):
        total = total + got[k].astype(F32)
    return total


def partial_sum_kernel(got, sent):
    low = added(got).astype(BF)
    for k in range(sent.shape[0]):
        sent[k] = low


def total_kernel(got, grad_mid, grad_in, grad_out):
    total = added(got).reshape(50, 128)
    grad_mid[:32] = total[:32, :64]
    grad_mid[32:] = total[:32, 64:]
    for t in range(9):
        pair = total[32 + 2 * t : 34 + 2 * t]
        grad_in[t // 3, t % 3] = pair[:, :64]
        grad_out[t // 3, t % 3] = pair[:, 64:]


def field_kernel(got, inverse_b, inverse_b0, untwist, inverse_a, field):
    real, imag = column_inverse_first(got[:, 0].reshape(256, 128), inverse_b, inverse_b0, untwist)
    x = from_blocks(exact(dot_nt, inverse_a, side_by_side([real, imag])))
    field[0] = x[:R]
    field[1] = x[R:]


class Staged:
    def __init__(self, copy, ref):
        self.copy, self.ref, self.waited = copy, ref, False

    def ready(self):
        if not self.waited:
            self.copy.wait()
            self.waited = True
        return self.ref

    def __getitem__(self, index):
        return self.ready()[index]


def call(kernel, outputs, inputs, scratch=(), scalars=0, staged=0, kept=0, far=0, far_out=0):
    count = len(inputs)
    outputs = outputs if isinstance(outputs, list) else [outputs]
    spec = lambda space: pl.BlockSpec(memory_space=space)
    specs = [spec(pltpu.SMEM)] * scalars
    specs += [spec(pltpu.VMEM)] * (count - scalars - staged - far)
    specs += [spec(pltpu.HBM)] * (staged + far)
    out_specs = [spec(pltpu.VMEM)] * (len(outputs) - far_out) + [spec(pltpu.HBM)] * far_out
    out_specs += [spec(pltpu.VMEM)] * kept
    first = count - staged - far
    dropped = staged - kept

    def run(*refs):
        given = list(refs[:count])
        own = len(outputs) - kept
        targets = refs[count + own : count + own + kept]
        rest = refs[count + own + kept :]
        if staged:
            for k in range(staged):
                target = rest[len(scratch) + k] if k < dropped else targets[k - dropped]
                copy = pltpu.make_async_copy(given[first + k], target, rest[-1].at[k])
                copy.start()
                given[first + k] = Staged(copy, target)
        kernel(*given, *refs[count : count + own], *rest[: len(scratch)])
        for k in range(staged):
            given[first + k].ready()

    held = [pltpu.VMEM(x.shape, x.dtype) for x in inputs[first : first + dropped]]
    kept_out = [pltpu.VMEM(x.shape, x.dtype) for x in inputs[first + dropped : first + staged]]
    pinned = [pltpu.with_memory_space_constraint(jnp.asarray(x), pltpu.HBM) for x in inputs[first:]]
    inputs = [*inputs[:first], *pinned]
    far_first = len(outputs) - far_out
    outputs = outputs[:far_first] + [pltpu.HBM(x.shape, x.dtype) for x in outputs[far_first:]]
    outputs += kept_out
    if staged:
        held.append(pltpu.SemaphoreType.DMA((staged,)))
    result = pl.pallas_call(
        run,
        out_shape=outputs,
        in_specs=specs,
        out_specs=out_specs,
        scratch_shapes=list(scratch) + held,
        compiler_params=pltpu.CompilerParams(vmem_limit_bytes=VMEM_LIMIT),
    )(*inputs)
    return result if len(outputs) > 1 else result[0]


def slope_one_kernel(stack, first_all):
    first = jnp.concatenate([first_all[: 3 * HID], first_all[4 * HID : 5 * HID]], axis=0)
    return lambda at: slope_of(*gelu_parts(dot(first, stack[:, at])))


def slope_two_kernel(middle_all, act_one):
    middle = middle_all[...]
    return lambda at: slope_of(*gelu_parts(dot(middle, act_one[:, at])))


def prefetch(arrays, after, maker, inputs, near=()):
    count, given = len(arrays), len(inputs)

    def run(*refs):
        sources, close, refs = refs[: count + given], refs[count + given + 1 :][: len(near)], refs[count + given + 1 + len(near) :]
        targets, slope_out, refs = refs[:count], refs[count], refs[count + 1 :]
        held, slope, semaphores, out_semaphores = refs[:given], *refs[given:]
        copies = []
        for k in list(range(count, count + given)) + list(range(count)):
            target = targets[k] if k < count else held[k - count]
            copies.append(pltpu.make_async_copy(sources[k], target, semaphores.at[k]))
            copies[-1].start()
        for copy in copies[:given]:
            copy.wait()
        slopes = maker(*close, *held)
        stores = []
        for index in range(NY // TILE):
            at = slice(index * TILE, index * TILE + TILE)
            slope[:, at] = slopes(at)
            stores.append(pltpu.make_async_copy(slope.at[:, at], slope_out.at[:, at], out_semaphores.at[index]))
            stores[-1].start()
        for copy in copies[given:] + stores:
            copy.wait()

    arrays = [jnp.asarray(x) for x in [*arrays, *inputs]]
    *tables, slope = pl.pallas_call(
        run,
        out_shape=[pltpu.VMEM(x.shape, x.dtype) for x in arrays[:count]] + [pltpu.HBM((OWN, NY), F32)],
        in_specs=[pl.BlockSpec(memory_space=pltpu.HBM)] * (count + given)
        + [pl.BlockSpec(memory_space=pl.ANY)]
        + [pl.BlockSpec(memory_space=pltpu.VMEM)] * len(near),
        out_specs=[pl.BlockSpec(memory_space=pltpu.VMEM)] * count + [pl.BlockSpec(memory_space=pltpu.HBM)],
        scratch_shapes=[pltpu.VMEM(x.shape, x.dtype) for x in arrays[count:]]
        + [
            pltpu.VMEM((OWN, NY), F32),
            pltpu.SemaphoreType.DMA((count + given,)),
            pltpu.SemaphoreType.DMA((NY // TILE,)),
        ],
        compiler_params=pltpu.CompilerParams(vmem_limit_bytes=VMEM_LIMIT),
    )(*[pltpu.with_memory_space_constraint(x, pltpu.HBM) for x in arrays], after, *near)
    return tables, slope


def groups_of(mask):
    return [[i for i in range(D) if i & ~mask == j] for j in range(D) if not j & mask]


def exchange(x, groups=None):
    return lax.all_to_all(x, "rows", split_axis=0, concat_axis=0, tiled=True, axis_index_groups=groups)


def body(velocity, cotangent, w_in, w_mid, w_out):
    columns = column_tables()
    rows = row_tables()
    net = network_tables()
    scale = STEP_SIZE / math.sqrt(NX * NY)
    shape = jax.ShapeDtypeStruct
    w_in = jnp.transpose(w_in, (1, 2, 3, 0))
    device = lax.axis_index("rows").reshape(1)
    down = [(i, (i + 1) % D) for i in range(D)]
    above = lax.ppermute(velocity, "rows", down)

    forward = [columns[k] for k in ("forward_a", "forward_b", "forward_b0", "twist")]
    weights = [w_in, w_mid, w_out, net["taps"], net["outs"], net["taps_inner"]]
    dual_sent, *prepared = call(
        early_kernel,
        [
            shape((D, 2, 128), BF),
            pltpu.VMEM((HID, NY), BF),
            pltpu.VMEM((2 * HID, NY), BF),
            pltpu.VMEM((6 * HID, 48), BF),
            pltpu.VMEM((24, 6 * HID), BF),
            pltpu.VMEM((OWN, OWN), BF),
        ],
        [cotangent, *weights, *forward, velocity],
        [pltpu.VMEM((24, NY), BF)],
        staged=12,
        kept=5,
    )
    early, tables = prepared[:5], prepared[5:]
    first_all, middle_all = early[2], early[4]

    big = shape((OWN, NY), BF)
    first_sent, stack, act_one, act_two = call(
        network_kernel,
        [shape((D, 2, 2, 128), BF), pltpu.VMEM((48, NY), BF), big, big],
        [dual_sent, *early, above, *tables],
        [
            pltpu.VMEM((3 * HID, NY), BF),
            pltpu.VMEM((3 * HID, NY), BF),
            pltpu.VMEM((24, NY), F32),
            pltpu.SemaphoreType.DMA((3, NY // TILE)),
        ],
        far_out=2,
    )
    first_got = exchange(first_sent)
    names = ("row_forward", "spin", "spin_step", "short_forward", "short_inverse", "short_rim", "spin_rim")
    tables, slope_one = prefetch(
        [*[rows[k] for k in names], rows["row_inverse"]],
        first_sent,
        slope_one_kernel,
        [],
        [stack, first_all],
    )
    second_sent = call(
        middle_kernel, shape((D, 3, 2, 128), BF), [device, first_got, *tables], scalars=1
    )
    second_got = exchange(second_sent)
    back = [columns[k] for k in ("inverse_b", "inverse_b0", "untwist")]
    empty = np.zeros((2, 128, 64), np.float32)
    untwists = np.concatenate([columns["untwist"], columns["untwist_rim"], empty], axis=2)
    tables, slope_two = prefetch(
        [
            *back[:2],
            untwists,
            table_pair(columns["inverse_a"] * scale),
            table_pair(columns["inverse_rim"] * scale),
            w_mid,
            w_out,
            net["duals"],
            net["taps_step"],
        ],
        second_sent,
        slope_two_kernel,
        [act_one],
        [middle_all],
    )
    one, two = groups_of(SUM_BITS), groups_of(D - 1 - SUM_BITS)
    partial = call(
        backward_kernel,
        shape((len(one[0]), 25, 2, 128), BF),
        [second_got, *tables, stack, act_one, act_two, slope_one, slope_two],
        [
            *[pltpu.VMEM((OWN, NY), t) for t in (BF, BF, F32, F32)],
            pltpu.VMEM((48, NY), BF),
            pltpu.VMEM((OWN, OWN), F32),
            pltpu.VMEM((OWN, 48), F32),
            pltpu.VMEM((OWN, 48), F32),
            pltpu.SemaphoreType.DMA((4, NY // BACK_TILE)),
        ],
        far=4,
    )
    partial = call(partial_sum_kernel, shape((len(two[0]), 25, 2, 128), BF), [exchange(partial, one)])
    new_velocity = call(
        field_kernel,
        shape((CH, R, NY), F32),
        [second_got, *back, table_pair(columns["inverse_a"])],
        staged=4,
    )
    grad_mid, grad_in, grad_out = call(
        total_kernel,
        [shape((HID, HID), F32), shape((3, 3, 2, HID), F32), shape((3, 3, 2, HID), F32)],
        [exchange(partial, two)],
    )
    return new_velocity, jnp.transpose(grad_in, (3, 0, 1, 2)), grad_mid, grad_out


def solution(mesh):
    in_specs = (P("batch", "rows", None), P("batch", "rows", None), P(), P(), P())
    out_specs = (
        P("batch", "rows", None),
        P("batch", None, None, None),
        P("batch", None),
        P("batch", None, None, None),
    )
    return jax.shard_map(body, mesh=mesh, in_specs=in_specs, out_specs=out_specs, check_vma=False)
```

```python
import functools
import math

import jax
import jax.numpy as jnp
import ml_dtypes
import numpy as np
from jax import lax
from jax.experimental import pallas as pl
from jax.experimental.pallas import tpu as pltpu
from jax.sharding import PartitionSpec as P

STEP_SIZE = 0.5
GELU_SCALE = 0.7978845608028654
GELU_CUBIC = 0.044715
BF = jnp.bfloat16
F32 = jnp.float32
TILE = 1024
BACK_TILE = 2048
SUM_BITS = 0b0001111
VMEM_LIMIT = 32 * 1024 * 1024

R = 4
D = 128
NX = R * D
OUTER = 32
NY = OUTER * 128
C = OUTER // 2
CH = 2
HID = 64
OWN = R * HID
STEP_ROWS = (-2, -1, 0, 1)
LATE_ROWS = (-2, -1, 0, -3)
EARLY_ROWS = (1, 2)


def table_pair(matrix):
    high = np.asarray(matrix, np.float64).astype(ml_dtypes.bfloat16)
    low = (matrix - high.astype(np.float64)).astype(ml_dtypes.bfloat16)
    return np.stack([high, low])


def column_tables():
    a = np.arange(OUTER)
    b = np.arange(128)
    d = np.arange(D)
    c = np.arange(C)
    eye = np.eye(R * CH).reshape(CH, R, CH, R)
    sign = np.where(a % 2 == 0, 1.0, -1.0)
    angle = 2 * np.pi * np.outer(c, a) / OUTER
    first = np.stack([np.cos(angle), -np.sin(angle)])
    first[0, 0] = 1.0
    first[1, 0] = sign
    forward_a = np.einsum("pca,hrgs->phcrags", first, eye).reshape(256, 256)
    last = np.stack([2 * np.cos(angle), -2 * np.sin(angle)])
    last[0, 0] = 1.0
    last[1, 0] = sign
    last = last / NY
    inverse_a = np.einsum("pca,gshr->agsphcr", last, eye).reshape(256, 256)
    half = np.zeros((2, 4, CH, 2))
    for h in range(CH):
        for e in range(2):
            half[h, h * 2 + e, h, e] = 1.0
    rim = np.zeros((8, CH, 2))
    rim[:4] = np.eye(4).reshape(4, CH, 2)
    inverse_rim = np.einsum("pca,khr->akphcr", last, rim).reshape(256, 128)
    theta = 2 * np.pi * np.outer(c, b) / NY
    cosine = np.cos(theta)
    sine = np.sin(theta)
    cosine[0] = 1.0
    sine[0] = 0.0
    spread = lambda t, n: np.broadcast_to(t[None, :, None, :], (CH, C, n, 128)).reshape(-1, 128)
    twist = np.stack([spread(cosine, R), spread(sine, R)]).astype(np.float32)
    twist_rim = np.stack([spread(cosine, 2), spread(sine, 2)]).astype(np.float32)
    phi = 2 * np.pi * np.outer(d, b) / 128
    matrix = np.zeros((D, 2, 2, 128))
    matrix[:, 0, 0] = np.cos(phi)
    matrix[:, 0, 1] = np.sin(phi)
    matrix[:, 1, 0] = -np.sin(phi)
    matrix[:, 1, 1] = np.cos(phi)
    psi = 2 * np.pi * np.outer(16 + 32 * (d - 64), b) / NY
    alternate = np.where(b % 2 == 0, 1.0, -1.0)
    zero = np.zeros((D, 2, 2, 128))
    zero[:64, 0, 0] = np.cos(phi[:64])
    zero[:64, 1, 0] = -np.sin(phi[:64])
    zero[0, 1, 0] = alternate
    zero[64:, 0, 1] = np.cos(psi[64:])
    zero[64:, 1, 1] = -np.sin(psi[64:])
    back = np.zeros((2, 128, D, 2))
    back[0, :, :, 0] = np.cos(phi).T
    back[0, :, :, 1] = -np.sin(phi).T
    back[1, :, :, 0] = np.sin(phi).T
    back[1, :, :, 1] = np.cos(phi).T
    back_zero = np.zeros((2, 128, D, 2))
    back_zero[0, :, :64, 0] = 2 * np.cos(phi[:64]).T
    back_zero[0, :, :64, 1] = -2 * np.sin(phi[:64]).T
    back_zero[0, :, 0, 0] = 1.0
    back_zero[0, :, 0, 1] = alternate
    back_zero[1, :, 64:, 0] = 2 * np.cos(psi[64:]).T
    back_zero[1, :, 64:, 1] = -2 * np.sin(psi[64:]).T
    return {
        "forward_a": table_pair(forward_a),
        "forward_b": table_pair(matrix.reshape(256, 256)),
        "forward_b0": table_pair(zero.reshape(256, 256))[0],
        "twist": twist,
        "inverse_b": table_pair(back.reshape(256, 256)),
        "inverse_b0": table_pair(back_zero.reshape(256, 256))[0],
        "inverse_a": inverse_a,
        "inverse_rim": inverse_rim,
        "untwist": np.ascontiguousarray(twist.transpose(0, 2, 1)),
        "untwist_rim": np.ascontiguousarray(twist_rim.transpose(0, 2, 1)),
    }


def row_tables():
    s = np.arange(D)
    m1 = np.arange(D)
    m2 = np.arange(R)
    phi = 2 * np.pi * np.outer(m1, s) / D
    forward = np.zeros((2, D, D, 2))
    forward[0, :, :, 0] = np.cos(phi)
    forward[0, :, :, 1] = np.sin(phi)
    forward[1, :, :, 0] = -np.sin(phi)
    forward[1, :, :, 1] = np.cos(phi)
    inverse = np.zeros((D, 2, 2, D))
    inverse[:, 0, 0] = np.cos(phi).T
    inverse[:, 0, 1] = -np.sin(phi).T
    inverse[:, 1, 0] = np.sin(phi).T
    inverse[:, 1, 1] = np.cos(phi).T
    inverse = inverse / NX
    eye = np.eye(CH * C)

    def short(rows, flip):
        angle = 2 * np.pi * np.outer(m2, rows) / R
        block = np.zeros((2, R, 2, len(rows)))
        block[0, :, 0] = np.cos(angle)
        block[1, :, 0] = -np.sin(angle) * flip
        block[0, :, 1] = np.sin(angle) * flip
        block[1, :, 1] = np.cos(angle)
        block = np.round(block)
        return np.einsum("pmqr,gk->pgmqkr", block, eye).reshape(2 * CH * C * R, 2, -1)

    own = np.arange(R)
    rim = np.array([-1, R])
    rim_block = np.zeros((256, 2, 128))
    rim_block[:, :, :64] = short(rim, 1.0)

    def lanes(rows):
        theta = 2 * np.pi * np.outer(m1, rows) / NX
        both = np.stack([np.cos(theta), np.sin(theta)])
        wide = np.broadcast_to(both[:, :, None, :], (2, D, CH * C, len(rows))).reshape(2, D, -1)
        out = np.zeros((2, D, 128), np.float32)
        out[:, :, : wide.shape[2]] = wide
        return out

    return {
        "row_forward": table_pair(forward.reshape(256, 256)),
        "row_inverse": table_pair(inverse.reshape(256, 256)),
        "short_forward": short(own, -1.0).reshape(256, 256).astype(ml_dtypes.bfloat16),
        "short_inverse": short(own, 1.0).reshape(256, 256).astype(ml_dtypes.bfloat16),
        "short_rim": rim_block.reshape(256, 256).astype(ml_dtypes.bfloat16),
        "spin": lanes(own),
        "spin_step": lanes(np.array(STEP_ROWS)),
        "spin_rim": lanes(rim - 2),
    }


def velocity_row(ch, row):
    return ch * R + row if row >= 0 else 8 + ch * R + row + R


def dual_row(ch, row):
    if row in STEP_ROWS:
        return ch * R + row + 2
    return 8 + ch * 2 + (0 if row < -2 else 1)


def network_tables():
    order = (*LATE_ROWS, *EARLY_ROWS)
    taps = np.zeros((6, 18, 48))
    for at, i in enumerate(order):
        for a in range(-1, 2):
            for b in range(-1, 2):
                for ch in range(CH):
                    t = (3 * (a + 1) + b + 1) * 2 + ch
                    taps[at, t, (b + 1) * 16 + velocity_row(ch, i + a)] = 1
    outs = np.zeros((6, 24, 18))
    for at, k in enumerate(order):
        for a in range(-1, 2):
            i = k - a
            if i in STEP_ROWS:
                for b in range(-1, 2):
                    for o in range(CH):
                        outs[at, (b + 1) * 8 + o * R + i + 2, (3 * (a + 1) + b + 1) * 2 + o] = 1
    duals = np.zeros((R, 18, 48))
    for at, i in enumerate(STEP_ROWS):
        for a in range(-1, 2):
            for b in range(-1, 2):
                for o in range(CH):
                    t = (3 * (a + 1) + b + 1) * 2 + o
                    duals[at, t, (b + 1) * 16 + dual_row(o, i - a)] = 1
    low = lambda t: t.astype(ml_dtypes.bfloat16)
    inner = taps.reshape(6, 18, 3, 16)[4:, :, :, :8].reshape(2, 18, 24)
    return {
        "taps": low(taps),
        "taps_inner": low(inner),
        "taps_step": low(taps[[0, 1, 2, 4]]),
        "outs": low(outs),
        "duals": low(duals),
    }


def dot(x, y):
    return jnp.dot(x, y, preferred_element_type=F32)


def dot_nt(x, y):
    return lax.dot_general(x, y, (((1,), (1,)), ((), ())), preferred_element_type=F32)


def dot_tn(x, y):
    return lax.dot_general(x, y, (((0,), (0,)), ((), ())), preferred_element_type=F32)


def halves(x):
    high = x.astype(BF)
    return high, (x - high.astype(F32)).astype(BF)


def exact(form, pair, x):
    high, low = halves(x)
    return form(pair[0], high) + (form(pair[1], high) + form(pair[0], low))


def pair_low(form, pair, x):
    return form(pair[0], x) + form(pair[1], x)


def to_blocks(x):
    return jnp.concatenate([x[:, 128 * a : 128 * a + 128] for a in range(OUTER)], axis=0)


def from_blocks(x):
    rows = x.shape[0] // OUTER
    return jnp.concatenate([x[rows * a : rows * a + rows] for a in range(OUTER)], axis=1)


def column_forward(x, forward_a, forward_b, forward_b0, twist):
    y = exact(dot, forward_a, to_blocks(x))
    real, imag = y[:128], y[128:]
    cosine, sine = twist[0], twist[1]
    both = jnp.concatenate([real * cosine + imag * sine, imag * cosine - real * sine], axis=1)
    general = exact(dot_nt, forward_b, both)
    zero = dot_nt(forward_b0[...], both.astype(BF))
    lane = lax.broadcasted_iota(jnp.int32, general.shape, 1)
    return jnp.where(lane % 64 < R, zero, general).astype(BF)


def column_inverse_first(x, inverse_b, inverse_b0, untwist):
    general = pair_low(dot, inverse_b, x)
    zero = dot(inverse_b0[...], x)
    lane = lax.broadcasted_iota(jnp.int32, general.shape, 1)
    y = jnp.where(lane % 64 < R, zero, general)
    real, imag = y[:128], y[128:]
    cosine, sine = untwist[0], untwist[1]
    return real * cosine - imag * sine, imag * cosine + real * sine


def multiplier(device):
    m1 = lax.broadcasted_iota(jnp.int32, (128, 128), 0)
    lane = lax.broadcasted_iota(jnp.int32, (128, 128), 1)
    m = m1 + 128 * (lane % R)
    m = jnp.where(2 * m < NX, m, jnp.where(2 * m == NX, 0, m - NX))
    c = (lane % 64) // R
    n = c + OUTER * device
    n = jnp.where(2 * n < NY, n, n - NY)
    packed = jnp.where(device < 64, OUTER * device, 16 + OUTER * (device - 64))
    n = jnp.where(c == 0, packed, n)
    wave_row = m.astype(F32) * (1.0 / NX)
    wave_col = n.astype(F32) * (1.0 / NY)
    row_square = wave_row * wave_row
    col_square = wave_col * wave_col
    square = row_square + col_square
    some = square > 0
    inverse = 1.0 / jnp.where(some, square, 1.0)
    same = jnp.where(some, jnp.where(lane < 64, col_square, row_square) * inverse, 1.0)
    sign = jnp.where(lane % 2 == 0, 1.0, -1.0)
    return sign * same, -sign * (wave_row * wave_col) * inverse


def side_by_side(parts):
    return jnp.concatenate(parts, axis=1)


def staggered(count, *stages):
    values = {}
    for step in range(count + len(stages) - 1):
        for lag in reversed(range(len(stages))):
            index = step - lag
            if 0 <= index < count:
                values[index] = stages[lag](index, values.get(index))


def flat_taps(weights):
    rows = [weights[t // 3, t % 3].astype(F32) for t in range(9)]
    return jnp.concatenate(rows, axis=0).astype(BF)


def diagonal(block, count):
    empty = jnp.zeros_like(block)
    rows = [side_by_side([block if i == k else empty for k in range(count)]) for i in range(count)]
    return jnp.concatenate(rows, axis=0)


def gelu_parts(pre):
    square = pre * pre
    tangent = jnp.tanh(pre * (GELU_SCALE + (GELU_SCALE * GELU_CUBIC) * square))
    gate = 0.5 + 0.5 * tangent
    return square, gate, pre * gate


def slope_of(square, gate, value):
    return gate + value * (1.0 - gate) * (2 * GELU_SCALE + (6 * GELU_SCALE * GELU_CUBIC) * square)


def early_kernel(
    field,
    w_in,
    w_mid,
    w_out,
    taps,
    outs,
    taps_inner,
    forward_a,
    forward_b,
    forward_b0,
    twist,
    velocity,
    sent,
    early_two,
    first_all,
    third,
    middle_all,
    inner,
):
    x = jnp.concatenate([field[0], field[1]], axis=0)
    sent[...] = column_forward(x, forward_a, forward_b, forward_b0, twist).reshape(D, 2, 128)
    base = jnp.concatenate([velocity[0], velocity[1]], axis=0)
    shifts = [pltpu.roll(base, 1, 1), base, pltpu.roll(base, NY - 1, 1)]
    inner[...] = jnp.concatenate(shifts, axis=0).astype(BF)
    flat_in = flat_taps(w_in.ready())
    first = jnp.concatenate([dot_tn(flat_in, taps_inner[i]).astype(BF) for i in range(2)], axis=0)
    middle = diagonal(w_mid[...], 2)
    for i in range(6):
        first_all[HID * i : HID * i + HID] = dot_tn(flat_in, taps[i]).astype(BF)
    flat_out = flat_taps(w_out.ready())
    third[...] = side_by_side([dot(outs[i], flat_out).astype(BF) for i in range(6)])
    middle_all[...] = diagonal(w_mid[...], R)

    def columns(index):
        return slice(index * TILE, index * TILE + TILE)

    def layer_one(index, _):
        return dot(first, inner[:, columns(index)])

    def gelu_one(index, pre):
        return gelu_parts(pre)[2].astype(BF)

    def layer_two(index, low):
        return dot(middle, low)

    def gelu_two(index, pre):
        early_two[:, columns(index)] = gelu_parts(pre)[2].astype(BF)

    staggered(NY // TILE, layer_one, gelu_one, layer_two, gelu_two)


def network_kernel(
    dual_sent,
    early_two,
    first_all,
    third,
    middle_all,
    above,
    forward_a,
    forward_b,
    forward_b0,
    twist,
    velocity,
    sent,
    stack,
    partial,
):
    sent[:, 1] = dual_sent[...]
    upper = [above[c] for c in range(CH)]
    base = jnp.concatenate([velocity[0], velocity[1], *upper], axis=0)
    stack[0:16, :] = pltpu.roll(base, 1, 1).astype(BF)
    stack[16:32, :] = base.astype(BF)
    stack[32:48, :] = pltpu.roll(base, NY - 1, 1).astype(BF)
    first, middle = first_all[:OWN], middle_all[...]

    def columns(index):
        return slice(index * TILE, index * TILE + TILE)

    def layer_one(index, _):
        return dot(first, stack[:, columns(index)])

    def gelu(index, pre):
        return gelu_parts(pre)[2].astype(BF)

    def layer_two(index, low):
        return dot(middle, low)

    def layer_three(index, low):
        at = columns(index)
        partial[:, at] = dot(third[:, :OWN], low) + dot(third[:, OWN:], early_two[:, at])

    staggered(NY // TILE, layer_one, gelu, layer_two, gelu, layer_three)
    correction = (
        pltpu.roll(partial[0:8, :], 1, 1) + partial[8:16, :] + pltpu.roll(partial[16:24, :], NY - 1, 1)
    )
    near = [jnp.concatenate([upper[c][1:], velocity[c][:3]], axis=0) for c in range(CH)]
    rows = [field[1:5] for field in near]
    pieces = []
    for c in range(CH):
        flux = near[0] * near[c]
        side = rows[1] * rows[c]
        pieces.append(
            (flux[2:] - flux[:-2]) + (pltpu.roll(side, NY - 1, 1) - pltpu.roll(side, 1, 1))
        )
    advect = 0.5 * jnp.concatenate(pieces, axis=0)
    provisional = jnp.concatenate(rows, axis=0) + STEP_SIZE * (correction - advect)
    sent[:, 0] = column_forward(provisional, forward_a, forward_b, forward_b0, twist).reshape(D, 2, 128)


def middle_kernel(
    device, got, row_forward, spin, spin_step, short_forward, short_inverse, short_rim, spin_rim, row_inverse, sent
):
    same, cross = multiplier(device[0])
    v = pair_low(dot, row_forward, side_by_side([got[:, k].reshape(256, 128) for k in range(2)]))
    plain = (spin[0], spin[1])
    step = (spin_step[0], spin_step[1])
    fields = []
    for k, (cosine, sine) in enumerate((step, plain)):
        real, imag = v[:128, 128 * k : 128 * k + 128], v[128:, 128 * k : 128 * k + 128]
        fields.append(side_by_side([real * cosine + imag * sine, imag * cosine - real * sine]))
    high, low = halves(jnp.concatenate(fields, axis=0))
    full = dot(high, short_forward[...]) + dot(low, short_forward[...])
    fields = []
    for k in range(2):
        part = full[128 * k : 128 * k + 128]
        real, imag = part[:, :128], part[:, 128:]
        real = same * real + cross * pltpu.roll(real, 64, 1)
        imag = same * imag + cross * pltpu.roll(imag, 64, 1)
        fields.append(side_by_side([real, imag]))
    high, low = halves(jnp.concatenate(fields, axis=0))
    full = dot(high, short_inverse[...]) + dot(low, short_inverse[...])
    rim = dot(high[128:], short_rim[...]) + dot(low[128:], short_rim[...])
    parts = []
    for part, (cosine, sine) in (
        (full[:128], plain),
        (full[128:], step),
        (rim, (spin_rim[0], spin_rim[1])),
    ):
        real, imag = part[:, :128], part[:, 128:]
        parts.append(jnp.concatenate([real * cosine - imag * sine, imag * cosine + real * sine], axis=0))
    out = exact(dot, row_inverse, side_by_side(parts)).astype(BF)
    for k in range(3):
        sent[:, k] = out[:, 128 * k : 128 * k + 128].reshape(D, 2, 128)


def backward_kernel(
    got,
    inverse_b,
    inverse_b0,
    untwist,
    inverse_a,
    inverse_rim,
    w_mid,
    w_out,
    duals,
    taps,
    stack,
    act_one_home,
    act_two_home,
    slope_one_home,
    slope_two_home,
    sent,
    act_one,
    act_two,
    slope_one,
    slope_two,
    dual_stack,
    sum_mid,
    sum_in,
    sum_out,
    semaphores,
):
    held = (slope_two, act_one, act_two, slope_one)
    homes = (slope_two_home, act_one_home, act_two_home, slope_one_home)
    count = NY // BACK_TILE

    def fetch(index):
        at = pl.ds(pl.multiple_of(index * BACK_TILE, BACK_TILE), BACK_TILE)
        for k in range(4):
            pltpu.make_async_copy(homes[k].at[:, at], held[k].at[:, at], semaphores.at[k, index]).start()

    fetch(0)
    both = side_by_side([got[:, 1].reshape(256, 128), got[:, 2].reshape(256, 128)])
    general = pair_low(dot, inverse_b, both)
    zero = dot(inverse_b0[...], both)
    lane = lax.broadcasted_iota(jnp.int32, general.shape, 1)
    beyond = jnp.where(lane < 128, lane % 64 - R, lane % 32 - 2)
    y = jnp.where(beyond < 0, zero, general)
    real, imag = y[:128], y[128:]
    cosine, sine = untwist[0], untwist[1]
    real, imag = real * cosine - imag * sine, imag * cosine + real * sine
    own = exact(dot_nt, inverse_a, side_by_side([real[:, :128], imag[:, :128]]))
    rim = exact(dot_nt, inverse_rim, side_by_side([real[:, 128:192], imag[:, 128:192]]))
    base = jnp.concatenate([from_blocks(own), from_blocks(rim)], axis=0)
    dual_stack[0:16, :] = pltpu.roll(base, NY - 1, 1).astype(BF)
    dual_stack[16:32, :] = base.astype(BF)
    dual_stack[32:48, :] = pltpu.roll(base, 1, 1).astype(BF)
    flat_out = flat_taps(w_out)
    spread_out = jnp.concatenate([dot_tn(flat_out, duals[i]).astype(BF) for i in range(R)], axis=0)
    middle = diagonal(w_mid[...].T, R)
    sum_mid[...] = jnp.zeros_like(sum_mid)
    sum_in[...] = jnp.zeros_like(sum_in)
    sum_out[...] = jnp.zeros_like(sum_out)

    def step(index, _):
        at = pl.ds(pl.multiple_of(index * BACK_TILE, BACK_TILE), BACK_TILE)
        @pl.when(index + 1 < count)
        def _():
            fetch(index + 1)

        def arrived(k):
            pltpu.make_async_copy(homes[k].at[:, at], held[k].at[:, at], semaphores.at[k, index]).wait()
            return held[k][:, at]

        dual = dual_stack[:, at]
        back_two = dot(spread_out, dual)
        delta_two = (back_two * arrived(0)).astype(BF)
        sum_mid[...] += dot_nt(delta_two, arrived(1))
        back_one = dot(middle, delta_two)
        sum_out[...] += dot_nt(arrived(2), dual)
        delta_one = (back_one * arrived(3)).astype(BF)
        sum_in[...] += dot_nt(delta_one, stack[:, at])
        return 0

    lax.fori_loop(0, count, step, 0, unroll=2)
    mid = sum(sum_mid[64 * i : 64 * i + 64, 64 * i : 64 * i + 64] for i in range(R))
    flips = []
    for source, choose in ((sum_in, taps), (sum_out, duals)):
        flip = jnp.zeros((18, HID), F32)
        for i in range(R):
            high, low = halves(source[64 * i : 64 * i + 64, :])
            flip = flip + (dot_nt(choose[i], high) + dot_nt(choose[i], low))
        flips.append(flip)
    packed = jnp.concatenate([side_by_side([mid[:32], mid[32:]]), side_by_side(flips)], axis=0)
    low = packed.astype(BF).reshape(25, 2, 128)
    for k in range(sent.shape[0]):
        sent[k] = low


def added(got):
    total = got[0].astype(F32)
    for k in range(1, got.shape[0]):
        total = total + got[k].astype(F32)
    return total


def partial_sum_kernel(got, sent):
    low = added(got).astype(BF)
    for k in range(sent.shape[0]):
        sent[k] = low


def total_kernel(got, grad_mid, grad_in, grad_out):
    total = added(got).reshape(50, 128)
    grad_mid[:32] = total[:32, :64]
    grad_mid[32:] = total[:32, 64:]
    for t in range(9):
        pair = total[32 + 2 * t : 34 + 2 * t]
        grad_in[t // 3, t % 3] = pair[:, :64]
        grad_out[t // 3, t % 3] = pair[:, 64:]


def field_kernel(got, inverse_b, inverse_b0, untwist, inverse_a, field):
    real, imag = column_inverse_first(got[:, 0].reshape(256, 128), inverse_b, inverse_b0, untwist)
    x = from_blocks(exact(dot_nt, inverse_a, side_by_side([real, imag])))
    field[0] = x[:R]
    field[1] = x[R:]


class Staged:
    def __init__(self, copy, ref):
        self.copy, self.ref, self.waited = copy, ref, False

    def ready(self):
        if not self.waited:
            self.copy.wait()
            self.waited = True
        return self.ref

    def __getitem__(self, index):
        return self.ready()[index]


def call(kernel, outputs, inputs, scratch=(), scalars=0, staged=0, kept=0, far=0, far_out=0):
    count = len(inputs)
    outputs = outputs if isinstance(outputs, list) else [outputs]
    spec = lambda space: pl.BlockSpec(memory_space=space)
    specs = [spec(pltpu.SMEM)] * scalars
    specs += [spec(pltpu.VMEM)] * (count - scalars - staged - far)
    specs += [spec(pltpu.HBM)] * (staged + far)
    out_specs = [spec(pltpu.VMEM)] * (len(outputs) - far_out) + [spec(pltpu.HBM)] * far_out
    out_specs += [spec(pltpu.VMEM)] * kept
    first = count - staged - far
    dropped = staged - kept

    def run(*refs):
        given = list(refs[:count])
        own = len(outputs) - kept
        targets = refs[count + own : count + own + kept]
        rest = refs[count + own + kept :]
        if staged:
            for k in range(staged):
                target = rest[len(scratch) + k] if k < dropped else targets[k - dropped]
                copy = pltpu.make_async_copy(given[first + k], target, rest[-1].at[k])
                copy.start()
                given[first + k] = Staged(copy, target)
        kernel(*given, *refs[count : count + own], *rest[: len(scratch)])
        for k in range(staged):
            given[first + k].ready()

    held = [pltpu.VMEM(x.shape, x.dtype) for x in inputs[first : first + dropped]]
    kept_out = [pltpu.VMEM(x.shape, x.dtype) for x in inputs[first + dropped : first + staged]]
    pinned = [pltpu.with_memory_space_constraint(jnp.asarray(x), pltpu.HBM) for x in inputs[first:]]
    inputs = [*inputs[:first], *pinned]
    far_first = len(outputs) - far_out
    outputs = outputs[:far_first] + [pltpu.HBM(x.shape, x.dtype) for x in outputs[far_first:]]
    outputs += kept_out
    if staged:
        held.append(pltpu.SemaphoreType.DMA((staged,)))
    result = pl.pallas_call(
        run,
        out_shape=outputs,
        in_specs=specs,
        out_specs=out_specs,
        scratch_shapes=list(scratch) + held,
        compiler_params=pltpu.CompilerParams(vmem_limit_bytes=VMEM_LIMIT),
    )(*inputs)
    return result if len(outputs) > 1 else result[0]


def layer_one_kernel(stack, first_all):
    first = jnp.concatenate([first_all[: 3 * HID], first_all[4 * HID : 5 * HID]], axis=0)
    return lambda at: dot(first, stack[:, at])


def layer_two_kernel(middle_all, act_one):
    middle = middle_all[...]
    return lambda at: dot(middle, act_one[:, at])


def prefetch(arrays, after, maker, near, wide=()):
    count, given, tiles = len(arrays), len(wide), NY // TILE

    def run(*refs):
        sources, refs = refs[: count + given], refs[count + given + 1 :]
        close, refs = refs[: len(near)], refs[len(near) :]
        targets, homes, refs = refs[:count], refs[count : count + 2], refs[count + 2 :]
        held, results, refs = refs[:given], refs[given : given + 2], refs[given + 2 :]
        semaphores, in_semaphores, out_semaphores = refs
        columns = [slice(index * TILE, index * TILE + TILE) for index in range(tiles)]
        pieces = [
            [
                pltpu.make_async_copy(sources[count + k].at[:, at], held[k].at[:, at], in_semaphores.at[k, index])
                for k in range(given)
            ]
            for index, at in enumerate(columns)
        ]
        copies = [pltpu.make_async_copy(sources[k], targets[k], semaphores.at[k]) for k in range(count)]
        for copy in sum(pieces, []) + copies:
            copy.start()
        layer = maker(*close, *held)
        for index, at in enumerate(columns):
            for copy in pieces[index]:
                copy.wait()
            square, gate, value = gelu_parts(layer(at))
            results[0][:, at] = value.astype(BF)
            results[1][:, at] = slope_of(square, gate, value)
            for k in range(2):
                copies.append(
                    pltpu.make_async_copy(results[k].at[:, at], homes[k].at[:, at], out_semaphores.at[k, index])
                )
                copies[-1].start()
        for copy in copies:
            copy.wait()

    arrays = [jnp.asarray(x) for x in [*arrays, *wide]]
    *tables, act, slope = pl.pallas_call(
        run,
        out_shape=[pltpu.VMEM(x.shape, x.dtype) for x in arrays[:count]]
        + [pltpu.HBM((OWN, NY), BF), pltpu.HBM((OWN, NY), F32)],
        in_specs=[pl.BlockSpec(memory_space=pltpu.HBM)] * (count + given)
        + [pl.BlockSpec(memory_space=pl.ANY)]
        + [pl.BlockSpec(memory_space=pltpu.VMEM)] * len(near),
        out_specs=[pl.BlockSpec(memory_space=pltpu.VMEM)] * count + [pl.BlockSpec(memory_space=pltpu.HBM)] * 2,
        scratch_shapes=[pltpu.VMEM(x.shape, x.dtype) for x in arrays[count:]]
        + [
            pltpu.VMEM((OWN, NY), BF),
            pltpu.VMEM((OWN, NY), F32),
            pltpu.SemaphoreType.DMA((count,)),
            pltpu.SemaphoreType.DMA((max(given, 1), tiles)),
            pltpu.SemaphoreType.DMA((2, tiles)),
        ],
        compiler_params=pltpu.CompilerParams(vmem_limit_bytes=VMEM_LIMIT),
    )(*[pltpu.with_memory_space_constraint(x, pltpu.HBM) for x in arrays], after, *near)
    return tables, act, slope


def groups_of(mask):
    return [[i for i in range(D) if i & ~mask == j] for j in range(D) if not j & mask]


def exchange(x, groups=None):
    return lax.all_to_all(x, "rows", split_axis=0, concat_axis=0, tiled=True, axis_index_groups=groups)


def body(velocity, cotangent, w_in, w_mid, w_out):
    columns = column_tables()
    rows = row_tables()
    net = network_tables()
    scale = STEP_SIZE / math.sqrt(NX * NY)
    shape = jax.ShapeDtypeStruct
    w_in = jnp.transpose(w_in, (1, 2, 3, 0))
    device = lax.axis_index("rows").reshape(1)
    down = [(i, (i + 1) % D) for i in range(D)]
    above = lax.ppermute(velocity, "rows", down)

    forward = [columns[k] for k in ("forward_a", "forward_b", "forward_b0", "twist")]
    weights = [w_in, w_mid, w_out, net["taps"], net["outs"], net["taps_inner"]]
    dual_sent, *prepared = call(
        early_kernel,
        [
            shape((D, 2, 128), BF),
            pltpu.VMEM((2 * HID, NY), BF),
            pltpu.VMEM((6 * HID, 48), BF),
            pltpu.VMEM((24, 6 * HID), BF),
            pltpu.VMEM((OWN, OWN), BF),
        ],
        [cotangent, *weights, *forward, velocity],
        [pltpu.VMEM((24, NY), BF)],
        staged=12,
        kept=5,
    )
    early, tables = prepared[:4], prepared[4:]
    first_all, middle_all = early[1], early[3]

    first_sent, stack = call(
        network_kernel,
        [shape((D, 2, 2, 128), BF), pltpu.VMEM((48, NY), BF)],
        [dual_sent, *early, above, *tables],
        [pltpu.VMEM((24, NY), F32)],
    )
    first_got = exchange(first_sent)
    names = ("row_forward", "spin", "spin_step", "short_forward", "short_inverse", "short_rim", "spin_rim")
    tables, act_one, slope_one = prefetch(
        [*[rows[k] for k in names], rows["row_inverse"]],
        first_sent,
        layer_one_kernel,
        [stack, first_all],
    )
    second_sent = call(
        middle_kernel, shape((D, 3, 2, 128), BF), [device, first_got, *tables], scalars=1
    )
    second_got = exchange(second_sent)
    back = [columns[k] for k in ("inverse_b", "inverse_b0", "untwist")]
    empty = np.zeros((2, 128, 64), np.float32)
    untwists = np.concatenate([columns["untwist"], columns["untwist_rim"], empty], axis=2)
    tables, act_two, slope_two = prefetch(
        [
            *back[:2],
            untwists,
            table_pair(columns["inverse_a"] * scale),
            table_pair(columns["inverse_rim"] * scale),
            w_mid,
            w_out,
            net["duals"],
            net["taps_step"],
        ],
        second_sent,
        layer_two_kernel,
        [middle_all],
        [act_one],
    )
    one, two = groups_of(SUM_BITS), groups_of(D - 1 - SUM_BITS)
    partial = call(
        backward_kernel,
        shape((len(one[0]), 25, 2, 128), BF),
        [second_got, *tables, stack, act_one, act_two, slope_one, slope_two],
        [
            *[pltpu.VMEM((OWN, NY), t) for t in (BF, BF, F32, F32)],
            pltpu.VMEM((48, NY), BF),
            pltpu.VMEM((OWN, OWN), F32),
            pltpu.VMEM((OWN, 48), F32),
            pltpu.VMEM((OWN, 48), F32),
            pltpu.SemaphoreType.DMA((4, NY // BACK_TILE)),
        ],
        far=4,
    )
    partial = call(partial_sum_kernel, shape((len(two[0]), 25, 2, 128), BF), [exchange(partial, one)])
    new_velocity = call(
        field_kernel,
        shape((CH, R, NY), F32),
        [second_got, *back, table_pair(columns["inverse_a"])],
        staged=4,
    )
    grad_mid, grad_in, grad_out = call(
        total_kernel,
        [shape((HID, HID), F32), shape((3, 3, 2, HID), F32), shape((3, 3, 2, HID), F32)],
        [exchange(partial, two)],
    )
    return new_velocity, jnp.transpose(grad_in, (3, 0, 1, 2)), grad_mid, grad_out


def solution(mesh):
    in_specs = (P("batch", "rows", None), P("batch", "rows", None), P(), P(), P())
    out_specs = (
        P("batch", "rows", None),
        P("batch", None, None, None),
        P("batch", None),
        P("batch", None, None, None),
    )
    return jax.shard_map(body, mesh=mesh, in_specs=in_specs, out_specs=out_specs, check_vma=False)
```

```python
import functools
import math

import jax
import jax.numpy as jnp
import ml_dtypes
import numpy as np
from jax import lax
from jax.experimental import pallas as pl
from jax.experimental.pallas import tpu as pltpu
from jax.sharding import PartitionSpec as P

STEP_SIZE = 0.5
GELU_SCALE = 0.7978845608028654
GELU_CUBIC = 0.044715
BF = jnp.bfloat16
F32 = jnp.float32
TILE = 1024
BACK_TILE = 2048
SUM_BITS = 0b0001111
VMEM_LIMIT = 32 * 1024 * 1024

R = 4
D = 128
NX = R * D
OUTER = 32
NY = OUTER * 128
C = OUTER // 2
CH = 2
HID = 64
OWN = R * HID
STEP_ROWS = (-2, -1, 0, 1)
LATE_ROWS = (-2, -1, 0, -3)
EARLY_ROWS = (1, 2)


def table_pair(matrix):
    high = np.asarray(matrix, np.float64).astype(ml_dtypes.bfloat16)
    low = (matrix - high.astype(np.float64)).astype(ml_dtypes.bfloat16)
    return np.stack([high, low])


def column_tables():
    a = np.arange(OUTER)
    b = np.arange(128)
    d = np.arange(D)
    c = np.arange(C)
    eye = np.eye(R * CH).reshape(CH, R, CH, R)
    sign = np.where(a % 2 == 0, 1.0, -1.0)
    angle = 2 * np.pi * np.outer(c, a) / OUTER
    first = np.stack([np.cos(angle), -np.sin(angle)])
    first[0, 0] = 1.0
    first[1, 0] = sign
    forward_a = np.einsum("pca,hrgs->phcrags", first, eye).reshape(256, 256)
    last = np.stack([2 * np.cos(angle), -2 * np.sin(angle)])
    last[0, 0] = 1.0
    last[1, 0] = sign
    last = last / NY
    inverse_a = np.einsum("pca,gshr->agsphcr", last, eye).reshape(256, 256)
    half = np.zeros((2, 4, CH, 2))
    for h in range(CH):
        for e in range(2):
            half[h, h * 2 + e, h, e] = 1.0
    rim = np.zeros((8, CH, 2))
    rim[:4] = np.eye(4).reshape(4, CH, 2)
    inverse_rim = np.einsum("pca,khr->akphcr", last, rim).reshape(256, 128)
    theta = 2 * np.pi * np.outer(c, b) / NY
    cosine = np.cos(theta)
    sine = np.sin(theta)
    cosine[0] = 1.0
    sine[0] = 0.0
    spread = lambda t, n: np.broadcast_to(t[None, :, None, :], (CH, C, n, 128)).reshape(-1, 128)
    twist = np.stack([spread(cosine, R), spread(sine, R)]).astype(np.float32)
    twist_rim = np.stack([spread(cosine, 2), spread(sine, 2)]).astype(np.float32)
    phi = 2 * np.pi * np.outer(d, b) / 128
    matrix = np.zeros((D, 2, 2, 128))
    matrix[:, 0, 0] = np.cos(phi)
    matrix[:, 0, 1] = np.sin(phi)
    matrix[:, 1, 0] = -np.sin(phi)
    matrix[:, 1, 1] = np.cos(phi)
    psi = 2 * np.pi * np.outer(16 + 32 * (d - 64), b) / NY
    alternate = np.where(b % 2 == 0, 1.0, -1.0)
    zero = np.zeros((D, 2, 2, 128))
    zero[:64, 0, 0] = np.cos(phi[:64])
    zero[:64, 1, 0] = -np.sin(phi[:64])
    zero[0, 1, 0] = alternate
    zero[64:, 0, 1] = np.cos(psi[64:])
    zero[64:, 1, 1] = -np.sin(psi[64:])
    back = np.zeros((2, 128, D, 2))
    back[0, :, :, 0] = np.cos(phi).T
    back[0, :, :, 1] = -np.sin(phi).T
    back[1, :, :, 0] = np.sin(phi).T
    back[1, :, :, 1] = np.cos(phi).T
    back_zero = np.zeros((2, 128, D, 2))
    back_zero[0, :, :64, 0] = 2 * np.cos(phi[:64]).T
    back_zero[0, :, :64, 1] = -2 * np.sin(phi[:64]).T
    back_zero[0, :, 0, 0] = 1.0
    back_zero[0, :, 0, 1] = alternate
    back_zero[1, :, 64:, 0] = 2 * np.cos(psi[64:]).T
    back_zero[1, :, 64:, 1] = -2 * np.sin(psi[64:]).T
    return {
        "forward_a": table_pair(forward_a),
        "forward_b": table_pair(matrix.reshape(256, 256)),
        "forward_b0": table_pair(zero.reshape(256, 256))[0],
        "twist": twist,
        "inverse_b": table_pair(back.reshape(256, 256)),
        "inverse_b0": table_pair(back_zero.reshape(256, 256))[0],
        "inverse_a": inverse_a,
        "inverse_rim": inverse_rim,
        "untwist": np.ascontiguousarray(twist.transpose(0, 2, 1)),
        "untwist_rim": np.ascontiguousarray(twist_rim.transpose(0, 2, 1)),
    }


def row_tables():
    s = np.arange(D)
    m1 = np.arange(D)
    m2 = np.arange(R)
    phi = 2 * np.pi * np.outer(m1, s) / D
    forward = np.zeros((2, D, D, 2))
    forward[0, :, :, 0] = np.cos(phi)
    forward[0, :, :, 1] = np.sin(phi)
    forward[1, :, :, 0] = -np.sin(phi)
    forward[1, :, :, 1] = np.cos(phi)
    inverse = np.zeros((D, 2, 2, D))
    inverse[:, 0, 0] = np.cos(phi).T
    inverse[:, 0, 1] = -np.sin(phi).T
    inverse[:, 1, 0] = np.sin(phi).T
    inverse[:, 1, 1] = np.cos(phi).T
    inverse = inverse / NX
    eye = np.eye(CH * C)

    def short(rows, flip):
        angle = 2 * np.pi * np.outer(m2, rows) / R
        block = np.zeros((2, R, 2, len(rows)))
        block[0, :, 0] = np.cos(angle)
        block[1, :, 0] = -np.sin(angle) * flip
        block[0, :, 1] = np.sin(angle) * flip
        block[1, :, 1] = np.cos(angle)
        block = np.round(block)
        return np.einsum("pmqr,gk->pgmqkr", block, eye).reshape(2 * CH * C * R, 2, -1)

    own = np.arange(R)
    rim = np.array([-1, R])
    rim_block = np.zeros((256, 2, 128))
    rim_block[:, :, :64] = short(rim, 1.0)

    def lanes(rows):
        theta = 2 * np.pi * np.outer(m1, rows) / NX
        both = np.stack([np.cos(theta), np.sin(theta)])
        wide = np.broadcast_to(both[:, :, None, :], (2, D, CH * C, len(rows))).reshape(2, D, -1)
        out = np.zeros((2, D, 128), np.float32)
        out[:, :, : wide.shape[2]] = wide
        return out

    return {
        "row_forward": table_pair(forward.reshape(256, 256)),
        "row_inverse": table_pair(inverse.reshape(256, 256)),
        "short_forward": short(own, -1.0).reshape(256, 256).astype(ml_dtypes.bfloat16),
        "short_inverse": short(own, 1.0).reshape(256, 256).astype(ml_dtypes.bfloat16),
        "short_rim": rim_block.reshape(256, 256).astype(ml_dtypes.bfloat16),
        "spin": lanes(own),
        "spin_step": lanes(np.array(STEP_ROWS)),
        "spin_rim": lanes(rim - 2),
    }


def velocity_row(ch, row):
    return ch * R + row if row >= 0 else 8 + ch * R + row + R


def dual_row(ch, row):
    if row in STEP_ROWS:
        return ch * R + row + 2
    return 8 + ch * 2 + (0 if row < -2 else 1)


def network_tables():
    order = (*LATE_ROWS, *EARLY_ROWS)
    taps = np.zeros((6, 18, 48))
    for at, i in enumerate(order):
        for a in range(-1, 2):
            for b in range(-1, 2):
                for ch in range(CH):
                    t = (3 * (a + 1) + b + 1) * 2 + ch
                    taps[at, t, (b + 1) * 16 + velocity_row(ch, i + a)] = 1
    outs = np.zeros((6, 24, 18))
    for at, k in enumerate(order):
        for a in range(-1, 2):
            i = k - a
            if i in STEP_ROWS:
                for b in range(-1, 2):
                    for o in range(CH):
                        outs[at, (b + 1) * 8 + o * R + i + 2, (3 * (a + 1) + b + 1) * 2 + o] = 1
    duals = np.zeros((R, 18, 48))
    for at, i in enumerate(STEP_ROWS):
        for a in range(-1, 2):
            for b in range(-1, 2):
                for o in range(CH):
                    t = (3 * (a + 1) + b + 1) * 2 + o
                    duals[at, t, (b + 1) * 16 + dual_row(o, i - a)] = 1
    low = lambda t: t.astype(ml_dtypes.bfloat16)
    inner = taps.reshape(6, 18, 3, 16)[4:, :, :, :8].reshape(2, 18, 24)
    return {
        "taps": low(taps),
        "taps_inner": low(inner),
        "taps_step": low(taps[[0, 1, 2, 4]]),
        "outs": low(outs),
        "duals": low(duals),
    }


def dot(x, y):
    return jnp.dot(x, y, preferred_element_type=F32)


def dot_nt(x, y):
    return lax.dot_general(x, y, (((1,), (1,)), ((), ())), preferred_element_type=F32)


def dot_tn(x, y):
    return lax.dot_general(x, y, (((0,), (0,)), ((), ())), preferred_element_type=F32)


def halves(x):
    high = x.astype(BF)
    return high, (x - high.astype(F32)).astype(BF)


def exact(form, pair, x):
    high, low = halves(x)
    return form(pair[0], high) + (form(pair[1], high) + form(pair[0], low))


def pair_low(form, pair, x):
    low = x.astype(BF)
    return form(pair[0], low) + form(pair[1], low)


def to_blocks(x):
    return jnp.concatenate([x[:, 128 * a : 128 * a + 128] for a in range(OUTER)], axis=0)


def from_blocks(x):
    rows = x.shape[0] // OUTER
    return jnp.concatenate([x[rows * a : rows * a + rows] for a in range(OUTER)], axis=1)


def column_forward(x, forward_a, forward_b, forward_b0, twist, product):
    y = product(dot, forward_a, to_blocks(x))
    real, imag = y[:128], y[128:]
    cosine, sine = twist[0], twist[1]
    both = jnp.concatenate([real * cosine + imag * sine, imag * cosine - real * sine], axis=1)
    general = product(dot_nt, forward_b, both)
    zero = dot_nt(forward_b0[...], both.astype(BF))
    lane = lax.broadcasted_iota(jnp.int32, general.shape, 1)
    return jnp.where(lane % 64 < R, zero, general).astype(BF)


def column_inverse_first(x, inverse_b, inverse_b0, untwist):
    general = pair_low(dot, inverse_b, x)
    zero = dot(inverse_b0[...], x)
    lane = lax.broadcasted_iota(jnp.int32, general.shape, 1)
    y = jnp.where(lane % 64 < R, zero, general)
    real, imag = y[:128], y[128:]
    cosine, sine = untwist[0], untwist[1]
    return real * cosine - imag * sine, imag * cosine + real * sine


def multiplier(device):
    m1 = lax.broadcasted_iota(jnp.int32, (128, 128), 0)
    lane = lax.broadcasted_iota(jnp.int32, (128, 128), 1)
    m = m1 + 128 * (lane % R)
    m = jnp.where(2 * m < NX, m, jnp.where(2 * m == NX, 0, m - NX))
    c = (lane % 64) // R
    n = c + OUTER * device
    n = jnp.where(2 * n < NY, n, n - NY)
    packed = jnp.where(device < 64, OUTER * device, 16 + OUTER * (device - 64))
    n = jnp.where(c == 0, packed, n)
    wave_row = m.astype(F32) * (1.0 / NX)
    wave_col = n.astype(F32) * (1.0 / NY)
    row_square = wave_row * wave_row
    col_square = wave_col * wave_col
    square = row_square + col_square
    some = square > 0
    inverse = 1.0 / jnp.where(some, square, 1.0)
    same = jnp.where(some, jnp.where(lane < 64, col_square, row_square) * inverse, 1.0)
    sign = jnp.where(lane % 2 == 0, 1.0, -1.0)
    return sign * same, -sign * (wave_row * wave_col) * inverse


def side_by_side(parts):
    return jnp.concatenate(parts, axis=1)


def staggered(count, *stages):
    values = {}
    for step in range(count + len(stages) - 1):
        for lag in reversed(range(len(stages))):
            index = step - lag
            if 0 <= index < count:
                values[index] = stages[lag](index, values.get(index))


def flat_taps(weights):
    rows = [weights[t // 3, t % 3].astype(F32) for t in range(9)]
    return jnp.concatenate(rows, axis=0).astype(BF)


def diagonal(block, count):
    empty = jnp.zeros_like(block)
    rows = [side_by_side([block if i == k else empty for k in range(count)]) for i in range(count)]
    return jnp.concatenate(rows, axis=0)


def gelu_parts(pre):
    square = pre * pre
    tangent = jnp.tanh(pre * (GELU_SCALE + (GELU_SCALE * GELU_CUBIC) * square))
    gate = 0.5 + 0.5 * tangent
    return square, gate, pre * gate


def slope_of(square, gate, value):
    return gate + value * (1.0 - gate) * (2 * GELU_SCALE + (6 * GELU_SCALE * GELU_CUBIC) * square)


def early_kernel(
    field,
    w_in,
    w_mid,
    w_out,
    taps,
    outs,
    taps_inner,
    forward_a,
    forward_b,
    forward_b0,
    twist,
    velocity,
    sent,
    early_two,
    first_all,
    third,
    middle_all,
    inner,
):
    x = jnp.concatenate([field[0], field[1]], axis=0)
    sent[...] = column_forward(x, forward_a, forward_b, forward_b0, twist, exact).reshape(D, 2, 128)
    base = jnp.concatenate([velocity[0], velocity[1]], axis=0)
    shifts = [pltpu.roll(base, 1, 1), base, pltpu.roll(base, NY - 1, 1)]
    inner[...] = jnp.concatenate(shifts, axis=0).astype(BF)
    flat_in = flat_taps(w_in.ready())
    first = jnp.concatenate([dot_tn(flat_in, taps_inner[i]).astype(BF) for i in range(2)], axis=0)
    middle = diagonal(w_mid[...], 2)
    for i in range(6):
        first_all[HID * i : HID * i + HID] = dot_tn(flat_in, taps[i]).astype(BF)
    flat_out = flat_taps(w_out.ready())
    third[...] = side_by_side([dot(outs[i], flat_out).astype(BF) for i in range(6)])
    middle_all[...] = diagonal(w_mid[...], R)

    def columns(index):
        return slice(index * TILE, index * TILE + TILE)

    def layer_one(index, _):
        return dot(first, inner[:, columns(index)])

    def gelu_one(index, pre):
        return gelu_parts(pre)[2].astype(BF)

    def layer_two(index, low):
        return dot(middle, low)

    def gelu_two(index, pre):
        early_two[:, columns(index)] = gelu_parts(pre)[2].astype(BF)

    staggered(NY // TILE, layer_one, gelu_one, layer_two, gelu_two)


def network_kernel(
    dual_sent,
    early_two,
    first_all,
    third,
    middle_all,
    above,
    forward_a,
    forward_b,
    forward_b0,
    twist,
    velocity,
    sent,
    stack,
    partial,
):
    sent[:, 1] = dual_sent[...]
    upper = [above[c] for c in range(CH)]
    base = jnp.concatenate([velocity[0], velocity[1], *upper], axis=0)
    stack[0:16, :] = pltpu.roll(base, 1, 1).astype(BF)
    stack[16:32, :] = base.astype(BF)
    stack[32:48, :] = pltpu.roll(base, NY - 1, 1).astype(BF)
    first, middle = first_all[:OWN], middle_all[...]

    def columns(index):
        return slice(index * TILE, index * TILE + TILE)

    def layer_one(index, _):
        return dot(first, stack[:, columns(index)])

    def gelu(index, pre):
        return gelu_parts(pre)[2].astype(BF)

    def layer_two(index, low):
        return dot(middle, low)

    def layer_three(index, low):
        at = columns(index)
        partial[:, at] = dot(third[:, :OWN], low) + dot(third[:, OWN:], early_two[:, at])

    staggered(NY // TILE, layer_one, gelu, layer_two, gelu, layer_three)
    correction = (
        pltpu.roll(partial[0:8, :], 1, 1) + partial[8:16, :] + pltpu.roll(partial[16:24, :], NY - 1, 1)
    )
    near = [jnp.concatenate([upper[c][1:], velocity[c][:3]], axis=0) for c in range(CH)]
    rows = [field[1:5] for field in near]
    pieces = []
    for c in range(CH):
        flux = near[0] * near[c]
        side = rows[1] * rows[c]
        pieces.append(
            (flux[2:] - flux[:-2]) + (pltpu.roll(side, NY - 1, 1) - pltpu.roll(side, 1, 1))
        )
    advect = 0.5 * jnp.concatenate(pieces, axis=0)
    provisional = jnp.concatenate(rows, axis=0) + STEP_SIZE * (correction - advect)
    sent[:, 0] = column_forward(provisional, forward_a, forward_b, forward_b0, twist, pair_low).reshape(D, 2, 128)


def middle_kernel(
    device, got, row_forward, spin, spin_step, short_forward, short_inverse, short_rim, spin_rim, row_inverse, sent
):
    same, cross = multiplier(device[0])
    v = pair_low(dot, row_forward, side_by_side([got[:, k].reshape(256, 128) for k in range(2)]))
    plain = (spin[0], spin[1])
    step = (spin_step[0], spin_step[1])
    fields = []
    for k, (cosine, sine) in enumerate((step, plain)):
        real, imag = v[:128, 128 * k : 128 * k + 128], v[128:, 128 * k : 128 * k + 128]
        fields.append(side_by_side([real * cosine + imag * sine, imag * cosine - real * sine]))
    high, low = halves(jnp.concatenate(fields, axis=0))
    full = dot(high, short_forward[...]) + dot(low, short_forward[...])
    fields = []
    for k in range(2):
        part = full[128 * k : 128 * k + 128]
        real, imag = part[:, :128], part[:, 128:]
        real = same * real + cross * pltpu.roll(real, 64, 1)
        imag = same * imag + cross * pltpu.roll(imag, 64, 1)
        fields.append(side_by_side([real, imag]))
    high, low = halves(jnp.concatenate(fields, axis=0))
    full = dot(high, short_inverse[...]) + dot(low, short_inverse[...])
    rim = dot(high[128:], short_rim[...]) + dot(low[128:], short_rim[...])
    parts = []
    for part, (cosine, sine) in (
        (full[:128], plain),
        (full[128:], step),
        (rim, (spin_rim[0], spin_rim[1])),
    ):
        real, imag = part[:, :128], part[:, 128:]
        parts.append(jnp.concatenate([real * cosine - imag * sine, imag * cosine + real * sine], axis=0))
    sent[:, 0] = pair_low(dot, row_inverse, parts[0]).astype(BF).reshape(D, 2, 128)
    out = exact(dot, row_inverse, side_by_side(parts[1:])).astype(BF)
    for k in range(2):
        sent[:, k + 1] = out[:, 128 * k : 128 * k + 128].reshape(D, 2, 128)


def backward_kernel(
    got,
    inverse_b,
    inverse_b0,
    untwist,
    inverse_a,
    inverse_rim,
    w_mid,
    w_out,
    duals,
    taps,
    stack,
    act_one_home,
    act_two_home,
    slope_one_home,
    slope_two_home,
    sent,
    act_one,
    act_two,
    slope_one,
    slope_two,
    dual_stack,
    sum_mid,
    sum_in,
    sum_out,
    semaphores,
):
    held = (slope_two, act_one, act_two, slope_one)
    homes = (slope_two_home, act_one_home, act_two_home, slope_one_home)
    count = NY // BACK_TILE

    def fetch(index):
        at = pl.ds(pl.multiple_of(index * BACK_TILE, BACK_TILE), BACK_TILE)
        for k in range(4):
            pltpu.make_async_copy(homes[k].at[:, at], held[k].at[:, at], semaphores.at[k, index]).start()

    fetch(0)
    both = side_by_side([got[:, 1].reshape(256, 128), got[:, 2].reshape(256, 128)])
    general = pair_low(dot, inverse_b, both)
    zero = dot(inverse_b0[...], both)
    lane = lax.broadcasted_iota(jnp.int32, general.shape, 1)
    beyond = jnp.where(lane < 128, lane % 64 - R, lane % 32 - 2)
    y = jnp.where(beyond < 0, zero, general)
    real, imag = y[:128], y[128:]
    cosine, sine = untwist[0], untwist[1]
    real, imag = real * cosine - imag * sine, imag * cosine + real * sine
    own = exact(dot_nt, inverse_a, side_by_side([real[:, :128], imag[:, :128]]))
    rim = exact(dot_nt, inverse_rim, side_by_side([real[:, 128:192], imag[:, 128:192]]))
    base = jnp.concatenate([from_blocks(own), from_blocks(rim)], axis=0)
    dual_stack[0:16, :] = pltpu.roll(base, NY - 1, 1).astype(BF)
    dual_stack[16:32, :] = base.astype(BF)
    dual_stack[32:48, :] = pltpu.roll(base, 1, 1).astype(BF)
    flat_out = flat_taps(w_out)
    spread_out = jnp.concatenate([dot_tn(flat_out, duals[i]).astype(BF) for i in range(R)], axis=0)
    middle = diagonal(w_mid[...].T, R)
    sum_mid[...] = jnp.zeros_like(sum_mid)
    sum_in[...] = jnp.zeros_like(sum_in)
    sum_out[...] = jnp.zeros_like(sum_out)

    def step(index, _):
        at = pl.ds(pl.multiple_of(index * BACK_TILE, BACK_TILE), BACK_TILE)
        @pl.when(index + 1 < count)
        def _():
            fetch(index + 1)

        def arrived(k):
            pltpu.make_async_copy(homes[k].at[:, at], held[k].at[:, at], semaphores.at[k, index]).wait()
            return held[k][:, at]

        dual = dual_stack[:, at]
        back_two = dot(spread_out, dual)
        delta_two = (back_two * arrived(0)).astype(BF)
        sum_mid[...] += dot_nt(delta_two, arrived(1))
        back_one = dot(middle, delta_two)
        sum_out[...] += dot_nt(arrived(2), dual)
        delta_one = (back_one * arrived(3)).astype(BF)
        sum_in[...] += dot_nt(delta_one, stack[:, at])
        return 0

    lax.fori_loop(0, count, step, 0, unroll=2)
    mid = sum(sum_mid[64 * i : 64 * i + 64, 64 * i : 64 * i + 64] for i in range(R))
    flips = []
    for source, choose in ((sum_in, taps), (sum_out, duals)):
        flip = jnp.zeros((18, HID), F32)
        for i in range(R):
            high, low = halves(source[64 * i : 64 * i + 64, :])
            flip = flip + (dot_nt(choose[i], high) + dot_nt(choose[i], low))
        flips.append(flip)
    packed = jnp.concatenate([side_by_side([mid[:32], mid[32:]]), side_by_side(flips)], axis=0)
    low = packed.astype(BF).reshape(25, 2, 128)
    for k in range(sent.shape[0]):
        sent[k] = low


def added(got):
    total = got[0].astype(F32)
    for k in range(1, got.shape[0]):
        total = total + got[k].astype(F32)
    return total


def partial_sum_kernel(got, sent):
    low = added(got).astype(BF)
    for k in range(sent.shape[0]):
        sent[k] = low


def total_kernel(got, grad_mid, grad_in, grad_out):
    total = added(got).reshape(50, 128)
    grad_mid[:32] = total[:32, :64]
    grad_mid[32:] = total[:32, 64:]
    for t in range(9):
        pair = total[32 + 2 * t : 34 + 2 * t]
        grad_in[t // 3, t % 3] = pair[:, :64]
        grad_out[t // 3, t % 3] = pair[:, 64:]


def field_kernel(got, inverse_b, inverse_b0, untwist, inverse_a, field):
    real, imag = column_inverse_first(got[:, 0].reshape(256, 128), inverse_b, inverse_b0, untwist)
    x = from_blocks(exact(dot_nt, inverse_a, side_by_side([real, imag])))
    field[0] = x[:R]
    field[1] = x[R:]


class Staged:
    def __init__(self, copy, ref):
        self.copy, self.ref, self.waited = copy, ref, False

    def ready(self):
        if not self.waited:
            self.copy.wait()
            self.waited = True
        return self.ref

    def __getitem__(self, index):
        return self.ready()[index]


def call(kernel, outputs, inputs, scratch=(), scalars=0, staged=0, kept=0, far=0, far_out=0):
    count = len(inputs)
    outputs = outputs if isinstance(outputs, list) else [outputs]
    spec = lambda space: pl.BlockSpec(memory_space=space)
    specs = [spec(pltpu.SMEM)] * scalars
    specs += [spec(pltpu.VMEM)] * (count - scalars - staged - far)
    specs += [spec(pltpu.HBM)] * (staged + far)
    out_specs = [spec(pltpu.VMEM)] * (len(outputs) - far_out) + [spec(pltpu.HBM)] * far_out
    out_specs += [spec(pltpu.VMEM)] * kept
    first = count - staged - far
    dropped = staged - kept

    def run(*refs):
        given = list(refs[:count])
        own = len(outputs) - kept
        targets = refs[count + own : count + own + kept]
        rest = refs[count + own + kept :]
        if staged:
            for k in range(staged):
                target = rest[len(scratch) + k] if k < dropped else targets[k - dropped]
                copy = pltpu.make_async_copy(given[first + k], target, rest[-1].at[k])
                copy.start()
                given[first + k] = Staged(copy, target)
        kernel(*given, *refs[count : count + own], *rest[: len(scratch)])
        for k in range(staged):
            given[first + k].ready()

    held = [pltpu.VMEM(x.shape, x.dtype) for x in inputs[first : first + dropped]]
    kept_out = [pltpu.VMEM(x.shape, x.dtype) for x in inputs[first + dropped : first + staged]]
    pinned = [pltpu.with_memory_space_constraint(jnp.asarray(x), pltpu.HBM) for x in inputs[first:]]
    inputs = [*inputs[:first], *pinned]
    far_first = len(outputs) - far_out
    outputs = outputs[:far_first] + [pltpu.HBM(x.shape, x.dtype) for x in outputs[far_first:]]
    outputs += kept_out
    if staged:
        held.append(pltpu.SemaphoreType.DMA((staged,)))
    result = pl.pallas_call(
        run,
        out_shape=outputs,
        in_specs=specs,
        out_specs=out_specs,
        scratch_shapes=list(scratch) + held,
        compiler_params=pltpu.CompilerParams(vmem_limit_bytes=VMEM_LIMIT),
    )(*inputs)
    return result if len(outputs) > 1 else result[0]


def layer_one_kernel(stack, first_all):
    first = jnp.concatenate([first_all[: 3 * HID], first_all[4 * HID : 5 * HID]], axis=0)
    return lambda at: dot(first, stack[:, at])


def layer_two_kernel(middle_all, act_one):
    middle = middle_all[...]
    return lambda at: dot(middle, act_one[:, at])


def prefetch(arrays, after, maker, near, wide=()):
    count, given, tiles = len(arrays), len(wide), NY // TILE

    def run(*refs):
        sources, refs = refs[: count + given], refs[count + given + 1 :]
        close, refs = refs[: len(near)], refs[len(near) :]
        targets, homes, refs = refs[:count], refs[count : count + 2], refs[count + 2 :]
        held, results, refs = refs[:given], refs[given : given + 2], refs[given + 2 :]
        semaphores, in_semaphores, out_semaphores = refs
        columns = [slice(index * TILE, index * TILE + TILE) for index in range(tiles)]
        pieces = [
            [
                pltpu.make_async_copy(sources[count + k].at[:, at], held[k].at[:, at], in_semaphores.at[k, index])
                for k in range(given)
            ]
            for index, at in enumerate(columns)
        ]
        copies = [pltpu.make_async_copy(sources[k], targets[k], semaphores.at[k]) for k in range(count)]
        for copy in sum(pieces, []) + copies:
            copy.start()
        layer = maker(*close, *held)
        for index, at in enumerate(columns):
            for copy in pieces[index]:
                copy.wait()
            square, gate, value = gelu_parts(layer(at))
            results[0][:, at] = value.astype(BF)
            results[1][:, at] = slope_of(square, gate, value)
            for k in range(2):
                copies.append(
                    pltpu.make_async_copy(results[k].at[:, at], homes[k].at[:, at], out_semaphores.at[k, index])
                )
                copies[-1].start()
        for copy in copies:
            copy.wait()

    arrays = [jnp.asarray(x) for x in [*arrays, *wide]]
    *tables, act, slope = pl.pallas_call(
        run,
        out_shape=[pltpu.VMEM(x.shape, x.dtype) for x in arrays[:count]]
        + [pltpu.HBM((OWN, NY), BF), pltpu.HBM((OWN, NY), F32)],
        in_specs=[pl.BlockSpec(memory_space=pltpu.HBM)] * (count + given)
        + [pl.BlockSpec(memory_space=pl.ANY)]
        + [pl.BlockSpec(memory_space=pltpu.VMEM)] * len(near),
        out_specs=[pl.BlockSpec(memory_space=pltpu.VMEM)] * count + [pl.BlockSpec(memory_space=pltpu.HBM)] * 2,
        scratch_shapes=[pltpu.VMEM(x.shape, x.dtype) for x in arrays[count:]]
        + [
            pltpu.VMEM((OWN, NY), BF),
            pltpu.VMEM((OWN, NY), F32),
            pltpu.SemaphoreType.DMA((count,)),
            pltpu.SemaphoreType.DMA((max(given, 1), tiles)),
            pltpu.SemaphoreType.DMA((2, tiles)),
        ],
        compiler_params=pltpu.CompilerParams(vmem_limit_bytes=VMEM_LIMIT),
    )(*[pltpu.with_memory_space_constraint(x, pltpu.HBM) for x in arrays], after, *near)
    return tables, act, slope


def groups_of(mask):
    return [[i for i in range(D) if i & ~mask == j] for j in range(D) if not j & mask]


def exchange(x, groups=None):
    return lax.all_to_all(x, "rows", split_axis=0, concat_axis=0, tiled=True, axis_index_groups=groups)


def body(velocity, cotangent, w_in, w_mid, w_out):
    columns = column_tables()
    rows = row_tables()
    net = network_tables()
    scale = STEP_SIZE / math.sqrt(NX * NY)
    shape = jax.ShapeDtypeStruct
    w_in = jnp.transpose(w_in, (1, 2, 3, 0))
    device = lax.axis_index("rows").reshape(1)
    down = [(i, (i + 1) % D) for i in range(D)]
    above = lax.ppermute(velocity, "rows", down)

    forward = [columns[k] for k in ("forward_a", "forward_b", "forward_b0", "twist")]
    weights = [w_in, w_mid, w_out, net["taps"], net["outs"], net["taps_inner"]]
    dual_sent, *prepared = call(
        early_kernel,
        [
            shape((D, 2, 128), BF),
            pltpu.VMEM((2 * HID, NY), BF),
            pltpu.VMEM((6 * HID, 48), BF),
            pltpu.VMEM((24, 6 * HID), BF),
            pltpu.VMEM((OWN, OWN), BF),
        ],
        [cotangent, *weights, *forward, velocity],
        [pltpu.VMEM((24, NY), BF)],
        staged=12,
        kept=5,
    )
    early, tables = prepared[:4], prepared[4:]
    first_all, middle_all = early[1], early[3]

    first_sent, stack = call(
        network_kernel,
        [shape((D, 2, 2, 128), BF), pltpu.VMEM((48, NY), BF)],
        [dual_sent, *early, above, *tables],
        [pltpu.VMEM((24, NY), F32)],
    )
    first_got = exchange(first_sent)
    names = ("row_forward", "spin", "spin_step", "short_forward", "short_inverse", "short_rim", "spin_rim")
    tables, act_one, slope_one = prefetch(
        [*[rows[k] for k in names], rows["row_inverse"]],
        first_sent,
        layer_one_kernel,
        [stack, first_all],
    )
    second_sent = call(
        middle_kernel, shape((D, 3, 2, 128), BF), [device, first_got, *tables], scalars=1
    )
    second_got = exchange(second_sent)
    back = [columns[k] for k in ("inverse_b", "inverse_b0", "untwist")]
    empty = np.zeros((2, 128, 64), np.float32)
    untwists = np.concatenate([columns["untwist"], columns["untwist_rim"], empty], axis=2)
    tables, act_two, slope_two = prefetch(
        [
            *back[:2],
            untwists,
            table_pair(columns["inverse_a"] * scale),
            table_pair(columns["inverse_rim"] * scale),
            w_mid,
            w_out,
            net["duals"],
            net["taps_step"],
        ],
        second_sent,
        layer_two_kernel,
        [middle_all],
        [act_one],
    )
    one, two = groups_of(SUM_BITS), groups_of(D - 1 - SUM_BITS)
    partial = call(
        backward_kernel,
        shape((len(one[0]), 25, 2, 128), BF),
        [second_got, *tables, stack, act_one, act_two, slope_one, slope_two],
        [
            *[pltpu.VMEM((OWN, NY), t) for t in (BF, BF, F32, F32)],
            pltpu.VMEM((48, NY), BF),
            pltpu.VMEM((OWN, OWN), F32),
            pltpu.VMEM((OWN, 48), F32),
            pltpu.VMEM((OWN, 48), F32),
            pltpu.SemaphoreType.DMA((4, NY // BACK_TILE)),
        ],
        far=4,
    )
    partial = call(partial_sum_kernel, shape((len(two[0]), 25, 2, 128), BF), [exchange(partial, one)])
    new_velocity = call(
        field_kernel,
        shape((CH, R, NY), F32),
        [second_got, *back, table_pair(columns["inverse_a"])],
        staged=4,
    )
    grad_mid, grad_in, grad_out = call(
        total_kernel,
        [shape((HID, HID), F32), shape((3, 3, 2, HID), F32), shape((3, 3, 2, HID), F32)],
        [exchange(partial, two)],
    )
    return new_velocity, jnp.transpose(grad_in, (3, 0, 1, 2)), grad_mid, grad_out


def solution(mesh):
    in_specs = (P("batch", "rows", None), P("batch", "rows", None), P(), P(), P())
    out_specs = (
        P("batch", "rows", None),
        P("batch", None, None, None),
        P("batch", None),
        P("batch", None, None, None),
    )
    return jax.shard_map(body, mesh=mesh, in_specs=in_specs, out_specs=out_specs, check_vma=False)
```

```python
import functools
import math

import jax
import jax.numpy as jnp
import ml_dtypes
import numpy as np
from jax import lax
from jax.experimental import pallas as pl
from jax.experimental.pallas import tpu as pltpu
from jax.sharding import PartitionSpec as P

STEP_SIZE = 0.5
GELU_SCALE = 0.7978845608028654
GELU_CUBIC = 0.044715
BF = jnp.bfloat16
F32 = jnp.float32
TILE = 1024
BACK_TILE = 2048
SUM_BITS = 0b0001111
VMEM_LIMIT = 32 * 1024 * 1024

R = 4
D = 128
NX = R * D
OUTER = 32
NY = OUTER * 128
C = OUTER // 2
CH = 2
HID = 64
OWN = R * HID
STEP_ROWS = (-2, -1, 0, 1)
LATE_ROWS = (-2, -1, 0, -3)
EARLY_ROWS = (1, 2)


def table_pair(matrix):
    high = np.asarray(matrix, np.float64).astype(ml_dtypes.bfloat16)
    low = (matrix - high.astype(np.float64)).astype(ml_dtypes.bfloat16)
    return np.stack([high, low])


def column_tables():
    a = np.arange(OUTER)
    b = np.arange(128)
    d = np.arange(D)
    c = np.arange(C)
    eye = np.eye(R * CH).reshape(CH, R, CH, R)
    sign = np.where(a % 2 == 0, 1.0, -1.0)
    angle = 2 * np.pi * np.outer(c, a) / OUTER
    first = np.stack([np.cos(angle), -np.sin(angle)])
    first[0, 0] = 1.0
    first[1, 0] = sign
    forward_a = np.einsum("pca,hrgs->phcrags", first, eye).reshape(256, 256)
    last = np.stack([2 * np.cos(angle), -2 * np.sin(angle)])
    last[0, 0] = 1.0
    last[1, 0] = sign
    last = last / NY
    inverse_a = np.einsum("pca,gshr->agsphcr", last, eye).reshape(256, 256)
    half = np.zeros((2, 4, CH, 2))
    for h in range(CH):
        for e in range(2):
            half[h, h * 2 + e, h, e] = 1.0
    rim = np.zeros((8, CH, 2))
    rim[:4] = np.eye(4).reshape(4, CH, 2)
    inverse_rim = np.einsum("pca,khr->akphcr", last, rim).reshape(256, 128)
    theta = 2 * np.pi * np.outer(c, b) / NY
    cosine = np.cos(theta)
    sine = np.sin(theta)
    cosine[0] = 1.0
    sine[0] = 0.0
    spread = lambda t, n: np.broadcast_to(t[None, :, None, :], (CH, C, n, 128)).reshape(-1, 128)
    twist = np.stack([spread(cosine, R), spread(sine, R)]).astype(np.float32)
    twist_rim = np.stack([spread(cosine, 2), spread(sine, 2)]).astype(np.float32)
    phi = 2 * np.pi * np.outer(d, b) / 128
    matrix = np.zeros((D, 2, 2, 128))
    matrix[:, 0, 0] = np.cos(phi)
    matrix[:, 0, 1] = np.sin(phi)
    matrix[:, 1, 0] = -np.sin(phi)
    matrix[:, 1, 1] = np.cos(phi)
    psi = 2 * np.pi * np.outer(16 + 32 * (d - 64), b) / NY
    alternate = np.where(b % 2 == 0, 1.0, -1.0)
    zero = np.zeros((D, 2, 2, 128))
    zero[:64, 0, 0] = np.cos(phi[:64])
    zero[:64, 1, 0] = -np.sin(phi[:64])
    zero[0, 1, 0] = alternate
    zero[64:, 0, 1] = np.cos(psi[64:])
    zero[64:, 1, 1] = -np.sin(psi[64:])
    back = np.zeros((2, 128, D, 2))
    back[0, :, :, 0] = np.cos(phi).T
    back[0, :, :, 1] = -np.sin(phi).T
    back[1, :, :, 0] = np.sin(phi).T
    back[1, :, :, 1] = np.cos(phi).T
    back_zero = np.zeros((2, 128, D, 2))
    back_zero[0, :, :64, 0] = 2 * np.cos(phi[:64]).T
    back_zero[0, :, :64, 1] = -2 * np.sin(phi[:64]).T
    back_zero[0, :, 0, 0] = 1.0
    back_zero[0, :, 0, 1] = alternate
    back_zero[1, :, 64:, 0] = 2 * np.cos(psi[64:]).T
    back_zero[1, :, 64:, 1] = -2 * np.sin(psi[64:]).T
    return {
        "forward_a": table_pair(forward_a),
        "forward_b": table_pair(matrix.reshape(256, 256)),
        "forward_b0": table_pair(zero.reshape(256, 256))[0],
        "twist": twist,
        "inverse_b": table_pair(back.reshape(256, 256)),
        "inverse_b0": table_pair(back_zero.reshape(256, 256))[0],
        "inverse_a": inverse_a,
        "inverse_rim": inverse_rim,
        "untwist": np.ascontiguousarray(twist.transpose(0, 2, 1)),
        "untwist_rim": np.ascontiguousarray(twist_rim.transpose(0, 2, 1)),
    }


def row_tables():
    s = np.arange(D)
    m1 = np.arange(D)
    m2 = np.arange(R)
    phi = 2 * np.pi * np.outer(m1, s) / D
    forward = np.zeros((2, D, D, 2))
    forward[0, :, :, 0] = np.cos(phi)
    forward[0, :, :, 1] = np.sin(phi)
    forward[1, :, :, 0] = -np.sin(phi)
    forward[1, :, :, 1] = np.cos(phi)
    inverse = np.zeros((D, 2, 2, D))
    inverse[:, 0, 0] = np.cos(phi).T
    inverse[:, 0, 1] = -np.sin(phi).T
    inverse[:, 1, 0] = np.sin(phi).T
    inverse[:, 1, 1] = np.cos(phi).T
    inverse = inverse / NX
    eye = np.eye(CH * C)

    def short(rows, flip):
        angle = 2 * np.pi * np.outer(m2, rows) / R
        block = np.zeros((2, R, 2, len(rows)))
        block[0, :, 0] = np.cos(angle)
        block[1, :, 0] = -np.sin(angle) * flip
        block[0, :, 1] = np.sin(angle) * flip
        block[1, :, 1] = np.cos(angle)
        block = np.round(block)
        return np.einsum("pmqr,gk->pgmqkr", block, eye).reshape(2 * CH * C * R, 2, -1)

    own = np.arange(R)
    rim = np.array([-1, R])
    rim_block = np.zeros((256, 2, 128))
    rim_block[:, :, :64] = short(rim, 1.0)

    def lanes(rows):
        theta = 2 * np.pi * np.outer(m1, rows) / NX
        both = np.stack([np.cos(theta), np.sin(theta)])
        wide = np.broadcast_to(both[:, :, None, :], (2, D, CH * C, len(rows))).reshape(2, D, -1)
        out = np.zeros((2, D, 128), np.float32)
        out[:, :, : wide.shape[2]] = wide
        return out

    return {
        "row_forward": table_pair(forward.reshape(256, 256)),
        "row_inverse": table_pair(inverse.reshape(256, 256)),
        "short_forward": short(own, -1.0).reshape(256, 256).astype(ml_dtypes.bfloat16),
        "short_inverse": short(own, 1.0).reshape(256, 256).astype(ml_dtypes.bfloat16),
        "short_rim": rim_block.reshape(256, 256).astype(ml_dtypes.bfloat16),
        "spin": lanes(own),
        "spin_step": lanes(np.array(STEP_ROWS)),
        "spin_rim": lanes(rim - 2),
    }


def velocity_row(ch, row):
    return ch * R + row if row >= 0 else 8 + ch * R + row + R


def dual_row(ch, row):
    if row in STEP_ROWS:
        return ch * R + row + 2
    return 8 + ch * 2 + (0 if row < -2 else 1)


def network_tables():
    order = (*LATE_ROWS, *EARLY_ROWS)
    taps = np.zeros((6, 18, 48))
    for at, i in enumerate(order):
        for a in range(-1, 2):
            for b in range(-1, 2):
                for ch in range(CH):
                    t = (3 * (a + 1) + b + 1) * 2 + ch
                    taps[at, t, (b + 1) * 16 + velocity_row(ch, i + a)] = 1
    outs = np.zeros((6, 24, 18))
    for at, k in enumerate(order):
        for a in range(-1, 2):
            i = k - a
            if i in STEP_ROWS:
                for b in range(-1, 2):
                    for o in range(CH):
                        outs[at, (b + 1) * 8 + o * R + i + 2, (3 * (a + 1) + b + 1) * 2 + o] = 1
    duals = np.zeros((R, 18, 48))
    for at, i in enumerate(STEP_ROWS):
        for a in range(-1, 2):
            for b in range(-1, 2):
                for o in range(CH):
                    t = (3 * (a + 1) + b + 1) * 2 + o
                    duals[at, t, (b + 1) * 16 + dual_row(o, i - a)] = 1
    low = lambda t: t.astype(ml_dtypes.bfloat16)
    inner = taps.reshape(6, 18, 3, 16)[4:, :, :, :8].reshape(2, 18, 24)
    return {
        "taps": low(taps),
        "taps_inner": low(inner),
        "taps_step": low(taps[[0, 1, 2, 4]]),
        "outs": low(outs),
        "duals": low(duals),
    }


def dot(x, y):
    return jnp.dot(x, y, preferred_element_type=F32)


def dot_nt(x, y):
    return lax.dot_general(x, y, (((1,), (1,)), ((), ())), preferred_element_type=F32)


def dot_tn(x, y):
    return lax.dot_general(x, y, (((0,), (0,)), ((), ())), preferred_element_type=F32)


def halves(x):
    high = x.astype(BF)
    return high, (x - high.astype(F32)).astype(BF)


def exact(form, pair, x):
    high, low = halves(x)
    return form(pair[0], high) + (form(pair[1], high) + form(pair[0], low))


def pair_low(form, pair, x):
    low = x.astype(BF)
    return form(pair[0], low) + form(pair[1], low)


def to_blocks(x):
    return jnp.concatenate([x[:, 128 * a : 128 * a + 128] for a in range(OUTER)], axis=0)


def from_blocks(x):
    rows = x.shape[0] // OUTER
    return jnp.concatenate([x[rows * a : rows * a + rows] for a in range(OUTER)], axis=1)


def column_forward(x, forward_a, forward_b, forward_b0, twist, product):
    y = product(dot, forward_a, to_blocks(x))
    real, imag = y[:128], y[128:]
    cosine, sine = twist[0], twist[1]
    both = jnp.concatenate([real * cosine + imag * sine, imag * cosine - real * sine], axis=1)
    general = product(dot_nt, forward_b, both)
    zero = dot_nt(forward_b0[...], both.astype(BF))
    lane = lax.broadcasted_iota(jnp.int32, general.shape, 1)
    return jnp.where(lane % 64 < R, zero, general).astype(BF)


def column_inverse_first(x, inverse_b, inverse_b0, untwist):
    general = pair_low(dot, inverse_b, x)
    zero = dot(inverse_b0[...], x)
    lane = lax.broadcasted_iota(jnp.int32, general.shape, 1)
    y = jnp.where(lane % 64 < R, zero, general)
    real, imag = y[:128], y[128:]
    cosine, sine = untwist[0], untwist[1]
    return real * cosine - imag * sine, imag * cosine + real * sine


def multiplier(device):
    m1 = lax.broadcasted_iota(jnp.int32, (128, 128), 0)
    lane = lax.broadcasted_iota(jnp.int32, (128, 128), 1)
    m = m1 + 128 * (lane % R)
    m = jnp.where(2 * m < NX, m, jnp.where(2 * m == NX, 0, m - NX))
    c = (lane % 64) // R
    n = c + OUTER * device
    n = jnp.where(2 * n < NY, n, n - NY)
    packed = jnp.where(device < 64, OUTER * device, 16 + OUTER * (device - 64))
    n = jnp.where(c == 0, packed, n)
    wave_row = m.astype(F32) * (1.0 / NX)
    wave_col = n.astype(F32) * (1.0 / NY)
    row_square = wave_row * wave_row
    col_square = wave_col * wave_col
    square = row_square + col_square
    some = square > 0
    inverse = 1.0 / jnp.where(some, square, 1.0)
    same = jnp.where(some, jnp.where(lane < 64, col_square, row_square) * inverse, 1.0)
    sign = jnp.where(lane % 2 == 0, 1.0, -1.0)
    return sign * same, -sign * (wave_row * wave_col) * inverse


def side_by_side(parts):
    return jnp.concatenate(parts, axis=1)


def staggered(count, *stages):
    values = {}
    for step in range(count + len(stages) - 1):
        for lag in reversed(range(len(stages))):
            index = step - lag
            if 0 <= index < count:
                values[index] = stages[lag](index, values.get(index))


def flat_taps(weights):
    rows = [weights[t // 3, t % 3].astype(F32) for t in range(9)]
    return jnp.concatenate(rows, axis=0).astype(BF)


def diagonal(block, count):
    empty = jnp.zeros_like(block)
    rows = [side_by_side([block if i == k else empty for k in range(count)]) for i in range(count)]
    return jnp.concatenate(rows, axis=0)


def gelu_parts(pre):
    square = pre * pre
    tangent = jnp.tanh(pre * (GELU_SCALE + (GELU_SCALE * GELU_CUBIC) * square))
    gate = 0.5 + 0.5 * tangent
    return square, gate, pre * gate


def slope_of(square, gate, value):
    return gate + value * (1.0 - gate) * (2 * GELU_SCALE + (6 * GELU_SCALE * GELU_CUBIC) * square)


def early_kernel(
    field,
    w_in,
    w_mid,
    w_out,
    taps,
    outs,
    taps_inner,
    forward_a,
    forward_b,
    forward_b0,
    twist,
    velocity,
    sent,
    early_two,
    first_all,
    third,
    middle_all,
    inner,
):
    x = jnp.concatenate([field[0], field[1]], axis=0)
    sent[...] = column_forward(x, forward_a, forward_b, forward_b0, twist, exact).reshape(D, 2, 128)
    base = jnp.concatenate([velocity[0], velocity[1]], axis=0)
    shifts = [pltpu.roll(base, 1, 1), base, pltpu.roll(base, NY - 1, 1)]
    inner[...] = jnp.concatenate(shifts, axis=0).astype(BF)
    flat_in = flat_taps(w_in.ready())
    first = jnp.concatenate([dot_tn(flat_in, taps_inner[i]).astype(BF) for i in range(2)], axis=0)
    middle = diagonal(w_mid[...], 2)
    for i in range(6):
        first_all[HID * i : HID * i + HID] = dot_tn(flat_in, taps[i]).astype(BF)
    flat_out = flat_taps(w_out.ready())
    third[...] = side_by_side([dot(outs[i], flat_out).astype(BF) for i in range(6)])
    middle_all[...] = diagonal(w_mid[...], R)

    def columns(index):
        return slice(index * TILE, index * TILE + TILE)

    def layer_one(index, _):
        return dot(first, inner[:, columns(index)])

    def gelu_one(index, pre):
        return gelu_parts(pre)[2].astype(BF)

    def layer_two(index, low):
        return dot(middle, low)

    def gelu_two(index, pre):
        early_two[:, columns(index)] = gelu_parts(pre)[2].astype(BF)

    staggered(NY // TILE, layer_one, gelu_one, layer_two, gelu_two)


def network_kernel(
    dual_sent,
    early_two,
    first_all,
    third,
    middle_all,
    above,
    forward_a,
    forward_b,
    forward_b0,
    twist,
    velocity,
    sent,
    stack,
    partial,
):
    sent[:, 1] = dual_sent[...]
    upper = [above[c] for c in range(CH)]
    base = jnp.concatenate([velocity[0], velocity[1], *upper], axis=0)
    stack[0:16, :] = pltpu.roll(base, 1, 1).astype(BF)
    stack[16:32, :] = base.astype(BF)
    stack[32:48, :] = pltpu.roll(base, NY - 1, 1).astype(BF)
    first, middle = first_all[:OWN], middle_all[...]

    def columns(index):
        return slice(index * TILE, index * TILE + TILE)

    def layer_one(index, _):
        return dot(first, stack[:, columns(index)])

    def gelu(index, pre):
        return gelu_parts(pre)[2].astype(BF)

    def layer_two(index, low):
        return dot(middle, low)

    def layer_three(index, low):
        at = columns(index)
        partial[:, at] = dot(third[:, :OWN], low) + dot(third[:, OWN:], early_two[:, at])

    staggered(NY // TILE, layer_one, gelu, layer_two, gelu, layer_three)
    correction = (
        pltpu.roll(partial[0:8, :], 1, 1) + partial[8:16, :] + pltpu.roll(partial[16:24, :], NY - 1, 1)
    )
    near = [jnp.concatenate([upper[c][1:], velocity[c][:3]], axis=0) for c in range(CH)]
    rows = [field[1:5] for field in near]
    pieces = []
    for c in range(CH):
        flux = near[0] * near[c]
        side = rows[1] * rows[c]
        pieces.append(
            (flux[2:] - flux[:-2]) + (pltpu.roll(side, NY - 1, 1) - pltpu.roll(side, 1, 1))
        )
    advect = 0.5 * jnp.concatenate(pieces, axis=0)
    provisional = jnp.concatenate(rows, axis=0) + STEP_SIZE * (correction - advect)
    sent[:, 0] = column_forward(provisional, forward_a, forward_b, forward_b0, twist, pair_low).reshape(D, 2, 128)


def middle_kernel(
    device, got, row_forward, spin, spin_step, short_forward, short_inverse, short_rim, spin_rim, row_inverse, sent
):
    same, cross = multiplier(device[0])
    v = pair_low(dot, row_forward, side_by_side([got[:, k].reshape(256, 128) for k in range(2)]))
    plain = (spin[0], spin[1])
    step = (spin_step[0], spin_step[1])
    fields = []
    for k, (cosine, sine) in enumerate((step, plain)):
        real, imag = v[:128, 128 * k : 128 * k + 128], v[128:, 128 * k : 128 * k + 128]
        fields.append(side_by_side([real * cosine + imag * sine, imag * cosine - real * sine]))
    high, low = halves(jnp.concatenate(fields, axis=0))
    full = dot(high, short_forward[...]) + dot(low, short_forward[...])
    fields = []
    for k in range(2):
        part = full[128 * k : 128 * k + 128]
        real, imag = part[:, :128], part[:, 128:]
        real = same * real + cross * pltpu.roll(real, 64, 1)
        imag = same * imag + cross * pltpu.roll(imag, 64, 1)
        fields.append(side_by_side([real, imag]))
    high, low = halves(jnp.concatenate(fields, axis=0))
    full = dot(high, short_inverse[...]) + dot(low, short_inverse[...])
    rim = dot(high[128:], short_rim[...]) + dot(low[128:], short_rim[...])
    parts = []
    for part, (cosine, sine) in (
        (full[:128], plain),
        (full[128:], step),
        (rim, (spin_rim[0], spin_rim[1])),
    ):
        real, imag = part[:, :128], part[:, 128:]
        parts.append(jnp.concatenate([real * cosine - imag * sine, imag * cosine + real * sine], axis=0))
    sent[:, 0] = pair_low(dot, row_inverse, parts[0]).astype(BF).reshape(D, 2, 128)
    out = exact(dot, row_inverse, side_by_side(parts[1:])).astype(BF)
    for k in range(2):
        sent[:, k + 1] = out[:, 128 * k : 128 * k + 128].reshape(D, 2, 128)


def backward_kernel(
    got,
    inverse_b,
    inverse_b0,
    untwist,
    inverse_a,
    inverse_rim,
    w_mid,
    w_out,
    duals,
    taps,
    stack,
    act_one_home,
    act_two_home,
    slope_one_home,
    slope_two_home,
    sent,
    act_one,
    act_two,
    slope_one,
    slope_two,
    dual_stack,
    sum_mid,
    sum_in,
    sum_out,
    semaphores,
):
    held = (slope_two, act_one, act_two, slope_one)
    homes = (slope_two_home, act_one_home, act_two_home, slope_one_home)
    count = NY // BACK_TILE

    def fetch(index):
        at = pl.ds(pl.multiple_of(index * BACK_TILE, BACK_TILE), BACK_TILE)
        for k in range(4):
            pltpu.make_async_copy(homes[k].at[:, at], held[k].at[:, at], semaphores.at[k, index]).start()

    fetch(0)
    both = side_by_side([got[:, 1].reshape(256, 128), got[:, 2].reshape(256, 128)])
    general = pair_low(dot, inverse_b, both)
    zero = dot(inverse_b0[...], both)
    lane = lax.broadcasted_iota(jnp.int32, general.shape, 1)
    beyond = jnp.where(lane < 128, lane % 64 - R, lane % 32 - 2)
    y = jnp.where(beyond < 0, zero, general)
    real, imag = y[:128], y[128:]
    cosine, sine = untwist[0], untwist[1]
    real, imag = real * cosine - imag * sine, imag * cosine + real * sine
    own = exact(dot_nt, inverse_a, side_by_side([real[:, :128], imag[:, :128]]))
    rim = exact(dot_nt, inverse_rim, side_by_side([real[:, 128:192], imag[:, 128:192]]))
    base = jnp.concatenate([from_blocks(own), from_blocks(rim)], axis=0)
    dual_stack[0:16, :] = pltpu.roll(base, NY - 1, 1).astype(BF)
    dual_stack[16:32, :] = base.astype(BF)
    dual_stack[32:48, :] = pltpu.roll(base, 1, 1).astype(BF)
    flat_out = flat_taps(w_out)
    spread_out = jnp.concatenate([dot_tn(flat_out, duals[i]).astype(BF) for i in range(R)], axis=0)
    middle = diagonal(w_mid[...].T, R)
    sum_mid[...] = jnp.zeros_like(sum_mid)
    sum_in[...] = jnp.zeros_like(sum_in)
    sum_out[...] = jnp.zeros_like(sum_out)

    def step(index, _):
        at = pl.ds(pl.multiple_of(index * BACK_TILE, BACK_TILE), BACK_TILE)
        @pl.when(index + 1 < count)
        def _():
            fetch(index + 1)

        def arrived(k):
            pltpu.make_async_copy(homes[k].at[:, at], held[k].at[:, at], semaphores.at[k, index]).wait()
            return held[k][:, at]

        dual = dual_stack[:, at]
        back_two = dot(spread_out, dual)
        delta_two = (back_two * arrived(0)).astype(BF)
        sum_mid[...] += dot_nt(delta_two, arrived(1))
        back_one = dot(middle, delta_two)
        sum_out[...] += dot_nt(arrived(2), dual)
        delta_one = (back_one * arrived(3).astype(F32)).astype(BF)
        sum_in[...] += dot_nt(delta_one, stack[:, at])
        return 0

    lax.fori_loop(0, count, step, 0, unroll=2)
    mid = sum(sum_mid[64 * i : 64 * i + 64, 64 * i : 64 * i + 64] for i in range(R))
    flips = []
    for source, choose in ((sum_in, taps), (sum_out, duals)):
        flip = jnp.zeros((18, HID), F32)
        for i in range(R):
            high, low = halves(source[64 * i : 64 * i + 64, :])
            flip = flip + (dot_nt(choose[i], high) + dot_nt(choose[i], low))
        flips.append(flip)
    packed = jnp.concatenate([side_by_side([mid[:32], mid[32:]]), side_by_side(flips)], axis=0)
    low = packed.astype(BF).reshape(25, 2, 128)
    for k in range(sent.shape[0]):
        sent[k] = low


def added(got):
    total = got[0].astype(F32)
    for k in range(1, got.shape[0]):
        total = total + got[k].astype(F32)
    return total


def partial_sum_kernel(got, sent):
    low = added(got).astype(BF)
    for k in range(sent.shape[0]):
        sent[k] = low


def total_kernel(got, grad_mid, grad_in, grad_out):
    total = added(got).reshape(50, 128)
    grad_mid[:32] = total[:32, :64]
    grad_mid[32:] = total[:32, 64:]
    for t in range(9):
        pair = total[32 + 2 * t : 34 + 2 * t]
        grad_in[t // 3, t % 3] = pair[:, :64]
        grad_out[t // 3, t % 3] = pair[:, 64:]


def field_kernel(got, inverse_b, inverse_b0, untwist, inverse_a, field):
    real, imag = column_inverse_first(got[:, 0].reshape(256, 128), inverse_b, inverse_b0, untwist)
    x = from_blocks(exact(dot_nt, inverse_a, side_by_side([real, imag])))
    field[0] = x[:R]
    field[1] = x[R:]


class Staged:
    def __init__(self, copy, ref):
        self.copy, self.ref, self.waited = copy, ref, False

    def ready(self):
        if not self.waited:
            self.copy.wait()
            self.waited = True
        return self.ref

    def __getitem__(self, index):
        return self.ready()[index]


def call(kernel, outputs, inputs, scratch=(), scalars=0, staged=0, kept=0, far=0, far_out=0):
    count = len(inputs)
    outputs = outputs if isinstance(outputs, list) else [outputs]
    spec = lambda space: pl.BlockSpec(memory_space=space)
    specs = [spec(pltpu.SMEM)] * scalars
    specs += [spec(pltpu.VMEM)] * (count - scalars - staged - far)
    specs += [spec(pltpu.HBM)] * (staged + far)
    out_specs = [spec(pltpu.VMEM)] * (len(outputs) - far_out) + [spec(pltpu.HBM)] * far_out
    out_specs += [spec(pltpu.VMEM)] * kept
    first = count - staged - far
    dropped = staged - kept

    def run(*refs):
        given = list(refs[:count])
        own = len(outputs) - kept
        targets = refs[count + own : count + own + kept]
        rest = refs[count + own + kept :]
        if staged:
            for k in range(staged):
                target = rest[len(scratch) + k] if k < dropped else targets[k - dropped]
                copy = pltpu.make_async_copy(given[first + k], target, rest[-1].at[k])
                copy.start()
                given[first + k] = Staged(copy, target)
        kernel(*given, *refs[count : count + own], *rest[: len(scratch)])
        for k in range(staged):
            given[first + k].ready()

    held = [pltpu.VMEM(x.shape, x.dtype) for x in inputs[first : first + dropped]]
    kept_out = [pltpu.VMEM(x.shape, x.dtype) for x in inputs[first + dropped : first + staged]]
    pinned = [pltpu.with_memory_space_constraint(jnp.asarray(x), pltpu.HBM) for x in inputs[first:]]
    inputs = [*inputs[:first], *pinned]
    far_first = len(outputs) - far_out
    outputs = outputs[:far_first] + [pltpu.HBM(x.shape, x.dtype) for x in outputs[far_first:]]
    outputs += kept_out
    if staged:
        held.append(pltpu.SemaphoreType.DMA((staged,)))
    result = pl.pallas_call(
        run,
        out_shape=outputs,
        in_specs=specs,
        out_specs=out_specs,
        scratch_shapes=list(scratch) + held,
        compiler_params=pltpu.CompilerParams(vmem_limit_bytes=VMEM_LIMIT),
    )(*inputs)
    return result if len(outputs) > 1 else result[0]


def layer_one_kernel(stack, first_all):
    first = jnp.concatenate([first_all[: 3 * HID], first_all[4 * HID : 5 * HID]], axis=0)
    return lambda at: dot(first, stack[:, at])


def layer_two_kernel(middle_all, act_one):
    middle = middle_all[...]
    return lambda at: dot(middle, act_one[:, at])


def prefetch(arrays, after, maker, near, wide=(), kept_as=F32):
    count, given, tiles = len(arrays), len(wide), NY // TILE

    def run(*refs):
        sources, refs = refs[: count + given], refs[count + given + 1 :]
        close, refs = refs[: len(near)], refs[len(near) :]
        targets, homes, refs = refs[:count], refs[count : count + 2], refs[count + 2 :]
        held, results, refs = refs[:given], refs[given : given + 2], refs[given + 2 :]
        semaphores, in_semaphores, out_semaphores = refs
        columns = [slice(index * TILE, index * TILE + TILE) for index in range(tiles)]
        pieces = [
            [
                pltpu.make_async_copy(sources[count + k].at[:, at], held[k].at[:, at], in_semaphores.at[k, index])
                for k in range(given)
            ]
            for index, at in enumerate(columns)
        ]
        copies = [pltpu.make_async_copy(sources[k], targets[k], semaphores.at[k]) for k in range(count)]
        for copy in sum(pieces, []) + copies:
            copy.start()
        layer = maker(*close, *held)
        for index, at in enumerate(columns):
            for copy in pieces[index]:
                copy.wait()
            square, gate, value = gelu_parts(layer(at))
            results[0][:, at] = value.astype(BF)
            results[1][:, at] = slope_of(square, gate, value).astype(kept_as)
            for k in range(2):
                copies.append(
                    pltpu.make_async_copy(results[k].at[:, at], homes[k].at[:, at], out_semaphores.at[k, index])
                )
                copies[-1].start()
        for copy in copies:
            copy.wait()

    arrays = [jnp.asarray(x) for x in [*arrays, *wide]]
    *tables, act, slope = pl.pallas_call(
        run,
        out_shape=[pltpu.VMEM(x.shape, x.dtype) for x in arrays[:count]]
        + [pltpu.HBM((OWN, NY), BF), pltpu.HBM((OWN, NY), kept_as)],
        in_specs=[pl.BlockSpec(memory_space=pltpu.HBM)] * (count + given)
        + [pl.BlockSpec(memory_space=pl.ANY)]
        + [pl.BlockSpec(memory_space=pltpu.VMEM)] * len(near),
        out_specs=[pl.BlockSpec(memory_space=pltpu.VMEM)] * count + [pl.BlockSpec(memory_space=pltpu.HBM)] * 2,
        scratch_shapes=[pltpu.VMEM(x.shape, x.dtype) for x in arrays[count:]]
        + [
            pltpu.VMEM((OWN, NY), BF),
            pltpu.VMEM((OWN, NY), kept_as),
            pltpu.SemaphoreType.DMA((count,)),
            pltpu.SemaphoreType.DMA((max(given, 1), tiles)),
            pltpu.SemaphoreType.DMA((2, tiles)),
        ],
        compiler_params=pltpu.CompilerParams(vmem_limit_bytes=VMEM_LIMIT),
    )(*[pltpu.with_memory_space_constraint(x, pltpu.HBM) for x in arrays], after, *near)
    return tables, act, slope


def groups_of(mask):
    return [[i for i in range(D) if i & ~mask == j] for j in range(D) if not j & mask]


def exchange(x, groups=None):
    return lax.all_to_all(x, "rows", split_axis=0, concat_axis=0, tiled=True, axis_index_groups=groups)


def body(velocity, cotangent, w_in, w_mid, w_out):
    columns = column_tables()
    rows = row_tables()
    net = network_tables()
    scale = STEP_SIZE / math.sqrt(NX * NY)
    shape = jax.ShapeDtypeStruct
    w_in = jnp.transpose(w_in, (1, 2, 3, 0))
    device = lax.axis_index("rows").reshape(1)
    down = [(i, (i + 1) % D) for i in range(D)]
    above = lax.ppermute(velocity, "rows", down)

    forward = [columns[k] for k in ("forward_a", "forward_b", "forward_b0", "twist")]
    weights = [w_in, w_mid, w_out, net["taps"], net["outs"], net["taps_inner"]]
    dual_sent, *prepared = call(
        early_kernel,
        [
            shape((D, 2, 128), BF),
            pltpu.VMEM((2 * HID, NY), BF),
            pltpu.VMEM((6 * HID, 48), BF),
            pltpu.VMEM((24, 6 * HID), BF),
            pltpu.VMEM((OWN, OWN), BF),
        ],
        [cotangent, *weights, *forward, velocity],
        [pltpu.VMEM((24, NY), BF)],
        staged=12,
        kept=5,
    )
    early, tables = prepared[:4], prepared[4:]
    first_all, middle_all = early[1], early[3]

    first_sent, stack = call(
        network_kernel,
        [shape((D, 2, 2, 128), BF), pltpu.VMEM((48, NY), BF)],
        [dual_sent, *early, above, *tables],
        [pltpu.VMEM((24, NY), F32)],
    )
    first_got = exchange(first_sent)
    names = ("row_forward", "spin", "spin_step", "short_forward", "short_inverse", "short_rim", "spin_rim")
    tables, act_one, slope_one = prefetch(
        [*[rows[k] for k in names], rows["row_inverse"]],
        first_sent,
        layer_one_kernel,
        [stack, first_all],
        kept_as=BF,
    )
    second_sent = call(
        middle_kernel, shape((D, 3, 2, 128), BF), [device, first_got, *tables], scalars=1
    )
    second_got = exchange(second_sent)
    back = [columns[k] for k in ("inverse_b", "inverse_b0", "untwist")]
    empty = np.zeros((2, 128, 64), np.float32)
    untwists = np.concatenate([columns["untwist"], columns["untwist_rim"], empty], axis=2)
    tables, act_two, slope_two = prefetch(
        [
            *back[:2],
            untwists,
            table_pair(columns["inverse_a"] * scale),
            table_pair(columns["inverse_rim"] * scale),
            w_mid,
            w_out,
            net["duals"],
            net["taps_step"],
        ],
        second_sent,
        layer_two_kernel,
        [middle_all],
        [act_one],
    )
    one, two = groups_of(SUM_BITS), groups_of(D - 1 - SUM_BITS)
    partial = call(
        backward_kernel,
        shape((len(one[0]), 25, 2, 128), BF),
        [second_got, *tables, stack, act_one, act_two, slope_one, slope_two],
        [
            *[pltpu.VMEM((OWN, NY), t) for t in (BF, BF, BF, F32)],
            pltpu.VMEM((48, NY), BF),
            pltpu.VMEM((OWN, OWN), F32),
            pltpu.VMEM((OWN, 48), F32),
            pltpu.VMEM((OWN, 48), F32),
            pltpu.SemaphoreType.DMA((4, NY // BACK_TILE)),
        ],
        far=4,
    )
    partial = call(partial_sum_kernel, shape((len(two[0]), 25, 2, 128), BF), [exchange(partial, one)])
    new_velocity = call(
        field_kernel,
        shape((CH, R, NY), F32),
        [second_got, *back, table_pair(columns["inverse_a"])],
        staged=4,
    )
    grad_mid, grad_in, grad_out = call(
        total_kernel,
        [shape((HID, HID), F32), shape((3, 3, 2, HID), F32), shape((3, 3, 2, HID), F32)],
        [exchange(partial, two)],
    )
    return new_velocity, jnp.transpose(grad_in, (3, 0, 1, 2)), grad_mid, grad_out


def solution(mesh):
    in_specs = (P("batch", "rows", None), P("batch", "rows", None), P(), P(), P())
    out_specs = (
        P("batch", "rows", None),
        P("batch", None, None, None),
        P("batch", None),
        P("batch", None, None, None),
    )
    return jax.shard_map(body, mesh=mesh, in_specs=in_specs, out_specs=out_specs, check_vma=False)
```
